32 devices in a mesh: gy: 4 (over y, core), gx: 8 (over z, x).
Axes of the slice: x: 2, y: 2, z: 4, core: 2. Of those that a mesh axis runs over, the one named last changes fastest.
Arguments:
- scan_features: bfloat16 [64, 248, 14336], P(None, 'gy', 'gx'), may hold values from -10 to 10
- occupancy: int32 [64, 248, 224], P(None, 'gy', 'gx'), may hold values from 0 to 1
- kernels: float32 [2, 576, 64], replicated, may hold values from -0.25 to 0.25
- kernel_m: float32 [2, 576, 64], replicated, may hold values from -0.0546875 to 0.0546875
- kernel_v: float32 [2, 576, 64], replicated, may hold values from 1.3516436e-05 to 0.00010813149
- norm_params: float32 [2, 2, 64], replicated, may hold values from -0.3 to 1.4, as said below
- norm_m: float32 [2, 2, 64], replicated, may hold values from -0.0546875 to 0.0546875
- norm_v: float32 [2, 2, 64], replicated, may hold values from 1.3516436e-05 to 0.00021626298
- cotangent: bfloat16 [64, 124, 7168], P(None, 'gy', 'gx'), may hold values from -8 to 8
Outputs:
- features: bfloat16 [64, 124, 7168], P(None, 'gy', 'gx')
- input_grad: bfloat16 [64, 248, 14336], P(None, 'gy', 'gx')
- grad_norm: float32 [], replicated
- new_kernels: float32 [2, 576, 64], replicated
- new_kernel_m: float32 [2, 576, 64], replicated
- new_kernel_v: float32 [2, 576, 64], replicated
- kernels_low: bfloat16 [2, 576, 64], replicated
- new_norm_params: float32 [2, 2, 64], replicated
- new_norm_m: float32 [2, 2, 64], replicated
- new_norm_v: float32 [2, 2, 64], replicated
The draws below stay inside these ranges and needn't reach their ends.
Inputs may be any that keep to these rules, and one draw needn't show every extreme that they name: `norm_params`: gains at index 0, shifts at index 1.
All inputs are finite; a program needn't handle non-finite values.
Results may differ from the reference program's by a relative error of at most 0.0082.
Values may be sent and summed in bfloat16 or wider, within the bound.
No kernel may reach another device: no remote copies, remote signals or barrier semaphores. Data moves between devices by JAX's collectives and lax.ppermute only.
A program may use at most 384 MiB of HBM per device.

```python
import math
import jax
import jax.numpy as jnp
from jax import lax

C = 64
SCANS = 64
H_OUT = 124
W_OUT = 112
H_IN = 248
W_IN = 224


def shared_field(key):
    coarse_rows = (H_OUT + 3) // 4
    coarse_cols = (W_OUT + 3) // 4
    field_key, loud_key = jax.random.split(key)
    coarse = jnp.clip(jax.random.normal(field_key, (SCANS, coarse_rows, coarse_cols), jnp.float32), -2.5, 2.5)
    loudness = jnp.exp(jax.random.uniform(loud_key, (SCANS, 1, 1, 1), jnp.float32, -0.8, 0.6))
    return (coarse, loudness)


def spread_noise(key, shape):
    return jnp.clip(jax.random.normal(key, shape, jnp.float32), -4.0, 4.0)


def draw_scan_features(key, part):
    coarse, loudness = shared_field(key)
    key = jax.random.fold_in(key, 11)
    noise_key, size_key, sign_key, tilt_key = jax.random.split(key, 4)
    noise = spread_noise(noise_key, (SCANS, H_IN, W_IN, C))
    offset_size = jax.random.uniform(size_key, (C,), jnp.float32, 0.3, 0.7)
    offset_sign = jnp.where(jax.random.uniform(sign_key, (C,), jnp.float32) < 0.5, -1.0, 1.0)
    tilts = jnp.clip(jax.random.normal(tilt_key, (C,), jnp.float32), -2.5, 2.5)
    row_block = jnp.arange(H_IN, dtype=jnp.int32) // 8
    col_block = jnp.arange(W_IN, dtype=jnp.int32) // 8
    region = coarse[:, row_block][:, :, col_block]
    values = loudness * (noise + offset_size * offset_sign + 0.7 * region[..., None] * tilts)
    return jnp.clip(values, -10.0, 10.0).reshape(SCANS, H_IN, W_IN * C).astype(jnp.bfloat16)


def draw_cotangent(key, part):
    coarse, loudness = shared_field(key)
    key = jax.random.fold_in(key, 23)
    noise_key, tilt_key = jax.random.split(key)
    noise = spread_noise(noise_key, (SCANS, H_OUT, W_OUT, C))
    tilts = jnp.clip(jax.random.normal(tilt_key, (C,), jnp.float32), -2.5, 2.5)
    row_block = jnp.arange(H_OUT, dtype=jnp.int32) // 4
    col_block = jnp.arange(W_OUT, dtype=jnp.int32) // 4
    region = coarse[:, row_block][:, :, col_block]
    values = noise + 0.8 * region[..., None] * tilts
    return jnp.clip(values, -8.0, 8.0).reshape(SCANS, H_OUT, W_OUT * C).astype(jnp.bfloat16)


def draw_occupancy(key, part):
    row_index = jnp.arange(H_IN, dtype=jnp.int32)[:, None]
    col_index = jnp.arange(W_IN, dtype=jnp.int32)[None, :]
    distance = col_index * 1000 // W_IN + jnp.abs(2 * row_index - H_IN) * 500 // H_IN
    chance = 50 + 850 * (1500 - distance) // 1500
    inside = col_index < W_IN * 27 // 28
    rolled = jax.random.randint(key, (SCANS, H_IN, W_IN), 0, 1000, dtype=jnp.int32)
    return jnp.where((rolled < chance) & inside, 1, 0).astype(jnp.int32)


def draw_norm_params(key, part):
    gain_key, shift_key = jax.random.split(jax.random.fold_in(key, 7))
    gain_rows = jnp.clip(1.0 + 0.15 * jax.random.normal(gain_key, (2, 1, C), jnp.float32), 0.6, 1.4)
    shifts = jnp.clip(0.12 * jax.random.normal(shift_key, (2, 1, C), jnp.float32), -0.3, 0.3)
    return jnp.concatenate([gain_rows, shifts], axis=1)


def centred(rng, shape, scale, bound, held_as=jnp.bfloat16):
    drawn = jax.random.normal(rng, shape, jnp.float32) * scale
    return jnp.minimum(jnp.maximum(drawn, -bound), bound).astype(held_as)


def setup_inputs(seed: int = 0) -> dict:
    key_of = jax.random.split(jax.random.key(seed), 10)
    return {
        "scan_features": draw_scan_features(jax.random.fold_in(key_of[9], 71), 0),
        "occupancy": draw_occupancy(jax.random.fold_in(key_of[9], 71), 0),
        "kernels": centred(key_of[2], (2, 9 * C, C), (9 * C) ** -0.5, 0.25, jnp.float32),
        "kernel_m": centred(key_of[3], (2, 9 * C, C), ((18 * C * C + 4 * C) ** -0.5), 0.0546875, jnp.float32),
        "kernel_v": jnp.clip(jnp.exp(jax.random.uniform(key_of[4], (2, 9 * C, C), jnp.float32, math.log(1.3516436411009636e-05), math.log(0.00010813149))), 1.3516436411009636e-05, 0.00010813149),
        "norm_params": draw_norm_params(jax.random.fold_in(key_of[9], 71), 0),
        "norm_m": centred(key_of[6], (2, 2, C), ((18 * C * C + 4 * C) ** -0.5), 0.0546875, jnp.float32),
        "norm_v": jnp.clip(jnp.exp(jax.random.uniform(key_of[7], (2, 2, C), jnp.float32, math.log(1.3516436411009636e-05), math.log(0.00021626298))), 1.3516436411009636e-05, 0.00021626298),
        "cotangent": draw_cotangent(jax.random.fold_in(key_of[9], 71), 0),
    }


@jax.custom_vjp
def low(v):
    return lax.optimization_barrier(v.astype(jnp.bfloat16)).astype(jnp.float32)

@jax.custom_vjp
def low_back(v):
    return v

def low_keep(v):
    return (low(v), None)

def low_pass(kept, grad):
    return (grad,)

def back_keep(v):
    return (v, None)

def back_low(kept, grad):
    return (low(grad),)
low.defvjp(low_keep, low_pass)
low_back.defvjp(back_keep, back_low)
norm_eps = 1e-05
adam_beta = 0.5
adam_eps = 1e-08
step_count = 5
clip_limit = 1.0
kernel_rate = 0.04
norm_rate = 0.25
kernel_decay = 0.01

def conv_layer(values, kernel, stride):
    return lax.conv_general_dilated(values, kernel, (stride, stride), ((1, 1), (1, 1)), dimension_numbers=('NHWC', 'HWIO', 'NHWC'), precision=lax.Precision.HIGHEST)

def norm_act(values, params):
    centre = lax.optimization_barrier(jnp.mean(values, axis=(0, 1, 2)))
    spread = lax.optimization_barrier(jnp.mean((values - centre) ** 2, axis=(0, 1, 2)))
    normed = (values - centre) * lax.rsqrt(spread + norm_eps)
    return jax.nn.silu(params[0] * normed + params[1])

def adam_step(weight_now, gradient, moment_one, moment_two, step_rate, decay_rate):
    first_new = adam_beta * moment_one + (1.0 - adam_beta) * gradient
    second_new = adam_beta * moment_two + (1.0 - adam_beta) * gradient * gradient
    correction = 1.0 - adam_beta ** step_count
    update = first_new / correction / (jnp.sqrt(second_new / correction) + adam_eps)
    return (weight_now - step_rate * (update + decay_rate * weight_now), first_new, second_new)

def reference(scan_features, occupancy, kernels, kernel_m, kernel_v, norm_params, norm_m, norm_v, cotangent):
    scan_count, in_rows, flat_cols = scan_features.shape
    channels = kernels.shape[2]
    in_cols = flat_cols // channels
    inputs = scan_features.astype(jnp.float32).reshape(scan_count, in_rows, in_cols, channels)
    live_mask = occupancy.astype(jnp.float32)[..., None]

    def forward(values, kernel_all, params):
        masked = values * live_mask
        kernel_one = low(kernel_all[0]).reshape(3, 3, channels, channels)
        kernel_two = low(kernel_all[1]).reshape(3, 3, channels, channels)
        conv_one = low_back(conv_layer(masked, kernel_one, 2))
        hidden = low(norm_act(conv_one, params[0]))
        conv_two = low_back(conv_layer(hidden, kernel_two, 1))
        return norm_act(conv_two, params[1])
    activated, pullback = jax.vjp(forward, inputs, kernels, norm_params)
    d_inputs, kernel_grad, norm_grad = pullback(cotangent.astype(jnp.float32).reshape(activated.shape))
    features = activated.astype(jnp.bfloat16).reshape(scan_count, in_rows // 2, in_cols // 2 * channels)
    input_grad = d_inputs.astype(jnp.bfloat16).reshape(scan_count, in_rows, in_cols * channels)
    grad_norm = jnp.sqrt(jnp.sum(kernel_grad * kernel_grad) + jnp.sum(norm_grad * norm_grad))
    factor = jnp.minimum(1.0, clip_limit / grad_norm)
    new_kernels, new_kernel_m, new_kernel_v = adam_step(kernels, kernel_grad * factor, kernel_m, kernel_v, kernel_rate, kernel_decay)
    new_norm_params, new_norm_m, new_norm_v = adam_step(norm_params, norm_grad * factor, norm_m, norm_v, norm_rate, 0.0)
    return (features, input_grad, grad_norm, new_kernels, new_kernel_m, new_kernel_v, new_kernels.astype(jnp.bfloat16), new_norm_params, new_norm_m, new_norm_v)
```

```python
import functools
import math

import jax
import jax.numpy as jnp
from jax import lax
from jax.experimental import pallas as pl
from jax.experimental.pallas import tpu as pltpu
from jax.sharding import PartitionSpec as P

norm_eps = 1e-05
adam_beta = 0.5
adam_eps = 1e-08
step_count = 5
clip_limit = 1.0
kernel_rate = 0.04
norm_rate = 0.25
kernel_decay = 0.01

f32, bf16 = (jnp.float32, jnp.bfloat16)
BOTH = ("gy", "gx")
S, C, L, BITS = (16, 64, 128, 13)


def params_of(limit=56):
    return pltpu.CompilerParams(
        dimension_semantics=("arbitrary",), vmem_limit_bytes=limit << 20
    )


def cost(microseconds):
    return pl.CostEstimate(
        flops=0, bytes_accessed=int(microseconds * 3.6e6), transcendentals=0
    )


def whole(shape):
    return pl.BlockSpec(shape, lambda g: (0,) * len(shape))


def scans(rows, lanes):
    return pl.BlockSpec((rows, S, lanes), lambda g: (0, g, 0))


def low_half(rows=S):
    return lax.broadcasted_iota(jnp.int32, (rows, L), 1) < C


def swap(x):
    return pltpu.roll(x, C, 1)


def fold(x):
    x = jnp.broadcast_to(x, (8, L))
    return (x + swap(x))[:1]


def pair(ref, row, t):
    return ref[row, :, t * L : (t + 1) * L]


def stats_of(st_ref, count):
    groups = 2 * st_ref.shape[0]
    means = st_ref[:, :L]
    mean = fold(jnp.sum(means, axis=0, keepdims=True)) / groups
    spread = st_ref[:, L:] + count * (means - mean) ** 2
    spread = fold(jnp.sum(spread, axis=0, keepdims=True)) / (groups * count)
    return (mean, lax.rsqrt(spread + norm_eps))


def sums_of(st_ref):
    both = jnp.sum(st_ref[...], axis=0, keepdims=True)
    return (fold(both[:, :L]), fold(both[:, L:]))


def merge_stats(step, mean, squares, count, run_ref):
    @pl.when(step == 0)
    def _():
        run_ref[0:1] = mean
        run_ref[1:2] = squares

    @pl.when(step > 0)
    def _():
        before = step.astype(f32)
        share = 1.0 / (before + 1.0)
        delta = mean - run_ref[0:1]
        run_ref[0:1] = run_ref[0:1] + delta * share
        run_ref[1:2] = run_ref[1:2] + squares + delta * delta * (count * before * share)


def send_stats(step, steps, run_ref, st_ref):
    @pl.when(step == steps - 1)
    def _():
        row = jnp.concatenate([run_ref[0:1], run_ref[1:2]], axis=1)
        st_ref[...] = jnp.broadcast_to(row, st_ref.shape)


def halves(x):
    return x[:8] + x[8:]


def prep_kernel(
    row_ref, col_ref, occ_ref, kt_ref, np_ref, bits_ref, xrow_ref, xcol_ref, w1_ref, w2_ref,
    w2b_ref, w1b_ref, np2_ref,
):
    cols, scan_count, rows = occ_ref.shape
    groups = bits_ref.shape[0]
    row_of = lax.broadcasted_iota(jnp.int32, (rows, groups * L), 0)
    group_of = lax.broadcasted_iota(jnp.int32, (rows, groups * L), 1) // L
    inner = row_of - group_of * BITS
    power = jnp.where(
        (inner >= 0) & (inner < BITS), (1 << jnp.clip(inner, 0, BITS)), 0
    ).astype(bf16)
    flat = occ_ref[...].astype(f32).astype(bf16).reshape(cols * scan_count, rows)
    words = jnp.dot(flat, power, preferred_element_type=f32).astype(jnp.int32)
    words = words.reshape(cols // 2, 2, scan_count, groups * L)
    low = low_half(scan_count)
    for g in range(groups):
        for t in range(cols // 2):
            lanes = slice(g * L, (g + 1) * L)
            word = jnp.where(low, words[t, 0, :, lanes], words[t, 1, :, lanes])
            bits_ref[g, :, t * L : (t + 1) * L] = word.astype(jnp.int16)

    def live(row, t):
        word = bits_ref[row // BITS, :, t * L : (t + 1) * L].astype(jnp.int32)
        return (word & (1 << (row % BITS))) != 0

    for t in range(cols // 2):
        x = row_ref[0, :, t * L : (t + 1) * L].astype(f32)
        xrow_ref[:, t * L : (t + 1) * L] = jnp.where(live(rows - 1, t), x, 0.0).astype(bf16)
    for i in range(rows // 2):
        even = jnp.where(live(2 * i, cols // 2 - 1), col_ref[2 * i].astype(f32), 0.0)
        odd = jnp.where(live(2 * i + 1, cols // 2 - 1), col_ref[2 * i + 1].astype(f32), 0.0)
        xcol_ref[i] = jnp.where(low, swap(even), odd).astype(bf16)
    back = [[kt_ref[l, :, k * C : (k + 1) * C] for k in range(9)] for l in range(2)]
    fore = [[jnp.transpose(b) for b in layer] for layer in back]
    none = jnp.zeros((C, C), f32)

    def put(ref, rows_of, cols_of, pick):
        for a in range(rows_of):
            blocks = [pick(a, b) for b in range(cols_of)]
            for k in range(0, cols_of, 2):
                two = jnp.concatenate(blocks[k : k + 2], axis=1).astype(bf16)
                ref[a * C : (a + 1) * C, k * C : (k + 2) * C] = two

    def tap(table, p, q):
        return table[3 * p + q] if 0 <= p < 3 and 0 <= q < 3 else none

    put(w1_ref, 30, 4, lambda a, b: tap(fore[0], a // 6 - 2 * (b // 2), a % 6 - 2 * (b % 2) - 1))
    put(w2_ref, 16, 4, lambda a, b: tap(fore[1], a // 4 - b // 2, a % 4 - b % 2))
    put(w2b_ref, 16, 4, lambda a, b: tap(back[1], b // 2 + 2 - a // 4, b % 2 + 2 - a % 4))
    put(w1b_ref, 12, 4, lambda a, b: tap(back[0], (1, 2, 0)[a // 4], b + 1 - 2 * (a % 4)))
    np2_ref[...] = jnp.concatenate([np_ref[...], np_ref[...]], axis=1)


def prepare(x, occ, kt, norm_params):
    rows, scan_count, lanes = x.shape
    cols = occ.shape[0]
    groups = -(-rows // BITS)
    full = lambda *shape: jax.ShapeDtypeStruct(shape, bf16)
    outs = [
        jax.ShapeDtypeStruct((groups, scan_count, lanes), jnp.int16),
        full(scan_count, lanes),
        full(rows // 2, scan_count, L),
        full(30 * C, 4 * C),
        full(16 * C, 4 * C),
        full(16 * C, 4 * C),
        full(12 * C, 4 * C),
        jax.ShapeDtypeStruct((4, L), f32),
    ]
    return pl.pallas_call(
        prep_kernel,
        grid=(1,),
        in_specs=[
            pl.BlockSpec((1, scan_count, lanes), lambda g: (rows - 1, 0, 0)),
            pl.BlockSpec((rows, scan_count, L), lambda g: (0, 0, lanes // L - 1)),
            whole(occ.shape),
            whole(kt.shape),
            whole((4, C)),
        ],
        out_specs=[whole(o.shape) for o in outs],
        out_shape=outs,
        compiler_params=params_of(),
        cost_estimate=cost(5),
        name="prepare",
    )(x, x, occ, kt, norm_params.reshape(4, C))


def conv_one_kernel(
    x_ref, bits_ref, xrow_ref, xcol_ref, w_ref, c_ref, st_ref, up_ref, down_ref, left_ref,
    right_ref, xs, run,
):
    step, steps = (pl.program_id(0), pl.num_programs(0))
    rows, tiles = (x_ref.shape[0], x_ref.shape[2] // L)
    out_rows, out_tiles = (rows // 2, tiles // 2)
    pairs = (out_rows + 1) // 2

    @pl.when(step == 0)
    def _():
        for k in range(rows + 1, 4 * pairs + 1):
            xs[k // 4, k % 4] = jnp.zeros_like(xs[0, 0])

    xs[0, 0, :, L:] = xrow_ref[...]
    for k in range(out_rows + 1):
        xs[2 * k // 4, 2 * k % 4, :, :L] = xcol_ref[k]
    for i in range(out_rows):
        k = 2 * i + 1
        xs[k // 4, k % 4, :, :L] = swap(xcol_ref[i + 1].astype(f32)).astype(bf16)

    def fill(t, _):
        lanes = pl.ds(pl.multiple_of(t * L, L), L)
        into = pl.ds(pl.multiple_of(t * L + L, L), L)
        for g in range(bits_ref.shape[0]):
            word = bits_ref[g, :, lanes].astype(jnp.int32)
            for r in range(g * BITS, min(rows, (g + 1) * BITS)):
                x = x_ref[r, :, lanes].astype(f32)
                x = jnp.where((word & (1 << (r - g * BITS))) != 0, x, 0.0)
                xs[(r + 1) // 4, (r + 1) % 4, :, into] = x.astype(bf16)
        return 0

    lax.fori_loop(0, tiles, fill, 0)
    total = jnp.zeros((8, L), f32)
    for t in range(out_tiles):
        lanes = slice(2 * t * L, (2 * t + 3) * L)
        pieces = [xs[0:pairs, q, :, lanes] for q in range(4)] + [xs[1 : pairs + 1, 0, :, lanes]]
        lhs = jnp.concatenate([p.reshape(pairs * S, 3 * L) for p in pieces], axis=1)
        acc = jnp.dot(lhs, w_ref[...], preferred_element_type=f32).reshape(pairs, S, 2 * L)
        for i in range(out_rows):
            block = acc[i // 2, :, (i % 2) * L : (i % 2 + 1) * L]
            c_ref[i, :, t * L : (t + 1) * L] = block
            total = total + halves(block)
    count = out_rows * out_tiles * S
    mean = jnp.sum(total, axis=0, keepdims=True) / count

    def square(i, acc):
        for t in range(out_tiles):
            d = pair(c_ref, i, t) - mean
            acc = acc + halves(d * d)
        return acc

    squares = lax.fori_loop(0, out_rows, square, jnp.zeros((8, L), f32))
    merge_stats(step, mean, jnp.sum(squares, axis=0, keepdims=True), float(count), run)
    send_stats(step, steps, run, st_ref)
    up_ref[...] = c_ref[0:3].astype(bf16)
    down_ref[...] = c_ref[out_rows - 2 : out_rows].astype(bf16)
    left_ref[...] = c_ref[:, :, :L].astype(bf16)
    right_ref[...] = c_ref[:, :, (out_tiles - 1) * L :].astype(bf16)


def conv_one(x, bits, xrow, xcol, w, devices):
    rows, scan_count, lanes = x.shape
    r, w_out = (rows // 2, lanes // 2)
    pairs = (r + 1) // 2
    shape = lambda dtype, *s: jax.ShapeDtypeStruct(s, dtype)
    return pl.pallas_call(
        conv_one_kernel,
        grid=(scan_count // S,),
        in_specs=[
            scans(rows, lanes),
            scans(bits.shape[0], lanes),
            pl.BlockSpec((S, lanes), lambda g: (g, 0)),
            scans(r + 1, L),
            whole(w.shape),
        ],
        out_specs=[
            scans(r, w_out),
            whole((devices, 2 * L)),
            scans(3, w_out),
            scans(2, w_out),
            scans(r, L),
            scans(r, L),
        ],
        out_shape=[
            shape(f32, r, scan_count, w_out),
            shape(f32, devices, 2 * L),
            shape(bf16, 3, scan_count, w_out),
            shape(bf16, 2, scan_count, w_out),
            shape(bf16, r, scan_count, L),
            shape(bf16, r, scan_count, L),
        ],
        scratch_shapes=[
            pltpu.VMEM((pairs + 1, 4, S, lanes + L), bf16),
            pltpu.VMEM((8, L), f32),
        ],
        compiler_params=params_of(),
        cost_estimate=cost(18),
        name="conv_one",
    )(x, bits, xrow, xcol, w)


def conv_two_kernel(
    flags, c_ref, up_ref, down_ref, left_ref, right_ref, st_ref, np_ref, w_ref, c2_ref, n1_ref,
    st2_ref, hs, run, *, count,
):
    step, steps = (pl.program_id(0), pl.num_programs(0))
    r, tiles = (c_ref.shape[0], c_ref.shape[2] // L)
    mean, inv = stats_of(st_ref, count)
    offset = -mean * inv
    scale = 0.5 * np_ref[0:1] * inv
    shift = 0.5 * (np_ref[0:1] * offset + np_ref[1:2])
    f_up, f_down, f_left, f_right = (flags[k].astype(f32) for k in range(4))

    def act(c, flag=None):
        c = c.astype(f32)
        h = c * scale + shift
        out = h + h * jnp.tanh(h)
        if flag is not None:
            out = out * flag
        return (out.astype(bf16), c * inv + offset)

    def own(i, _):
        row = i + 2
        for t in range(tiles):
            hid, n = act(pair(c_ref, i, t))
            hs[row // 2, row % 2, :, (t + 1) * L : (t + 2) * L] = hid
            n1_ref[i, :, t * L : (t + 1) * L] = n
        hid, _n = act(left_ref[row], f_left)
        hs[row // 2, row % 2, :, :L] = hid
        hid, n = act(right_ref[row], f_right)
        hs[row // 2, row % 2, :, (tiles + 1) * L :] = hid
        n1_ref[i, :, tiles * L :] = n
        return 0

    lax.fori_loop(0, r, own, 0)
    for row in [0, 1, r + 2, r + 3, r + 4]:
        src, k, flag = (up_ref, row, f_up) if row < 2 else (down_ref, row - r - 2, f_down)
        for t in range(tiles):
            hid, n = act(pair(src, k, t), flag)
            hs[row // 2, row % 2, :, (t + 1) * L : (t + 2) * L] = hid
            if row == r + 2:
                n1_ref[r, :, t * L : (t + 1) * L] = n
        hid, _n = act(left_ref[row], flag * f_left)
        hs[row // 2, row % 2, :, :L] = hid
        hid, n = act(right_ref[row], flag * f_right)
        hs[row // 2, row % 2, :, (tiles + 1) * L :] = hid
        if row == r + 2:
            n1_ref[r, :, tiles * L :] = n
    pairs = (r + 3) // 2
    low = low_half()
    for k in range(tiles + 1):
        lanes = slice(k * L, (k + 2) * L)
        pieces = [hs[a : a + pairs, b, :, lanes] for a in range(2) for b in range(2)]
        lhs = jnp.concatenate([p.reshape(pairs * S, 2 * L) for p in pieces], axis=1)
        acc = jnp.dot(lhs, w_ref[...], preferred_element_type=f32).reshape(pairs, S, 2 * L)
        for row in range(r + 3):
            c2_ref[row, :, k * L : (k + 1) * L] = acc[row // 2, :, (row % 2) * L : (row % 2 + 1) * L]

    def tile_of(row, k):
        if k == 0:
            return jnp.where(low, pair(c2_ref, row, tiles), pair(c2_ref, row, 0))
        return pair(c2_ref, row, k)

    def add(i, acc):
        for k in range(tiles):
            acc = acc + halves(tile_of(i + 1, k))
        return acc

    total = lax.fori_loop(0, r, add, jnp.zeros((8, L), f32))
    cells = r * tiles * S
    mean2 = jnp.sum(total, axis=0, keepdims=True) / cells

    def square(i, acc):
        for k in range(tiles):
            d = tile_of(i + 1, k) - mean2
            acc = acc + halves(d * d)
        return acc

    squares = lax.fori_loop(0, r, square, jnp.zeros((8, L), f32))
    merge_stats(step, mean2, jnp.sum(squares, axis=0, keepdims=True), float(cells), run)
    send_stats(step, steps, run, st2_ref)


def conv_two(flags, c1, up, down, left, right, st, np2, w, count):
    r, scan_count, lanes = c1.shape
    tiles = lanes // L
    devices = st.shape[0]
    return pl.pallas_call(
        functools.partial(conv_two_kernel, count=count),
        grid=(scan_count // S,),
        in_specs=[
            pl.BlockSpec(memory_space=pltpu.SMEM),
            scans(r, lanes),
            scans(2, lanes),
            scans(3, lanes),
            scans(r + 5, L),
            scans(r + 5, L),
            whole(st.shape),
            whole(np2.shape),
            whole(w.shape),
        ],
        out_specs=[scans(r + 3, lanes + L), scans(r + 1, lanes + L), whole((devices, 2 * L))],
        out_shape=[
            jax.ShapeDtypeStruct((r + 3, scan_count, lanes + L), f32),
            jax.ShapeDtypeStruct((r + 1, scan_count, lanes + L), f32),
            jax.ShapeDtypeStruct((devices, 2 * L), f32),
        ],
        scratch_shapes=[
            pltpu.VMEM(((r + 5) // 2, 2, S, lanes + 2 * L), bf16),
            pltpu.VMEM((8, L), f32),
        ],
        compiler_params=params_of(),
        cost_estimate=cost(16),
        name="conv_two",
    )(flags, c1, up, down, left, right, st, np2, w)


def output_kernel(
    c2_ref, st_ref, np_ref, cot_ref, up_ref, down_ref, left_ref, right_ref, feat_ref, d_ref,
    sum_ref, run, *, count,
):
    step, steps = (pl.program_id(0), pl.num_programs(0))
    r, tiles = (cot_ref.shape[0], cot_ref.shape[2] // L)
    packed = left_ref.shape[0]
    mean, inv = stats_of(st_ref, count)
    offset = -mean * inv
    scale = 0.5 * np_ref[2:3] * inv
    shift = 0.5 * (np_ref[2:3] * offset + np_ref[3:4])
    low = low_half()

    def line(row, cot_of, own_row, sums):
        far = row >= packed
        line_of = row - jnp.where(far, packed, 0)
        before = left_ref[line_of].astype(f32)
        before = jnp.where(far, swap(before), before)
        beyond = right_ref[line_of].astype(f32)
        beyond = jnp.where(far, swap(beyond), beyond)
        last = None
        for k in range(tiles + 1):
            here = cot_of(k).astype(f32) if k < tiles else beyond
            cot = swap(jnp.where(low, here, before))
            before = here
            c = pair(c2_ref, row, k)
            n = c * inv + offset
            h = c * scale + shift
            t = jnp.tanh(h)
            plus = 1.0 + t
            d = (0.5 * cot) * (plus * (1.0 + h * (1.0 - t)))
            d_ref[row, :, k * L : (k + 1) * L] = d
            if own_row is None:
                continue
            f = h * plus
            if k > 0:
                both = swap(jnp.where(low, f, last))
                feat_ref[own_row, :, (k - 1) * L : k * L] = both.astype(bf16)
            last = f
            if k == 0:
                d = jnp.where(low, 0.0, d)
            if k == tiles:
                d = jnp.where(low, d, 0.0)
            sums = (sums[0] + halves(d), sums[1] + halves(d * n))
        return sums

    def own(i, sums):
        return line(i + 1, lambda k: pair(cot_ref, i, k), i, sums)

    zero = jnp.zeros((8, L), f32)
    sums = lax.fori_loop(0, r, own, (zero, zero))
    line(0, lambda k: pair(up_ref, 0, k), None, None)
    for j in range(2):
        line(r + 1 + j, lambda k, j=j: pair(down_ref, j, k), None, None)
    add_sums(step, steps, sums, run, sum_ref)


def add_sums(step, steps, sums, run, sum_ref):
    row = jnp.concatenate([jnp.sum(s, axis=0, keepdims=True) for s in sums], axis=1)

    @pl.when(step == 0)
    def _():
        run[0:1] = row

    @pl.when(step > 0)
    def _():
        run[0:1] = run[0:1] + row

    @pl.when(step == steps - 1)
    def _():
        sum_ref[...] = jnp.broadcast_to(run[0:1], sum_ref.shape)


def output(c2, st, np2, cot, up, down, left, right, count):
    r, scan_count, lanes = cot.shape
    devices = st.shape[0]
    wide = lanes + L
    return pl.pallas_call(
        functools.partial(output_kernel, count=count),
        grid=(scan_count // S,),
        in_specs=[
            scans(r + 3, wide),
            whole(st.shape),
            whole(np2.shape),
            scans(r, lanes),
            scans(1, lanes),
            scans(2, lanes),
            scans(left.shape[0], L),
            scans(right.shape[0], L),
        ],
        out_specs=[scans(r, lanes), scans(r + 3, wide), whole((devices, 2 * L))],
        out_shape=[
            jax.ShapeDtypeStruct((r, scan_count, lanes), bf16),
            jax.ShapeDtypeStruct((r + 3, scan_count, wide), f32),
            jax.ShapeDtypeStruct((devices, 2 * L), f32),
        ],
        scratch_shapes=[pltpu.VMEM((8, 2 * L), f32)],
        compiler_params=params_of(),
        cost_estimate=cost(16),
        name="output",
    )(c2, st, np2, cot, up, down, left, right)


def back_two_kernel(
    flags, d_ref, c2_ref, n1_ref, st_ref, sum_ref, np_ref, w_ref, dp_ref, edge_ref, kg_ref,
    sum1_ref, ds, hs, grad, run, *, count,
):
    step, steps = (pl.program_id(0), pl.num_programs(0))
    r, tiles = (n1_ref.shape[0] - 1, n1_ref.shape[2] // L - 1)
    cells = 2.0 * count * st_ref.shape[0]
    mean, inv = stats_of(st_ref, count)
    shift_sum, gain_sum = sums_of(sum_ref)
    gain = np_ref[2:3] * inv
    c_n = -gain * inv * gain_sum / cells
    c_0 = -gain * shift_sum / cells - c_n * mean
    f_up, f_down, f_left, f_right = (flags[k].astype(f32) for k in range(4))
    low = low_half()
    left = jnp.where(low, f_left, 1.0)
    right = jnp.where(low, 1.0, f_right)

    def line(row, flag):
        for k in range(tiles + 1):
            d = pair(d_ref, row, k) * gain + (pair(c2_ref, row, k) * c_n + c_0)
            if k == 0:
                d = d * left
            if k == tiles:
                d = d * right
            if flag is not None:
                d = d * flag
            ds[row // 2, row % 2, :, k * L : (k + 1) * L] = d.astype(bf16)

    def own(i, _):
        line(i + 1, None)
        for t in range(tiles):
            h = 0.5 * (pair(n1_ref, i, t) * np_ref[0:1] + np_ref[1:2])
            hs[i, :, t * L : (t + 1) * L] = (h + h * jnp.tanh(h)).astype(bf16)
        return 0

    lax.fori_loop(0, r, own, 0)
    line(0, f_up)
    line(r + 1, f_down)
    line(r + 2, f_down)

    @pl.when(step == 0)
    def _():
        grad[...] = jnp.zeros_like(grad)

    total = None
    for t in range(tiles):
        lanes = slice(t * L, (t + 2) * L)
        rows = ds[:, :, :, lanes].reshape(r + 3, S, 2 * L)
        rhs = jnp.concatenate([rows[a : a + r].reshape(r * S, 2 * L) for a in range(3)], axis=1)
        lhs = hs[:, :, t * L : (t + 1) * L].reshape(r * S, L)
        part = lax.dot_general(lhs, rhs, (((0,), (0,)), ((), ())), preferred_element_type=f32)
        total = part if total is None else total + part
    grad[...] += total
    pairs = (r + 1) // 2
    sums = (jnp.zeros((8, L), f32), jnp.zeros((8, L), f32))
    for t in range(tiles):
        lanes = slice(t * L, (t + 2) * L)
        pieces = [ds[a : a + pairs, b, :, lanes] for a in range(2) for b in range(2)]
        lhs = jnp.concatenate([p.reshape(pairs * S, 2 * L) for p in pieces], axis=1)
        acc = jnp.dot(lhs, w_ref[...], preferred_element_type=f32).reshape(pairs, S, 2 * L)
        for i in range(r + 1):
            n = pair(n1_ref, i, t)
            h = 0.5 * (n * np_ref[0:1] + np_ref[1:2])
            tan = jnp.tanh(h)
            d = acc[i // 2, :, (i % 2) * L : (i % 2 + 1) * L]
            d = (0.5 * d) * ((1.0 + tan) * (1.0 + h * (1.0 - tan)))
            dp_ref[i, :, t * L : (t + 1) * L] = d
            if i < r:
                sums = (sums[0] + halves(d), sums[1] + halves(d * n))
    add_sums(step, steps, sums, run, sum1_ref)
    for i in range(pairs):
        both = jnp.where(low, pair(dp_ref, i, 0), swap(pair(dp_ref, pairs + i, 0)))
        edge_ref[i] = both.astype(bf16)

    @pl.when(step == steps - 1)
    def _():
        for p in range(3):
            for q in range(3):
                block = None
                for w in range(2):
                    at = (2 - p) * 4 * C + (w + 2 - q) * C
                    part = grad[w * C : (w + 1) * C, at : at + C]
                    block = part if block is None else block + part
                kg_ref[3 * p + q] = jnp.transpose(block)


def back_two(flags, d, c2, n1, st, sums, np2, w, count):
    r, scan_count, wide = n1.shape
    r, lanes = (r - 1, wide - L)
    devices = st.shape[0]
    return pl.pallas_call(
        functools.partial(back_two_kernel, count=count),
        grid=(scan_count // S,),
        in_specs=[
            pl.BlockSpec(memory_space=pltpu.SMEM),
            scans(r + 3, wide),
            scans(r + 3, wide),
            scans(r + 1, wide),
            whole(st.shape),
            whole(sums.shape),
            whole(np2.shape),
            whole(w.shape),
        ],
        out_specs=[
            scans(r + 1, lanes),
            scans((r + 1) // 2, L),
            whole((9, C, C)),
            whole((devices, 2 * L)),
        ],
        out_shape=[
            jax.ShapeDtypeStruct((r + 1, scan_count, lanes), f32),
            jax.ShapeDtypeStruct(((r + 1) // 2, scan_count, L), bf16),
            jax.ShapeDtypeStruct((9, C, C), f32),
            jax.ShapeDtypeStruct((devices, 2 * L), f32),
        ],
        scratch_shapes=[
            pltpu.VMEM(((r + 3) // 2, 2, S, wide), bf16),
            pltpu.VMEM((r, S, lanes), bf16),
            pltpu.VMEM((L, 12 * C), f32),
            pltpu.VMEM((8, 2 * L), f32),
        ],
        compiler_params=params_of(),
        cost_estimate=cost(18),
        name="back_two",
    )(flags, d, c2, n1, st, sums, np2, w)


def back_one_kernel(
    flags, dp_ref, edge_ref, n1_ref, x_ref, bits_ref, st_ref, sum_ref, np_ref, kg2_ref, ds, kg_ref,
    xm, grad, *, count,
):
    step, steps = (pl.program_id(0), pl.num_programs(0))
    r, tiles = (n1_ref.shape[0] - 1, n1_ref.shape[2] // L - 1)
    cells = 2.0 * count * st_ref.shape[0]
    _mean, inv = stats_of(st_ref, count)
    shift_sum, gain_sum = sums_of(sum_ref)
    gain = np_ref[0:1] * inv
    c_n = -gain * gain_sum / cells
    c_0 = -gain * shift_sum / cells
    f_down, f_right = (flags[1].astype(f32), flags[3].astype(f32))
    packed = edge_ref.shape[0]

    def line(i, flag):
        far = i >= packed
        beyond = edge_ref[i - jnp.where(far, packed, 0)].astype(f32)
        beyond = jnp.where(far, swap(beyond), beyond)
        for t in range(tiles + 1):
            d = pair(dp_ref, i, t) if t < tiles else beyond
            d = d * gain + (pair(n1_ref, i, t) * c_n + c_0)
            if t == tiles:
                d = d * f_right
            if flag is not None:
                d = d * flag
            ds[i, :, t * L : (t + 1) * L] = d.astype(bf16)

    def own(i, _):
        line(i, None)
        return 0

    lax.fori_loop(0, r, own, 0)
    line(r, f_down)

    def fill(t, _):
        lanes = pl.ds(pl.multiple_of(t * L, L), L)
        for g in range(bits_ref.shape[0]):
            word = bits_ref[g, :, lanes].astype(jnp.int32)
            for row in range(g * BITS, min(2 * r, (g + 1) * BITS)):
                x = x_ref[row, :, lanes].astype(f32)
                x = jnp.where((word & (1 << (row - g * BITS))) != 0, x, 0.0)
                xm[row % 2, row // 2, :, lanes] = x.astype(bf16)
        return 0

    lax.fori_loop(0, 2 * tiles, fill, 0)

    @pl.when(step == 0)
    def _():
        grad[...] = jnp.zeros_like(grad)

    turned = (((0,), (0,)), ((), ()))
    totals = [None, None, None]
    for t in range(tiles):
        lanes = slice(t * L, (t + 2) * L)
        xl = slice(2 * t * L, 2 * (t + 1) * L)
        rows = [ds[a : a + r, :, lanes].reshape(r * S, 2 * L) for a in range(2)]
        xe, xo = (xm[a, :, :, xl].reshape(r * S, 2 * L) for a in range(2))
        for k, (a, b) in enumerate(((xe, rows[0]), (xo, rows[0]), (xo, rows[1]))):
            part = lax.dot_general(a, b, turned, preferred_element_type=f32)
            totals[k] = part if totals[k] is None else totals[k] + part
    for k in range(3):
        grad[k] += totals[k]

    @pl.when(step == steps - 1)
    def _():
        blocks = []
        for p in range(3):
            g = (2, 0, 1)[p]
            for q in range(3):
                block = None
                for v in range(3):
                    u = q - 1 + 2 * v
                    if 0 <= u < 4:
                        part = grad[g, u * C : (u + 1) * C, v * C : (v + 1) * C]
                        block = part if block is None else block + part
                blocks.append(jnp.transpose(block))
        blocks += [kg2_ref[8]] + [kg2_ref[k] for k in range(8)]
        for a in range(9):
            kg_ref[a * C : (a + 1) * C] = jnp.concatenate(blocks[2 * a : 2 * a + 2], axis=1)
        if kg_ref.shape[0] > 9 * C:
            kg_ref[9 * C :] = jnp.zeros((kg_ref.shape[0] - 9 * C, L), f32)


def back_one(flags, dp, edge, n1, x, bits, st, sums, np2, kg2, count):
    rows, scan_count, lanes = x.shape
    r, tiles = (rows // 2, lanes // L // 2)
    devices = st.shape[0]
    share = 8 * -(-9 * C // (8 * devices))
    wide = (tiles + 1) * L
    return pl.pallas_call(
        functools.partial(back_one_kernel, count=count),
        grid=(scan_count // S,),
        in_specs=[
            pl.BlockSpec(memory_space=pltpu.SMEM),
            scans(r + 1, tiles * L),
            scans(edge.shape[0], L),
            scans(r + 1, wide),
            scans(rows, lanes),
            scans(bits.shape[0], lanes),
            whole(st.shape),
            whole(sums.shape),
            whole(np2.shape),
            whole(kg2.shape),
        ],
        out_specs=[scans(r + 1, wide), whole((devices * share, L))],
        out_shape=[
            jax.ShapeDtypeStruct((r + 1, scan_count, wide), bf16),
            jax.ShapeDtypeStruct((devices * share, L), f32),
        ],
        scratch_shapes=[
            pltpu.VMEM((2, r, S, lanes), bf16),
            pltpu.VMEM((3, 4 * C, 4 * C), f32),
        ],
        compiler_params=params_of(),
        cost_estimate=cost(16),
        name="back_one",
    )(flags, dp, edge, n1, x, bits, st, sums, np2, kg2)


def input_grad_kernel(ds, bits_ref, w_ref, *rest):
    ig_ref = rest[-1]
    r, tiles = (ds.shape[0] - 1, ds.shape[2] // L - 1)
    for t in range(tiles):
        lanes = slice(t * L, (t + 2) * L)
        rows = [ds[a : a + r, :, lanes].reshape(r * S, 2 * L) for a in range(2)]
        even = jnp.dot(rows[0], w_ref[: 4 * C], preferred_element_type=f32)
        odd = jnp.dot(
            jnp.concatenate(rows, axis=1), w_ref[4 * C :], preferred_element_type=f32
        )
        for k, block in enumerate((even, odd)):
            block = block.reshape(r, S, 2 * L)
            for h in range(2):
                xl = slice((2 * t + h) * L, (2 * t + h + 1) * L)
                for i in range(r):
                    row = 2 * i + k
                    word = bits_ref[row // BITS, :, xl].astype(jnp.int32)
                    live = (word & (1 << (row % BITS))) != 0
                    d = jnp.where(live, block[i, :, h * L : (h + 1) * L], 0.0)
                    ig_ref[row, :, xl] = d.astype(bf16)


def input_gradient(d, bits, w, part, before):
    r, scan_count, wide = d.shape
    rows, lanes = (2 * (r - 1), 2 * (wide - L))
    steps = scan_count // S // 2
    at = lambda n, m: pl.BlockSpec((n, S, m), lambda g: (0, g + part * steps, 0))
    earlier = () if before is None else (before,)
    return pl.pallas_call(
        input_grad_kernel,
        grid=(steps,),
        in_specs=[at(r, wide), at(bits.shape[0], lanes), whole(w.shape)]
        + [pl.BlockSpec(memory_space=pl.ANY)] * len(earlier),
        out_specs=at(rows, lanes),
        out_shape=jax.ShapeDtypeStruct((rows, scan_count, lanes), bf16),
        input_output_aliases={3: 0} if earlier else {},
        compiler_params=params_of(),
        cost_estimate=cost(7),
        name="input_gradient",
    )(d, bits, w, *earlier)


def adam_step(weight_now, gradient, moment_one, moment_two, step_rate, decay_rate):
    first_new = adam_beta * moment_one + (1.0 - adam_beta) * gradient
    second_new = adam_beta * moment_two + (1.0 - adam_beta) * gradient * gradient
    correction = 1.0 - adam_beta**step_count
    update = first_new / correction / (jnp.sqrt(second_new / correction) + adam_eps)
    return (weight_now - step_rate * (update + decay_rate * weight_now), first_new, second_new)


def update_kernel(
    g_ref, s1_ref, s2_ref, k_ref, km_ref, kv_ref, n_ref, nm_ref, nv_ref, gn_ref, ok_ref, okm_ref,
    okv_ref, olow_ref, on_ref, onm_ref, onv_ref,
):
    norm_rows = []
    for ref in (s1_ref, s2_ref):
        shift_sum, gain_sum = sums_of(ref)
        norm_rows += [gain_sum[:, :C], shift_sum[:, :C]]
    g_norm = jnp.concatenate(norm_rows, axis=0)
    squares = jnp.sum(jnp.sum(g_ref[: 9 * C] ** 2, axis=0, keepdims=True), axis=1, keepdims=True)
    squares = squares + jnp.sum(
        jnp.sum(g_norm * g_norm, axis=0, keepdims=True), axis=1, keepdims=True
    )
    norm = jnp.sqrt(squares)
    gn_ref[...] = norm
    factor = jnp.minimum(1.0, clip_limit / norm)
    on, onm, onv = adam_step(
        n_ref[...], g_norm * factor, nm_ref[...], nv_ref[...], norm_rate, 0.0
    )
    on_ref[...] = on
    onm_ref[...] = onm
    onv_ref[...] = onv
    for layer in range(2):
        for a in range(5):
            width = L if a < 4 else C
            at = slice(a * L, a * L + width)
            if a == 4:
                g = g_ref[4 * C : 5 * C, layer * C : (layer + 1) * C]
            else:
                first = (a + 5 * layer) * C
                g = g_ref[first : first + C, :]
            k, km, kv = adam_step(
                k_ref[layer, :, at], g * factor, km_ref[layer, :, at], kv_ref[layer, :, at],
                kernel_rate, kernel_decay,
            )
            ok_ref[layer, :, at] = k
            okm_ref[layer, :, at] = km
            okv_ref[layer, :, at] = kv
            olow_ref[layer, :, at] = k.astype(bf16)


def update(grads, sums1, sums2, kt, kmt, kvt, norm_params, norm_m, norm_v):
    flat = lambda a: a.reshape(4, C)
    big = jax.ShapeDtypeStruct(kt.shape, f32)
    small = jax.ShapeDtypeStruct((4, C), f32)
    outs = [
        jax.ShapeDtypeStruct((1, 1), f32), big, big, big,
        jax.ShapeDtypeStruct(kt.shape, bf16), small, small, small,
    ]
    args = [grads, sums1, sums2, kt, kmt, kvt, flat(norm_params), flat(norm_m), flat(norm_v)]
    return pl.pallas_call(
        update_kernel,
        grid=(1,),
        in_specs=[whole(a.shape) for a in args],
        out_specs=[whole(o.shape) for o in outs],
        out_shape=outs,
        compiler_params=params_of(),
        cost_estimate=cost(3),
        name="update",
    )(*args)


def shifted(block, axis, distance):
    devices = range(lax.axis_size(axis))
    route = [(i - distance, i) for i in devices if i - distance in devices]
    return lax.ppermute(block, axis, route)


def exchange(rows):
    return lax.all_to_all(rows, BOTH, 0, 0, tiled=True)


def per_device(
    scan_features, occupancy, kernels, kernel_m, kernel_v, norm_params, norm_m, norm_v, cotangent
):
    x = jnp.transpose(scan_features, (1, 0, 2))
    cot = jnp.transpose(cotangent, (1, 0, 2))
    occ = jnp.transpose(occupancy, (2, 0, 1))
    kt, kmt, kvt = (jnp.transpose(a, (0, 2, 1)) for a in (kernels, kernel_m, kernel_v))
    gy, gx = (lax.axis_size("gy"), lax.axis_size("gx"))
    devices = gy * gx
    y, z = (lax.axis_index("gy"), lax.axis_index("gx"))
    flags = jnp.stack([y > 0, y < gy - 1, z > 0, z < gx - 1]).astype(jnp.int32)
    rows, scan_count, lanes = x.shape
    r, tiles = (rows // 2, lanes // L // 2)
    count = float(scan_count * r * tiles)
    last = (tiles - 1) * L

    bits, xrow, xcol, w1, w2, w2b, w1b, np2 = prepare(x, occ, kt, norm_params)
    down = shifted(jnp.concatenate([xrow, cot[r - 1]], axis=1), "gy", 1)
    cot_down = shifted(cot[:2], "gy", -1)
    xrow_in, cot_up = (down[:, :lanes], down[None, :, lanes:])
    xcol_in = shifted(jnp.concatenate([xrow_in[None, :, lanes - L :], xcol], axis=0), "gx", 1)
    packed = (r + 3) // 2

    def cot_column(at, first):
        column = jnp.concatenate(
            [a[:, :, at : at + C] for a in (cot_up, cot, cot_down)], axis=0
        )
        pieces = [column[:packed], column[packed:]]
        return jnp.concatenate(pieces[::first], axis=2)

    cot_left = shifted(cot_column(last + C, -1), "gx", 1)
    cot_right = shifted(cot_column(0, 1), "gx", -1)

    c1, st1, up, down, left, right = conv_one(x, bits, xrow_in, xcol_in, w1, devices)
    down_in = shifted(up, "gy", -1)
    up_in = shifted(down, "gy", 1)
    lines = lambda own, at: jnp.concatenate(
        [up_in[:, :, at : at + L], own, down_in[:, :, at : at + L]], axis=0
    )
    left_in = shifted(lines(right, last), "gx", 1)
    right_in = shifted(lines(left, 0), "gx", -1)
    st1 = exchange(st1)

    c2, n1, st2 = conv_two(flags, c1, up_in, down_in, left_in, right_in, st1, np2, w2, count)
    st2 = exchange(st2)
    features, d2, sums2 = output(c2, st2, np2, cot, cot_up, cot_down, cot_left, cot_right, count)
    sums2 = exchange(sums2)
    d1, edge, kg2, sums1 = back_two(flags, d2, c2, n1, st2, sums2, np2, w2b, count)
    edge = shifted(edge, "gx", -1)
    sums1 = exchange(sums1)
    d1, grads = back_one(flags, d1, edge, n1, x, bits, st1, sums1, np2, kg2, count)
    share = grads.shape[0] // devices
    grads = exchange(grads)
    input_grad = input_gradient(d1, bits, w1b, 0, None)
    mine = jnp.sum(grads.reshape(devices, share, L), axis=0)
    grads = exchange(jnp.broadcast_to(mine[None], (devices, share, L)).reshape(-1, L))
    input_grad = input_gradient(d1, bits, w1b, 1, input_grad)
    norm, k, km, kv, low, n, nm, nv = update(
        grads, sums1, sums2, kt, kmt, kvt, norm_params, norm_m, norm_v
    )
    back = lambda a: jnp.transpose(a, (0, 2, 1))
    deep = lambda a: a.reshape(norm_params.shape)
    return (
        jnp.transpose(features, (1, 0, 2)),
        jnp.transpose(input_grad, (1, 0, 2)),
        norm.reshape(()),
        back(k),
        back(km),
        back(kv),
        back(low),
        deep(n),
        deep(nm),
        deep(nv),
    )


def solution(mesh):
    split = P(None, "gy", "gx")
    return jax.shard_map(
        per_device,
        mesh=mesh,
        in_specs=(split, split) + (P(),) * 6 + (split,),
        out_specs=(split, split) + (P(),) * 8,
        check_vma=False,
    )
```

```python
import functools
import math

import jax
import jax.numpy as jnp
from jax import lax
from jax.experimental import pallas as pl
from jax.experimental.pallas import tpu as pltpu
from jax.sharding import PartitionSpec as P

norm_eps = 1e-05
adam_beta = 0.5
adam_eps = 1e-08
step_count = 5
clip_limit = 1.0
kernel_rate = 0.04
norm_rate = 0.25
kernel_decay = 0.01

f32, bf16 = (jnp.float32, jnp.bfloat16)
BOTH = ("gy", "gx")
S, C, L, BITS = (16, 64, 128, 13)


def params_of(limit=56):
    return pltpu.CompilerParams(
        dimension_semantics=("arbitrary",), vmem_limit_bytes=limit << 20
    )


def cost(microseconds):
    return pl.CostEstimate(
        flops=0, bytes_accessed=int(microseconds * 3.6e6), transcendentals=0
    )


def whole(shape):
    return pl.BlockSpec(shape, lambda g: (0,) * len(shape))


def scans(rows, lanes):
    return pl.BlockSpec((rows, S, lanes), lambda g: (0, g, 0))


def low_half(rows=S):
    return lax.broadcasted_iota(jnp.int32, (rows, L), 1) < C


def swap(x):
    return pltpu.roll(x, C, 1)


def fold(x):
    x = jnp.broadcast_to(x, (8, L))
    return (x + swap(x))[:1]


def live(word, row, x):
    bit = 1 << (row % BITS)
    if x.dtype == bf16:
        return jnp.where((word & jnp.int16(bit)) != 0, x, jnp.zeros_like(x))
    return jnp.where((word.astype(jnp.int32) & bit) != 0, x, 0.0)


def pair(ref, row, t):
    return ref[row, :, t * L : (t + 1) * L]


def stats_of(st_ref, count):
    groups = 2 * st_ref.shape[0]
    means = st_ref[:, 0, :]
    mean = fold(jnp.sum(means, axis=0, keepdims=True)) / groups
    spread = st_ref[:, 1, :] + count * (means - mean) ** 2
    spread = fold(jnp.sum(spread, axis=0, keepdims=True)) / (groups * count)
    return (mean, lax.rsqrt(spread + norm_eps))


def sums_of(st_ref):
    return tuple(fold(jnp.sum(st_ref[:, k, :], axis=0, keepdims=True)) for k in range(2))


def pilot_of(block):
    flat = block.reshape(-1, L)
    return jnp.sum(flat, axis=0, keepdims=True) / flat.shape[0]


def finish_stats(step, steps, pilot, sums, count, run_ref, st_ref):
    off, squares = (jnp.sum(s, axis=0, keepdims=True) for s in sums)
    mean = pilot + off / count
    squares = squares - off * off / count

    @pl.when(step == 0)
    def _():
        run_ref[0:1] = mean
        run_ref[1:2] = squares

    @pl.when(step > 0)
    def _():
        before = step.astype(f32)
        share = 1.0 / (before + 1.0)
        delta = mean - run_ref[0:1]
        run_ref[0:1] = run_ref[0:1] + delta * share
        run_ref[1:2] = run_ref[1:2] + squares + delta * delta * (count * before * share)

    @pl.when(step == steps - 1)
    def _():
        st_ref[...] = jnp.broadcast_to(run_ref[0:2][None], st_ref.shape)


def off_sums(blocks, pilot):
    sums = [jnp.zeros((8, L), f32), jnp.zeros((8, L), f32)]
    for block in blocks:
        d = block - pilot
        sums = [sums[0] + halves(d), sums[1] + halves(d * d)]
    return sums


def added(a, b):
    return b if a is None else [x + y for x, y in zip(a, b)]


def rim_of(first, second, row, low):
    half = first.shape[0]
    if row < half:
        return jnp.where(low, first[row].astype(f32), second[row].astype(f32))
    row = row - half
    return swap(jnp.where(low, second[row].astype(f32), first[row].astype(f32)))


def halves(x):
    return x[:8] + x[8:]


def occupancy_words(occ, groups, first):
    rows = occ.shape[1]
    shape = (rows, groups * L)
    group_of = lax.broadcasted_iota(jnp.int32, shape, 1) // L + first
    inner = lax.broadcasted_iota(jnp.int32, shape, 0) - group_of * BITS
    power = jnp.where(
        (inner >= 0) & (inner < BITS), (1 << jnp.clip(inner, 0, BITS)), 0
    ).astype(bf16)
    low = occ.astype(f32).astype(bf16)
    return jnp.dot(low, power, preferred_element_type=f32).astype(jnp.int32)


def edges_kernel(
    row_ref, col_ref, occ_ref, cot_last_ref, cot_first_ref, down_ref, up_ref, corner_ref, xcol_ref
):
    cols, scan_count, rows = occ_ref.shape
    lanes = row_ref.shape[2]
    groups = -(-rows // BITS)
    low = low_half(scan_count)
    words = occupancy_words(occ_ref[...].reshape(cols * scan_count, rows), 1, groups - 1)
    words = words.reshape(cols // 2, 2, scan_count, L)
    for t in range(cols // 2):
        word = jnp.where(low, words[t, 0], words[t, 1])
        x = live(word, rows - 1, row_ref[0, :, t * L : (t + 1) * L].astype(f32)).astype(bf16)
        down_ref[:, t * L : (t + 1) * L] = x
    corner_ref[...] = x
    down_ref[:, lanes:] = cot_last_ref[0]
    up_ref[...] = cot_first_ref[...]
    words = occupancy_words(occ_ref[cols - 1], groups, 0)
    for i in range(rows // 2):
        even, odd = (
            live(
                words[:, row // BITS * L : (row // BITS + 1) * L], row, col_ref[row].astype(f32)
            )
            for row in (2 * i, 2 * i + 1)
        )
        xcol_ref[i] = jnp.where(low, swap(even), odd).astype(bf16)


def edges(x, occ, cot):
    rows, scan_count, lanes = x.shape
    r, wide = (rows // 2, lanes // 2)
    outs = [
        jax.ShapeDtypeStruct((scan_count, lanes + wide), bf16),
        jax.ShapeDtypeStruct((2, scan_count, wide), bf16),
        jax.ShapeDtypeStruct((scan_count, L), bf16),
        jax.ShapeDtypeStruct((r, scan_count, L), bf16),
    ]
    return pl.pallas_call(
        edges_kernel,
        grid=(1,),
        in_specs=[
            pl.BlockSpec((1, scan_count, lanes), lambda g: (rows - 1, 0, 0)),
            pl.BlockSpec((rows, scan_count, L), lambda g: (0, 0, lanes // L - 1)),
            whole(occ.shape),
            pl.BlockSpec((1, scan_count, wide), lambda g: (r - 1, 0, 0)),
            pl.BlockSpec((2, scan_count, wide), lambda g: (0, 0, 0)),
        ],
        out_specs=[whole(o.shape) for o in outs],
        out_shape=outs,
        compiler_params=params_of(),
        cost_estimate=cost(3),
        name="edges",
    )(x, x, occ, cot, cot)


def prep_kernel(occ_ref, kt_ref, np_ref, bits_ref, w1_ref, w2_ref, w2b_ref, w1b_ref, np2_ref):
    cols, scan_count, rows = occ_ref.shape
    groups = bits_ref.shape[0]
    words = occupancy_words(occ_ref[...].reshape(cols * scan_count, rows), groups, 0)
    words = words.reshape(cols // 2, 2, scan_count, groups * L)
    low = low_half(scan_count)
    for g in range(groups):
        for t in range(cols // 2):
            lanes = slice(g * L, (g + 1) * L)
            word = jnp.where(low, words[t, 0, :, lanes], words[t, 1, :, lanes])
            bits_ref[g, :, t * L : (t + 1) * L] = word.astype(jnp.int16)
    back = [[kt_ref[l, :, k * C : (k + 1) * C] for k in range(9)] for l in range(2)]
    fore = [[jnp.transpose(b) for b in layer] for layer in back]
    none = jnp.zeros((C, C), f32)

    def put(ref, rows_of, cols_of, pick):
        for a in range(rows_of):
            blocks = [pick(a, b) for b in range(cols_of)]
            for k in range(0, cols_of, 2):
                two = jnp.concatenate(blocks[k : k + 2], axis=1).astype(bf16)
                ref[a * C : (a + 1) * C, k * C : (k + 2) * C] = two

    def tap(table, p, q):
        return table[3 * p + q] if 0 <= p < 3 and 0 <= q < 3 else none

    put(w1_ref, 30, 4, lambda a, b: tap(fore[0], a // 6 - 2 * (b // 2), a % 6 - 2 * (b % 2) - 1))
    put(w2_ref, 16, 4, lambda a, b: tap(fore[1], a // 4 - b // 2, a % 4 - b % 2))
    put(w2b_ref, 16, 4, lambda a, b: tap(back[1], b // 2 + 2 - a // 4, b % 2 + 2 - a % 4))
    put(w1b_ref, 12, 4, lambda a, b: tap(back[0], (1, 2, 0)[a // 4], b + 3 - 2 * (a % 4)))
    np2_ref[...] = jnp.concatenate([np_ref[...], np_ref[...]], axis=1)


def prepare(occ, kt, norm_params):
    cols, scan_count, rows = occ.shape
    full = lambda *shape: jax.ShapeDtypeStruct(shape, bf16)
    outs = [
        jax.ShapeDtypeStruct((-(-rows // BITS), scan_count, cols * C), jnp.int16),
        full(30 * C, 4 * C),
        full(16 * C, 4 * C),
        full(16 * C, 4 * C),
        full(12 * C, 4 * C),
        jax.ShapeDtypeStruct((4, L), f32),
    ]
    return pl.pallas_call(
        prep_kernel,
        grid=(1,),
        in_specs=[whole(occ.shape), whole(kt.shape), whole((4, C))],
        out_specs=[whole(o.shape) for o in outs],
        out_shape=outs,
        compiler_params=params_of(),
        cost_estimate=cost(4),
        name="prepare",
    )(occ, kt, norm_params.reshape(4, C))


def mask_tile(x_ref, bits_ref, t, xs, into):
    rows = x_ref.shape[0]
    for g in range(bits_ref.shape[0]):
        word = bits_ref[g, :, t * L : (t + 1) * L]
        for row in range(g * BITS, min(rows, (g + 1) * BITS)):
            x = live(word, row, pair(x_ref, row, t))
            xs[(row + 1) // 4, (row + 1) % 4, :, into * L : (into + 1) * L] = x


def clear_rows(rows, pairs, xs):
    for k in range(rows + 1, 4 * pairs + 1):
        xs[k // 4, k % 4] = jnp.zeros_like(xs[0, 0])


def conv_rows(xs, lanes, w, r):
    pairs = (r + 1) // 2
    pieces = [xs[0:pairs, q, :, lanes] for q in range(4)] + [xs[1 : pairs + 1, 0, :, lanes]]
    lhs = jnp.concatenate([p.reshape(pairs * S, p.shape[2]) for p in pieces], axis=1)
    acc = jnp.dot(lhs, w, preferred_element_type=f32).reshape(pairs, S, 2 * L)
    return [acc[i // 2, :, (i % 2) * L : (i % 2 + 1) * L] for i in range(r)]


def first_last_kernel(
    xa_ref, xb_ref, ba_ref, bb_ref, xrow_ref, xcol_ref, corner_ref, w_ref, c_ref, st_ref, er_ref,
    el_ref, edge_ref, xs, run,
):
    step, steps = (pl.program_id(0), pl.num_programs(0))
    rows, lanes = (xa_ref.shape[0], xrow_ref.shape[1] * 2 // 3)
    r = rows // 2
    low = low_half()

    @pl.when(step == 0)
    def _():
        clear_rows(rows, (r + 1) // 2, xs)

    xs[0, 0, :, L : 2 * L] = xrow_ref[:, :L]
    xs[0, 0, :, 2 * L :] = xrow_ref[:, lanes - 2 * L : lanes]
    xs[0, 0, :, :L] = corner_ref[...]
    for i in range(r):
        k = 2 * i + 2
        xs[k // 4, k % 4, :, :L] = xcol_ref[i]
        k = 2 * i + 1
        xs[k // 4, k % 4, :, :L] = swap(xcol_ref[i].astype(f32)).astype(bf16)
    mask_tile(xa_ref, ba_ref, 0, xs, 1)
    mask_tile(xb_ref, bb_ref, 0, xs, 2)
    mask_tile(xb_ref, bb_ref, 1, xs, 3)
    wide = 3 * L
    some = lambda a: jnp.concatenate(
        [w_ref[q * wide + a * L : q * wide + (a + 2) * L] for q in range(5)], axis=0
    )
    last = conv_rows(xs, slice(2 * L, 4 * L), some(0), r)
    first = conv_rows(xs, slice(0, 2 * L), some(1), r)
    edge = [jnp.where(low, b, a) for a, b in zip(first, last)]
    pilot = pilot_of(jnp.concatenate(edge[: r // 2], axis=0))
    for i in range(r):
        c_ref[i, :, :L] = first[i]
        c_ref[i, :, L:] = last[i]
        edge_ref[i] = edge[i].astype(bf16)
    finish_stats(step, steps, pilot, off_sums(edge, pilot), float(r * S), run, st_ref)
    half = er_ref.shape[0]
    for k in range(half):
        far = swap(edge[k + half]) if k + half < r else jnp.zeros((S, L), f32)
        er_ref[k] = jnp.where(low, edge[k], far).astype(bf16)
        el_ref[k] = jnp.where(low, far, edge[k]).astype(bf16)


def first_last(x, bits, down, xcol, corner, w):
    rows, scan_count, lanes = x.shape
    r = rows // 2
    shape = lambda dtype, *s: jax.ShapeDtypeStruct(s, dtype)
    at = lambda n, width, k: pl.BlockSpec((n, S, width), lambda g: (0, g, k))
    end = lanes // (2 * L) - 1
    return pl.pallas_call(
        first_last_kernel,
        grid=(scan_count // S,),
        in_specs=[
            at(rows, L, 0),
            at(rows, 2 * L, end),
            at(bits.shape[0], L, 0),
            at(bits.shape[0], 2 * L, end),
            pl.BlockSpec((S, down.shape[1]), lambda g: (g, 0)),
            scans(r, L),
            pl.BlockSpec((S, L), lambda g: (g, 0)),
            whole(w.shape),
        ],
        out_specs=[
            scans(r, 2 * L),
            whole((1, 2, L)),
            scans((r + 1) // 2, L),
            scans((r + 1) // 2, L),
            scans(r, L),
        ],
        out_shape=[
            shape(f32, r, scan_count, 2 * L),
            shape(f32, 1, 2, L),
            shape(bf16, (r + 1) // 2, scan_count, L),
            shape(bf16, (r + 1) // 2, scan_count, L),
            shape(bf16, r, scan_count, L),
        ],
        scratch_shapes=[
            pltpu.VMEM(((r + 1) // 2 + 1, 4, S, 4 * L), bf16),
            pltpu.VMEM((8, L), f32),
        ],
        compiler_params=params_of(),
        cost_estimate=cost(5),
        name="conv_one_ends",
    )(x, x, bits, bits, down, xcol, corner, w)


def conv_one_kernel(
    x_ref, bits_ref, xrow_ref, ends_ref, w_ref, c_ref, st_ref, up_ref, down_ref, xs, run
):
    step, steps = (pl.program_id(0), pl.num_programs(0))
    rows, tiles = (x_ref.shape[0], x_ref.shape[2] // L)
    r, inner = (rows // 2, tiles // 2 - 1)

    @pl.when(step == 0)
    def _():
        clear_rows(rows, (r + 1) // 2, xs)

    xs[0, 0] = xrow_ref[:, : tiles * L]
    sums, pilot = (None, None)
    filled = 0
    for t in range(inner):
        while filled < 2 * t + 3:
            mask_tile(x_ref, bits_ref, filled, xs, filled)
            filled += 1
        blocks = conv_rows(xs, slice(2 * t * L, (2 * t + 3) * L), w_ref[...], r)
        if pilot is None:
            pilot = pilot_of(jnp.concatenate(blocks[: r // 2], axis=0))
        sums = added(sums, off_sums(blocks, pilot))
        for i, block in enumerate(blocks):
            c_ref[i, :, t * L : (t + 1) * L] = block
    finish_stats(step, steps, pilot, sums, float(r * inner * S), run, st_ref)
    up_ref[...] = c_ref[0:3].astype(bf16)
    down_ref[...] = c_ref[r - 2 : r].astype(bf16)

    @pl.when(step == steps - 1)
    def _():
        own, more = (float(r * S) * steps * n for n in (inner, 1))
        delta = ends_ref[0, 0:1] - run[0:1]
        mean = run[0:1] + delta * (more / (own + more))
        squares = run[1:2] + ends_ref[0, 1:2] + delta * delta * (own * more / (own + more))
        row = jnp.concatenate([mean, squares], axis=0)
        st_ref[...] = jnp.broadcast_to(row[None], st_ref.shape)


def conv_one(x, bits, down, ends, w, devices):
    rows, scan_count, lanes = x.shape
    r, wide = (rows // 2, lanes // 2 - L)
    shape = lambda dtype, *s: jax.ShapeDtypeStruct(s, dtype)
    return pl.pallas_call(
        conv_one_kernel,
        grid=(scan_count // S,),
        in_specs=[
            scans(rows, lanes),
            scans(bits.shape[0], lanes),
            pl.BlockSpec((S, down.shape[1]), lambda g: (g, 0)),
            whole(ends.shape),
            whole(w.shape),
        ],
        out_specs=[
            scans(r, wide),
            whole((devices, 2, L)),
            scans(3, wide),
            scans(2, wide),
        ],
        out_shape=[
            shape(f32, r, scan_count, wide),
            shape(f32, devices, 2, L),
            shape(bf16, 3, scan_count, wide),
            shape(bf16, 2, scan_count, wide),
        ],
        scratch_shapes=[
            pltpu.VMEM(((r + 1) // 2 + 1, 4, S, lanes), bf16),
            pltpu.VMEM((8, L), f32),
        ],
        compiler_params=params_of(),
        cost_estimate=cost(13),
        name="conv_one",
    )(x, bits, down, ends, w)


def conv_two_kernel(
    flags, c_ref, ends_ref, up_ref, down_ref, left_ref, right_ref, st_ref, np_ref, w_ref, c2_ref,
    n1_ref, hid_ref, st2_ref, hs, rim, run, *, count,
):
    step, steps = (pl.program_id(0), pl.num_programs(0))
    r, tiles = (c_ref.shape[0], c_ref.shape[2] // L + 2)
    t_out = tiles - 1
    mean, inv = stats_of(st_ref, count)
    offset = -mean * inv
    scale = 0.5 * np_ref[0:1] * inv
    shift = 0.5 * (np_ref[0:1] * offset + np_ref[1:2])
    f_up, f_down, f_left, f_right = (flags[k].astype(f32) for k in range(4))
    low = low_half()
    left = jnp.where(low, f_left, 1.0)
    right = jnp.where(low, 1.0, f_right)
    for row in range(r):
        rim[row] = rim_of(left_ref, right_ref, row, low)

    def act(row, t):
        ends = (0, tiles - 1)
        if 2 <= row < r + 2:
            flag = None
            c = pair(ends_ref, row - 2, min(t, 1)) if t in ends else pair(c_ref, row - 2, t - 1)
            beyond = rim[row - 2] if t in ends else None
        else:
            src, k, flag = (up_ref, row, f_up) if row < 2 else (down_ref, row - r - 2, f_down)
            c = pair(src, k, tiles - 2 if t in ends else t - 1).astype(f32)
            beyond = pair(src, k, tiles - 1).astype(f32) if t in ends else None
        if t == 0:
            c = jnp.where(low, beyond, c)
        if t == tiles - 1:
            c = jnp.where(low, c, beyond)
        h = c * scale + shift
        out = h + h * jnp.tanh(h)
        if t == 0:
            out = out * left
        if t == tiles - 1:
            out = out * right
        if flag is not None:
            out = out * flag
        out = out.astype(bf16)
        hs[row // 2, row % 2, :, t * L : (t + 1) * L] = out
        if 1 <= row < r + 3:
            hid_ref[row - 1, :, t * L : (t + 1) * L] = out
        if 2 <= row < r + 3:
            n1_ref[row - 2, :, t * L : (t + 1) * L] = (c * inv + offset).astype(bf16)

    pairs = (r + 3) // 2
    sums, pilot = (None, None)
    for t in range(tiles):
        for row in range(r + 5):
            act(row, t)
        k = t - 1
        if k < 0:
            continue
        lanes = slice(k * L, (k + 2) * L)
        pieces = [hs[a : a + pairs, b, :, lanes] for a in range(2) for b in range(2)]
        lhs = jnp.concatenate([p.reshape(pairs * S, 2 * L) for p in pieces], axis=1)
        acc = jnp.dot(lhs, w_ref[...], preferred_element_type=f32).reshape(pairs, S, 2 * L)
        if pilot is None:
            pilot = pilot_of(acc[1 : r // 2, :, :L])
        blocks = []
        for row in range(r + 3):
            block = acc[row // 2, :, (row % 2) * L : (row % 2 + 1) * L]
            c2_ref[row, :, k * L : (k + 1) * L] = block
            if 0 < row <= r:
                blocks.append(block)
        sums = added(sums, off_sums(blocks, pilot))
    finish_stats(step, steps, pilot, sums, float(r * t_out * S), run, st2_ref)


def conv_two(flags, c1, ends, up, down, left, right, st, np2, w, count):
    r, scan_count, wide = c1.shape
    wide = wide + 2 * L
    lanes = wide - L
    devices = st.shape[0]
    return pl.pallas_call(
        functools.partial(conv_two_kernel, count=count),
        grid=(scan_count // S,),
        in_specs=[
            pl.BlockSpec(memory_space=pltpu.SMEM),
            scans(r, wide - 2 * L),
            scans(r, 2 * L),
            scans(2, wide),
            scans(3, wide),
            scans(left.shape[0], L),
            scans(right.shape[0], L),
            whole(st.shape),
            whole(np2.shape),
            whole(w.shape),
        ],
        out_specs=[
            scans(r + 3, lanes),
            scans(r + 1, wide),
            scans(r + 2, wide),
            whole((devices, 2, L)),
        ],
        out_shape=[
            jax.ShapeDtypeStruct((r + 3, scan_count, lanes), f32),
            jax.ShapeDtypeStruct((r + 1, scan_count, wide), bf16),
            jax.ShapeDtypeStruct((r + 2, scan_count, wide), bf16),
            jax.ShapeDtypeStruct((devices, 2, L), f32),
        ],
        scratch_shapes=[
            pltpu.VMEM(((r + 5) // 2, 2, S, wide), bf16),
            pltpu.VMEM((r, S, L), f32),
            pltpu.VMEM((8, L), f32),
        ],
        compiler_params=params_of(),
        cost_estimate=cost(14),
        name="conv_two",
    )(flags, c1, ends, up, down, left, right, st, np2, w)


def output_kernel(
    c2_ref, st_ref, np_ref, cot_ref, up_ref, down_ref, feat_ref, d_ref, sum_ref, run, *, count,
):
    step, steps = (pl.program_id(0), pl.num_programs(0))
    r, tiles = (cot_ref.shape[0], cot_ref.shape[2] // L)
    mean, inv = stats_of(st_ref, count)
    offset = -mean * inv
    scale = 0.5 * np_ref[2:3] * inv
    shift = 0.5 * (np_ref[2:3] * offset + np_ref[3:4])
    above = 2 * tiles

    def slope(c, cot):
        h = c * scale + shift
        t = jnp.tanh(h)
        plus = 1.0 + t
        return (h * plus, (0.5 * cot.astype(f32)) * (plus * (1.0 + h * (1.0 - t))))

    def own(i, sums):
        for t in range(tiles):
            c = pair(c2_ref, i + 1, t)
            f, d = slope(c, pair(cot_ref, i, t))
            feat_ref[i, :, t * L : (t + 1) * L] = f.astype(bf16)
            d_ref[i + 1, :, t * L : (t + 1) * L] = d
            sums = (sums[0] + halves(d), sums[1] + halves(d * (c * inv + offset)))
        return sums

    zero = jnp.zeros((8, L), f32)
    sums = lax.fori_loop(0, r, own, (zero, zero))
    for t in range(tiles):
        lanes = slice(t * L, (t + 1) * L)
        cot = up_ref[:, (above + t) * L : (above + t + 1) * L]
        d_ref[0, :, lanes] = slope(pair(c2_ref, 0, t), cot)[1]
        for k in range(2):
            row = r + 1 + k
            d_ref[row, :, lanes] = slope(pair(c2_ref, row, t), pair(down_ref, k, t))[1]
    add_sums(step, steps, sums, run, sum_ref)


def add_sums(step, steps, sums, run, sum_ref):
    rows = jnp.concatenate([jnp.sum(s, axis=0, keepdims=True) for s in sums], axis=0)

    @pl.when(step == 0)
    def _():
        run[0:2] = rows

    @pl.when(step > 0)
    def _():
        run[0:2] = run[0:2] + rows

    @pl.when(step == steps - 1)
    def _():
        sum_ref[...] = jnp.broadcast_to(run[0:2][None], sum_ref.shape)


def output(c2, st, np2, cot, up, down, count):
    r, scan_count, lanes = cot.shape
    devices = st.shape[0]
    return pl.pallas_call(
        functools.partial(output_kernel, count=count),
        grid=(scan_count // S,),
        in_specs=[
            scans(r + 3, lanes),
            whole(st.shape),
            whole(np2.shape),
            scans(r, lanes),
            pl.BlockSpec((S, up.shape[1]), lambda g: (g, 0)),
            scans(2, lanes),
        ],
        out_specs=[scans(r, lanes), scans(r + 3, lanes), whole((devices, 2, L))],
        out_shape=[
            jax.ShapeDtypeStruct((r, scan_count, lanes), bf16),
            jax.ShapeDtypeStruct((r + 3, scan_count, lanes), f32),
            jax.ShapeDtypeStruct((devices, 2, L), f32),
        ],
        scratch_shapes=[pltpu.VMEM((8, L), f32)],
        compiler_params=params_of(),
        cost_estimate=cost(12),
        name="output",
    )(c2, st, np2, cot, up, down)


def norm_back_two(flags, st_ref, sum_ref, np_ref, count, rows):
    cells = 2.0 * count * st_ref.shape[0]
    mean, inv = stats_of(st_ref, count)
    shift_sum, gain_sum = sums_of(sum_ref)
    gain = np_ref[2:3] * inv
    c_n = -gain * inv * gain_sum / cells
    c_0 = -gain * shift_sum / cells - c_n * mean
    f_up, f_down = (flags[k].astype(f32) for k in range(2))

    def back(row, d, c):
        d = d * gain + (c * c_n + c_0)
        if isinstance(row, int):
            if row == 0:
                d = d * f_up
            if row > rows:
                d = d * f_down
        return d

    return back


def rim_two_kernel(
    flags, da_ref, db_ref, ca_ref, cb_ref, st_ref, sum_ref, np_ref, er_ref, el_ref, *, count
):
    rows = da_ref.shape[0]
    back = norm_back_two(flags, st_ref, sum_ref, np_ref, count, rows - 3)
    low = low_half()
    half = rows // 2
    both = lambda row: jnp.where(
        low, back(row, da_ref[row], ca_ref[row]), back(row, db_ref[row], cb_ref[row])
    )
    for k in range(half):
        near, far = (both(k), swap(both(k + half)))
        el_ref[k] = jnp.where(low, near, far).astype(bf16)
        er_ref[k] = jnp.where(low, far, near).astype(bf16)


def rim_two(flags, d, c2, st, sums, np2, count):
    rows, scan_count, lanes = d.shape
    at = lambda k: pl.BlockSpec((rows, S, L), lambda g: (0, g, k))
    last = lanes // L - 1
    return pl.pallas_call(
        functools.partial(rim_two_kernel, count=count),
        grid=(scan_count // S,),
        in_specs=[
            pl.BlockSpec(memory_space=pltpu.SMEM), at(0), at(last), at(0), at(last),
            whole(st.shape), whole(sums.shape), whole(np2.shape),
        ],
        out_specs=[scans(rows // 2, L)] * 2,
        out_shape=[jax.ShapeDtypeStruct((rows // 2, scan_count, L), bf16)] * 2,
        compiler_params=params_of(),
        cost_estimate=cost(3),
        name="rim_two",
    )(flags, d, d, c2, c2, st, sums, np2)


def back_two_kernel(
    flags, d_ref, c2_ref, hid_ref, st_ref, sum_ref, np_ref, ds_ref, kg_ref, grad, *, count
):
    step, steps = (pl.program_id(0), pl.num_programs(0))
    r, tiles = (c2_ref.shape[0] - 3, c2_ref.shape[2] // L)
    back = norm_back_two(flags, st_ref, sum_ref, np_ref, count, r)

    @pl.when(step == 0)
    def _():
        grad[...] = jnp.zeros_like(grad)

    total = None
    for t in range(tiles):
        for row in range(r + 3):
            d = back(row, pair(d_ref, row, t), pair(c2_ref, row, t))
            ds_ref[row, :, t * L : (t + 1) * L] = d.astype(bf16)
        lanes = slice(t * L, (t + 2) * L)
        rhs = jnp.concatenate(
            [hid_ref[p : p + r, :, lanes].reshape(r * S, 2 * L) for p in range(3)], axis=1
        )
        lhs = ds_ref[1 : r + 1, :, t * L : (t + 1) * L].reshape(r * S, L)
        part = lax.dot_general(lhs, rhs, (((0,), (0,)), ((), ())), preferred_element_type=f32)
        total = part if total is None else total + part
    grad[...] += total

    @pl.when(step == steps - 1)
    def _():
        for p in range(3):
            for q in range(3):
                block = None
                for w in range(2):
                    at = 4 * p * C + (w + q) * C
                    part = grad[w * C : (w + 1) * C, at : at + C]
                    block = part if block is None else block + part
                kg_ref[3 * p + q] = block


def back_two(flags, d, c2, hid, st, sums, np2, count):
    r, scan_count, wide = hid.shape
    r, lanes = (r - 2, wide - L)
    return pl.pallas_call(
        functools.partial(back_two_kernel, count=count),
        grid=(scan_count // S,),
        in_specs=[
            pl.BlockSpec(memory_space=pltpu.SMEM),
            scans(r + 3, lanes),
            scans(r + 3, lanes),
            scans(r + 2, wide),
            whole(st.shape),
            whole(sums.shape),
            whole(np2.shape),
        ],
        out_specs=[scans(r + 3, lanes), whole((9, C, C))],
        out_shape=[
            jax.ShapeDtypeStruct((r + 3, scan_count, lanes), bf16),
            jax.ShapeDtypeStruct((9, C, C), f32),
        ],
        scratch_shapes=[pltpu.VMEM((L, 12 * C), f32)],
        compiler_params=params_of(),
        cost_estimate=cost(12),
        name="back_two",
    )(flags, d, c2, hid, st, sums, np2)


def hidden_kernel(
    ds_ref, left_ref, right_ref, n1_ref, np_ref, w_ref, dp_ref, edge_ref, sum1_ref, rim, run
):
    step, steps = (pl.program_id(0), pl.num_programs(0))
    r, tiles = (n1_ref.shape[0] - 1, n1_ref.shape[2] // L)
    pairs = (r + 1) // 2
    low = low_half()
    for row in range(r + 3):
        rim[row] = rim_of(right_ref, left_ref, row, low).astype(bf16)
    sums = None
    for t in range(tiles):
        parts = []
        for k in (t - 1, t):
            part = ds_ref[:, :, k * L : (k + 1) * L] if 0 <= k < tiles - 1 else rim[...]
            parts.append(part.reshape(pairs + 1, 2, S, L))
        pieces = [p[a : a + pairs, b] for a in range(2) for b in range(2) for p in parts]
        lhs = jnp.concatenate([p.reshape(pairs * S, L) for p in pieces], axis=1)
        acc = jnp.dot(lhs, w_ref[...], preferred_element_type=f32).reshape(pairs, S, 2 * L)
        part = [jnp.zeros((8, L), f32), jnp.zeros((8, L), f32)]
        for i in range(r + 1):
            n = pair(n1_ref, i, t).astype(f32)
            h = 0.5 * (n * np_ref[0:1] + np_ref[1:2])
            tan = jnp.tanh(h)
            d = acc[i // 2, :, (i % 2) * L : (i % 2 + 1) * L]
            d = (0.5 * d) * ((1.0 + tan) * (1.0 + h * (1.0 - tan)))
            dp_ref[i, :, t * L : (t + 1) * L] = d
            if i < r:
                if t == 0:
                    d = jnp.where(low, 0.0, d)
                if t == tiles - 1:
                    d = jnp.where(low, d, 0.0)
                part = [part[0] + halves(d), part[1] + halves(d * n)]
        sums = added(sums, part)
    add_sums(step, steps, sums, run, sum1_ref)
    for i in range(pairs):
        both = jnp.where(low, swap(pair(dp_ref, pairs + i, 0)), pair(dp_ref, i, 0))
        edge_ref[i] = both.astype(bf16)


def hidden_gradient(ds, left, right, n1, np2, w, devices):
    r, scan_count, wide = n1.shape
    r, lanes = (r - 1, wide - L)
    half = left.shape[0]
    return pl.pallas_call(
        hidden_kernel,
        grid=(scan_count // S,),
        in_specs=[
            scans(r + 3, lanes),
            scans(half, L),
            scans(half, L),
            scans(r + 1, wide),
            whole(np2.shape),
            whole(w.shape),
        ],
        out_specs=[
            scans(r + 1, wide),
            scans((r + 1) // 2, L),
            whole((devices, 2, L)),
        ],
        out_shape=[
            jax.ShapeDtypeStruct((r + 1, scan_count, wide), f32),
            jax.ShapeDtypeStruct(((r + 1) // 2, scan_count, L), bf16),
            jax.ShapeDtypeStruct((devices, 2, L), f32),
        ],
        scratch_shapes=[pltpu.VMEM((r + 3, S, L), bf16), pltpu.VMEM((8, L), f32)],
        compiler_params=params_of(),
        cost_estimate=cost(12),
        name="hidden_gradient",
    )(ds, left, right, n1, np2, w)


def back_one_kernel(
    flags, dp_ref, edge_ref, n1_ref, x_ref, bits_ref, st_ref, sum_ref, np_ref, kg2_ref, ds, kg_ref,
    xm, grad, *, count,
):
    step, steps = (pl.program_id(0), pl.num_programs(0))
    r, tiles = (n1_ref.shape[0] - 1, n1_ref.shape[2] // L - 1)
    cells = 2.0 * count * st_ref.shape[0]
    _mean, inv = stats_of(st_ref, count)
    shift_sum, gain_sum = sums_of(sum_ref)
    gain = np_ref[0:1] * inv
    c_n = -gain * gain_sum / cells
    c_0 = -gain * shift_sum / cells
    f_down, f_right = (flags[1].astype(f32), flags[3].astype(f32))
    packed = edge_ref.shape[0]
    low = low_half()
    right = jnp.where(low, 1.0, f_right)

    @pl.when(step == 0)
    def _():
        grad[...] = jnp.zeros_like(grad)

    def line(i, t):
        d = pair(dp_ref, i, t)
        if t == tiles:
            beyond = edge_ref[i % packed].astype(f32)
            d = jnp.where(low, d, swap(beyond) if i >= packed else beyond)
        d = d * gain + (pair(n1_ref, i, t).astype(f32) * c_n + c_0)
        if t == tiles:
            d = d * right
        if i == r:
            d = d * f_down
        ds[i, :, t * L : (t + 1) * L] = d.astype(bf16)

    turned = (((0,), (0,)), ((), ()))
    totals = [None, None, None]
    done = 0
    for t in range(tiles):
        while done < t + 2:
            for i in range(r + 1):
                line(i, done)
            done += 1
        for k in (2 * t, 2 * t + 1):
            for g in range(bits_ref.shape[0]):
                word = bits_ref[g, :, k * L : (k + 1) * L]
                for row in range(g * BITS, min(2 * r, (g + 1) * BITS)):
                    x = live(word, row, pair(x_ref, row, k))
                    xm[row % 2, row // 2, :, k * L : (k + 1) * L] = x
        lanes = slice(t * L, (t + 2) * L)
        xl = slice(2 * t * L, 2 * (t + 1) * L)
        rows = [ds[a : a + r, :, lanes].reshape(r * S, 2 * L) for a in range(2)]
        xe, xo = (xm[a, :, :, xl].reshape(r * S, 2 * L) for a in range(2))
        for k, (a, b) in enumerate(((xe, rows[0]), (xo, rows[0]), (xo, rows[1]))):
            part = lax.dot_general(a, b, turned, preferred_element_type=f32)
            totals[k] = part if totals[k] is None else totals[k] + part
    for k in range(3):
        grad[k] += totals[k]

    @pl.when(step == steps - 1)
    def _():
        blocks = []
        for p in range(3):
            g = (2, 0, 1)[p]
            for q in range(3):
                block = None
                for v in range(1, 4):
                    u = q - 3 + 2 * v
                    if 0 <= u < 4:
                        part = grad[g, u * C : (u + 1) * C, v * C : (v + 1) * C]
                        block = part if block is None else block + part
                blocks.append(jnp.transpose(block))
        blocks += [kg2_ref[8]] + [kg2_ref[k] for k in range(8)]
        for a in range(9):
            kg_ref[a * C : (a + 1) * C] = jnp.concatenate(blocks[2 * a : 2 * a + 2], axis=1)
        if kg_ref.shape[0] > 9 * C:
            kg_ref[9 * C :] = jnp.zeros((kg_ref.shape[0] - 9 * C, L), f32)


def back_one(flags, dp, edge, n1, x, bits, st, sums, np2, kg2, count):
    rows, scan_count, lanes = x.shape
    r, tiles = (rows // 2, lanes // L // 2)
    devices = st.shape[0]
    share = 8 * -(-9 * C // (8 * devices))
    wide = (tiles + 1) * L
    return pl.pallas_call(
        functools.partial(back_one_kernel, count=count),
        grid=(scan_count // S,),
        in_specs=[
            pl.BlockSpec(memory_space=pltpu.SMEM),
            scans(r + 1, wide),
            scans(edge.shape[0], L),
            scans(r + 1, wide),
            scans(rows, lanes),
            scans(bits.shape[0], lanes),
            whole(st.shape),
            whole(sums.shape),
            whole(np2.shape),
            whole(kg2.shape),
        ],
        out_specs=[scans(r + 1, wide), whole((devices * share, L))],
        out_shape=[
            jax.ShapeDtypeStruct((r + 1, scan_count, wide), bf16),
            jax.ShapeDtypeStruct((devices * share, L), f32),
        ],
        scratch_shapes=[
            pltpu.VMEM((2, r, S, lanes), bf16),
            pltpu.VMEM((3, 4 * C, 4 * C), f32),
        ],
        compiler_params=params_of(),
        cost_estimate=cost(16),
        name="back_one",
    )(flags, dp, edge, n1, x, bits, st, sums, np2, kg2)


def input_grad_kernel(ds, bits_ref, w_ref, *rest):
    ig_ref = rest[-1]
    r, tiles = (ds.shape[0] - 1, ds.shape[2] // L - 1)
    for t in range(tiles):
        lanes = slice(t * L, (t + 2) * L)
        rows = [ds[a : a + r, :, lanes].reshape(r * S, 2 * L) for a in range(2)]
        even = jnp.dot(rows[0], w_ref[: 4 * C], preferred_element_type=f32)
        odd = jnp.dot(
            jnp.concatenate(rows, axis=1), w_ref[4 * C :], preferred_element_type=f32
        )
        for k, block in enumerate((even, odd)):
            block = block.reshape(r, S, 2 * L)
            for h in range(2):
                xl = slice((2 * t + h) * L, (2 * t + h + 1) * L)
                for i in range(r):
                    row = 2 * i + k
                    d = block[i, :, h * L : (h + 1) * L].astype(bf16)
                    ig_ref[row, :, xl] = live(bits_ref[row // BITS, :, xl], row, d)


def input_gradient(d, bits, w, part, before):
    r, scan_count, wide = d.shape
    rows, lanes = (2 * (r - 1), 2 * (wide - L))
    steps = scan_count // S // 2
    at = lambda n, m: pl.BlockSpec((n, S, m), lambda g: (0, g + part * steps, 0))
    earlier = () if before is None else (before,)
    return pl.pallas_call(
        input_grad_kernel,
        grid=(steps,),
        in_specs=[at(r, wide), at(bits.shape[0], lanes), whole(w.shape)]
        + [pl.BlockSpec(memory_space=pl.ANY)] * len(earlier),
        out_specs=at(rows, lanes),
        out_shape=jax.ShapeDtypeStruct((rows, scan_count, lanes), bf16),
        input_output_aliases={3: 0} if earlier else {},
        compiler_params=params_of(),
        cost_estimate=cost(7),
        name="input_gradient",
    )(d, bits, w, *earlier)


def adam_step(weight_now, gradient, moment_one, moment_two, step_rate, decay_rate):
    first_new = adam_beta * moment_one + (1.0 - adam_beta) * gradient
    second_new = adam_beta * moment_two + (1.0 - adam_beta) * gradient * gradient
    correction = 1.0 - adam_beta**step_count
    update = first_new / correction / (jnp.sqrt(second_new / correction) + adam_eps)
    return (weight_now - step_rate * (update + decay_rate * weight_now), first_new, second_new)


def update_kernel(
    g_ref, s1_ref, s2_ref, k_ref, km_ref, kv_ref, n_ref, nm_ref, nv_ref, gn_ref, ok_ref, okm_ref,
    okv_ref, olow_ref, on_ref, onm_ref, onv_ref,
):
    norm_rows = []
    for ref in (s1_ref, s2_ref):
        shift_sum, gain_sum = sums_of(ref)
        norm_rows += [gain_sum[:, :C], shift_sum[:, :C]]
    g_norm = jnp.concatenate(norm_rows, axis=0)
    squares = jnp.sum(jnp.sum(g_ref[: 9 * C] ** 2, axis=0, keepdims=True), axis=1, keepdims=True)
    squares = squares + jnp.sum(
        jnp.sum(g_norm * g_norm, axis=0, keepdims=True), axis=1, keepdims=True
    )
    norm = jnp.sqrt(squares)
    gn_ref[...] = norm
    factor = jnp.minimum(1.0, clip_limit / norm)
    on, onm, onv = adam_step(
        n_ref[...], g_norm * factor, nm_ref[...], nv_ref[...], norm_rate, 0.0
    )
    on_ref[...] = on
    onm_ref[...] = onm
    onv_ref[...] = onv
    for layer in range(2):
        for a in range(5):
            width = L if a < 4 else C
            at = slice(a * L, a * L + width)
            if a == 4:
                g = g_ref[4 * C : 5 * C, layer * C : (layer + 1) * C]
            else:
                first = (a + 5 * layer) * C
                g = g_ref[first : first + C, :]
            k, km, kv = adam_step(
                k_ref[layer, :, at], g * factor, km_ref[layer, :, at], kv_ref[layer, :, at],
                kernel_rate, kernel_decay,
            )
            ok_ref[layer, :, at] = k
            okm_ref[layer, :, at] = km
            okv_ref[layer, :, at] = kv
            olow_ref[layer, :, at] = k.astype(bf16)


def update(grads, sums1, sums2, kt, kmt, kvt, norm_params, norm_m, norm_v):
    flat = lambda a: a.reshape(4, C)
    big = jax.ShapeDtypeStruct(kt.shape, f32)
    small = jax.ShapeDtypeStruct((4, C), f32)
    outs = [
        jax.ShapeDtypeStruct((1, 1), f32), big, big, big,
        jax.ShapeDtypeStruct(kt.shape, bf16), small, small, small,
    ]
    args = [grads, sums1, sums2, kt, kmt, kvt, flat(norm_params), flat(norm_m), flat(norm_v)]
    return pl.pallas_call(
        update_kernel,
        grid=(1,),
        in_specs=[whole(a.shape) for a in args],
        out_specs=[whole(o.shape) for o in outs],
        out_shape=outs,
        compiler_params=params_of(),
        cost_estimate=cost(3),
        name="update",
    )(*args)


def shifted(block, axis, distance):
    devices = range(lax.axis_size(axis))
    route = [(i - distance, i) for i in devices if i - distance in devices]
    return lax.ppermute(block, axis, route)


def exchange(rows):
    return lax.all_to_all(rows, BOTH, 0, 0, tiled=True)


def per_device(
    scan_features, occupancy, kernels, kernel_m, kernel_v, norm_params, norm_m, norm_v, cotangent
):
    x = jnp.transpose(scan_features, (1, 0, 2))
    cot = jnp.transpose(cotangent, (1, 0, 2))
    occ = jnp.transpose(occupancy, (2, 0, 1))
    kt, kmt, kvt = (jnp.transpose(a, (0, 2, 1)) for a in (kernels, kernel_m, kernel_v))
    gy, gx = (lax.axis_size("gy"), lax.axis_size("gx"))
    devices = gy * gx
    y, z = (lax.axis_index("gy"), lax.axis_index("gx"))
    flags = jnp.stack([y > 0, y < gy - 1, z > 0, z < gx - 1]).astype(jnp.int32)
    rows, scan_count, lanes = x.shape
    r, tiles = (rows // 2, lanes // L // 2)
    count = float(scan_count * r * tiles)
    last = (tiles - 1) * L

    down, cot_down, corner, xcol = edges(x, occ, cot)
    xcol = shifted(xcol, "gx", 1)
    down = shifted(down, "gy", 1)
    cot_down = shifted(cot_down, "gy", -1)
    corner = lax.ppermute(
        corner, BOTH, [(i, i + gx + 1) for i in range(devices - gx) if (i + 1) % gx]
    )
    bits, w1, w2, w2b, w1b, np2 = prepare(occ, kt, norm_params)

    ends, st1, going_right, going_left, edge = first_last(x, bits, down, xcol, corner, w1)
    left_in = shifted(going_right, "gx", 1)
    right_in = shifted(going_left, "gx", -1)
    c1, st1, up, low_rows = conv_one(x, bits, down, st1, w1, devices)
    half = (r + 1) // 2

    def beyond(a, b):
        near, far = (slice(0, C), slice(C, L))
        if a >= half:
            a, b, near, far = (a - half, b - half, far, near)
        return jnp.concatenate([left_in[a:b, :, near], right_in[a:b, :, far]], axis=2)

    up = jnp.concatenate([up, edge[:3], beyond(0, 3)], axis=2)
    low_rows = jnp.concatenate([low_rows, edge[r - 2 :], beyond(r - 2, r)], axis=2)
    down_in = shifted(up, "gy", -1)
    up_in = shifted(low_rows, "gy", 1)
    st1 = exchange(st1)

    c2, n1, hid, st2 = conv_two(
        flags, c1, ends, up_in, down_in, left_in, right_in, st1, np2, w2, count
    )
    st2 = exchange(st2)
    features, d2, sums2 = output(c2, st2, np2, cot, down, cot_down, count)
    sums2 = exchange(sums2)
    going_right, going_left = rim_two(flags, d2, c2, st2, sums2, np2, count)
    left_in = shifted(going_right, "gx", 1)
    right_in = shifted(going_left, "gx", -1)
    ds, kg2 = back_two(flags, d2, c2, hid, st2, sums2, np2, count)
    d1, edge, sums1 = hidden_gradient(ds, left_in, right_in, n1, np2, w2b, devices)
    edge = shifted(edge, "gx", -1)
    sums1 = exchange(sums1)
    d1, grads = back_one(flags, d1, edge, n1, x, bits, st1, sums1, np2, kg2, count)
    share = grads.shape[0] // devices
    grads = exchange(grads)
    input_grad = input_gradient(d1, bits, w1b, 0, None)
    mine = jnp.sum(grads.reshape(devices, share, L), axis=0)
    grads = exchange(jnp.broadcast_to(mine[None], (devices, share, L)).reshape(-1, L))
    input_grad = input_gradient(d1, bits, w1b, 1, input_grad)
    norm, k, km, kv, low, n, nm, nv = update(
        grads, sums1, sums2, kt, kmt, kvt, norm_params, norm_m, norm_v
    )
    back = lambda a: jnp.transpose(a, (0, 2, 1))
    deep = lambda a: a.reshape(norm_params.shape)
    return (
        jnp.transpose(features, (1, 0, 2)),
        jnp.transpose(input_grad, (1, 0, 2)),
        norm.reshape(()),
        back(k),
        back(km),
        back(kv),
        back(low),
        deep(n),
        deep(nm),
        deep(nv),
    )


def solution(mesh):
    split = P(None, "gy", "gx")
    return jax.shard_map(
        per_device,
        mesh=mesh,
        in_specs=(split, split) + (P(),) * 6 + (split,),
        out_specs=(split, split) + (P(),) * 8,
        check_vma=False,
    )
```

```python
import functools
import math

import jax
import jax.numpy as jnp
from jax import lax
from jax.experimental import pallas as pl
from jax.experimental.pallas import tpu as pltpu
from jax.sharding import PartitionSpec as P

norm_eps = 1e-05
adam_beta = 0.5
adam_eps = 1e-08
step_count = 5
clip_limit = 1.0
kernel_rate = 0.04
norm_rate = 0.25
kernel_decay = 0.01

f32, bf16 = (jnp.float32, jnp.bfloat16)
BOTH = ("gy", "gx")
S, C, L, BITS = (16, 64, 128, 13)


def params_of(limit=20):
    return pltpu.CompilerParams(
        dimension_semantics=("arbitrary",), vmem_limit_bytes=limit << 20
    )


def cost(microseconds):
    return pl.CostEstimate(
        flops=0, bytes_accessed=int(microseconds * 3.6e6), transcendentals=0
    )


def whole(shape):
    return pl.BlockSpec(shape, lambda g: (0,) * len(shape))


def scans(rows, lanes):
    return pl.BlockSpec((rows, S, lanes), lambda g: (0, g, 0))


def resident(shape, dtype):
    return pltpu.VMEM(shape, dtype)


held = pl.BlockSpec(memory_space=pltpu.VMEM)


def hbm(array):
    return pltpu.with_memory_space_constraint(array, pltpu.HBM)


def part_of(ref, step):
    return ref.at[:, pl.ds(pl.multiple_of(step * S, S), S), :]


def low_half(rows=S):
    return lax.broadcasted_iota(jnp.int32, (rows, L), 1) < C


def swap(x):
    return pltpu.roll(x, C, 1)


def fold(x):
    x = jnp.broadcast_to(x, (8, L))
    return (x + swap(x))[:1]


def live(word, row, x):
    bit = 1 << (row % BITS)
    if x.dtype == bf16:
        return jnp.where((word & jnp.int16(bit)) != 0, x, jnp.zeros_like(x))
    return jnp.where((word.astype(jnp.int32) & bit) != 0, x, 0.0)


def pair(ref, row, t):
    return ref[row, :, t * L : (t + 1) * L]


def stats_of(st_ref, count):
    groups = 2 * st_ref.shape[0]
    means = st_ref[:, 0, :]
    mean = fold(jnp.sum(means, axis=0, keepdims=True)) / groups
    spread = st_ref[:, 1, :] + count * (means - mean) ** 2
    spread = fold(jnp.sum(spread, axis=0, keepdims=True)) / (groups * count)
    return (mean, lax.rsqrt(spread + norm_eps))


def sums_of(st_ref):
    return tuple(fold(jnp.sum(st_ref[:, k, :], axis=0, keepdims=True)) for k in range(2))


def pilot_of(block):
    flat = block.reshape(-1, L)
    return jnp.sum(flat, axis=0, keepdims=True) / flat.shape[0]


def finish_stats(step, steps, pilot, sums, count, run_ref, st_ref):
    off, squares = (jnp.sum(s, axis=0, keepdims=True) for s in sums)
    mean = pilot + off / count
    squares = squares - off * off / count

    @pl.when(step == 0)
    def _():
        run_ref[0:1] = mean
        run_ref[1:2] = squares

    @pl.when(step > 0)
    def _():
        before = step.astype(f32)
        share = 1.0 / (before + 1.0)
        delta = mean - run_ref[0:1]
        run_ref[0:1] = run_ref[0:1] + delta * share
        run_ref[1:2] = run_ref[1:2] + squares + delta * delta * (count * before * share)

    @pl.when(step == steps - 1)
    def _():
        st_ref[...] = jnp.broadcast_to(run_ref[0:2][None], st_ref.shape)


def off_sums(blocks, pilot):
    sums = [jnp.zeros((8, L), f32), jnp.zeros((8, L), f32)]
    for block in blocks:
        d = block - pilot
        sums = [sums[0] + halves(d), sums[1] + halves(d * d)]
    return sums


def added(a, b):
    return b if a is None else [x + y for x, y in zip(a, b)]


def rim_of(first, second, row, low):
    half = first.shape[0]
    if row < half:
        return jnp.where(low, first[row].astype(f32), second[row].astype(f32))
    row = row - half
    return swap(jnp.where(low, second[row].astype(f32), first[row].astype(f32)))


def halves(x):
    return x[:8] + x[8:]


def occupancy_words(occ, groups, first):
    rows = occ.shape[1]
    shape = (rows, groups * L)
    group_of = lax.broadcasted_iota(jnp.int32, shape, 1) // L + first
    inner = lax.broadcasted_iota(jnp.int32, shape, 0) - group_of * BITS
    power = jnp.where(
        (inner >= 0) & (inner < BITS), (1 << jnp.clip(inner, 0, BITS)), 0
    ).astype(bf16)
    low = occ.astype(f32).astype(bf16)
    return jnp.dot(low, power, preferred_element_type=f32).astype(jnp.int32)


def edges_kernel(
    row_ref, col_ref, occ_ref, cot_last_ref, cot_first_ref, down_ref, up_ref, corner_ref, xcol_ref
):
    cols, scan_count, rows = occ_ref.shape
    lanes = row_ref.shape[2]
    groups = -(-rows // BITS)
    low = low_half(scan_count)
    words = occupancy_words(occ_ref[...].reshape(cols * scan_count, rows), 1, groups - 1)
    words = words.reshape(cols // 2, 2, scan_count, L)
    for t in range(cols // 2):
        word = jnp.where(low, words[t, 0], words[t, 1])
        x = live(word, rows - 1, row_ref[0, :, t * L : (t + 1) * L].astype(f32)).astype(bf16)
        down_ref[:, t * L : (t + 1) * L] = x
    corner_ref[...] = x
    down_ref[:, lanes:] = cot_last_ref[0]
    up_ref[...] = cot_first_ref[...]
    words = occupancy_words(occ_ref[cols - 1], groups, 0)
    for i in range(rows // 2):
        even, odd = (
            live(
                words[:, row // BITS * L : (row // BITS + 1) * L], row, col_ref[row].astype(f32)
            )
            for row in (2 * i, 2 * i + 1)
        )
        xcol_ref[i] = jnp.where(low, swap(even), odd).astype(bf16)


def edges(x, occ, cot):
    rows, scan_count, lanes = x.shape
    r, wide = (rows // 2, lanes // 2)
    outs = [
        jax.ShapeDtypeStruct((scan_count, lanes + wide), bf16),
        jax.ShapeDtypeStruct((2, scan_count, wide), bf16),
        jax.ShapeDtypeStruct((scan_count, L), bf16),
        jax.ShapeDtypeStruct((r, scan_count, L), bf16),
    ]
    return pl.pallas_call(
        edges_kernel,
        grid=(1,),
        in_specs=[
            pl.BlockSpec((1, scan_count, lanes), lambda g: (rows - 1, 0, 0)),
            pl.BlockSpec((rows, scan_count, L), lambda g: (0, 0, lanes // L - 1)),
            whole(occ.shape),
            pl.BlockSpec((1, scan_count, wide), lambda g: (r - 1, 0, 0)),
            pl.BlockSpec((2, scan_count, wide), lambda g: (0, 0, 0)),
        ],
        out_specs=[whole(o.shape) for o in outs],
        out_shape=outs,
        compiler_params=params_of(),
        cost_estimate=cost(3),
        name="edges",
    )(hbm(x), hbm(x), hbm(occ), hbm(cot), hbm(cot))


def prep_kernel(occ_ref, kt_ref, np_ref, bits_ref, w1_ref, w2_ref, w2b_ref, w1b_ref, np2_ref):
    cols, scan_count, rows = occ_ref.shape
    groups = bits_ref.shape[0]
    words = occupancy_words(occ_ref[...].reshape(cols * scan_count, rows), groups, 0)
    words = words.reshape(cols // 2, 2, scan_count, groups * L)
    low = low_half(scan_count)
    for g in range(groups):
        for t in range(cols // 2):
            lanes = slice(g * L, (g + 1) * L)
            word = jnp.where(low, words[t, 0, :, lanes], words[t, 1, :, lanes])
            bits_ref[g, :, t * L : (t + 1) * L] = word.astype(jnp.int16)
    back = [[kt_ref[l, :, k * C : (k + 1) * C] for k in range(9)] for l in range(2)]
    fore = [[jnp.transpose(b) for b in layer] for layer in back]
    none = jnp.zeros((C, C), f32)

    def put(ref, rows_of, cols_of, pick):
        for a in range(rows_of):
            blocks = [pick(a, b) for b in range(cols_of)]
            for k in range(0, cols_of, 2):
                two = jnp.concatenate(blocks[k : k + 2], axis=1).astype(bf16)
                ref[a * C : (a + 1) * C, k * C : (k + 2) * C] = two

    def tap(table, p, q):
        return table[3 * p + q] if 0 <= p < 3 and 0 <= q < 3 else none

    put(w1_ref, 30, 4, lambda a, b: tap(fore[0], a // 6 - 2 * (b // 2), a % 6 - 2 * (b % 2) - 1))
    put(w2_ref, 16, 4, lambda a, b: tap(fore[1], a // 4 - b // 2, a % 4 - b % 2))
    put(w2b_ref, 16, 4, lambda a, b: tap(back[1], b // 2 + 2 - a // 4, b % 2 + 2 - a % 4))
    put(w1b_ref, 12, 4, lambda a, b: tap(back[0], (1, 2, 0)[a // 4], b + 3 - 2 * (a % 4)))
    np2_ref[...] = jnp.concatenate([np_ref[...], np_ref[...]], axis=1)


def prepare(occ, kt, norm_params):
    cols, scan_count, rows = occ.shape
    full = lambda *shape: jax.ShapeDtypeStruct(shape, bf16)
    outs = [
        jax.ShapeDtypeStruct((-(-rows // BITS), scan_count, cols * C), jnp.int16),
        full(30 * C, 4 * C),
        full(16 * C, 4 * C),
        full(16 * C, 4 * C),
        full(12 * C, 4 * C),
        jax.ShapeDtypeStruct((4, L), f32),
    ]
    return pl.pallas_call(
        prep_kernel,
        grid=(1,),
        in_specs=[whole(occ.shape), whole(kt.shape), whole((4, C))],
        out_specs=[whole(o.shape) for o in outs],
        out_shape=outs,
        compiler_params=params_of(),
        cost_estimate=cost(4),
        name="prepare",
    )(hbm(occ), kt, norm_params.reshape(4, C))


def mask_tile(x_ref, bits_ref, t, xs, into):
    rows = x_ref.shape[0]
    for g in range(bits_ref.shape[0]):
        word = bits_ref[g, :, t * L : (t + 1) * L]
        for row in range(g * BITS, min(rows, (g + 1) * BITS)):
            x = live(word, row, pair(x_ref, row, t))
            xs[(row + 1) // 4, (row + 1) % 4, :, into * L : (into + 1) * L] = x


def clear_rows(rows, pairs, xs):
    for k in range(rows + 1, 4 * pairs + 1):
        xs[k // 4, k % 4] = jnp.zeros_like(xs[0, 0])


def conv_rows(xs, lanes, w, r):
    pairs = (r + 1) // 2
    pieces = [xs[0:pairs, q, :, lanes] for q in range(4)] + [xs[1 : pairs + 1, 0, :, lanes]]
    lhs = jnp.concatenate([p.reshape(pairs * S, p.shape[2]) for p in pieces], axis=1)
    acc = jnp.dot(lhs, w, preferred_element_type=f32).reshape(pairs, S, 2 * L)
    return [acc[i // 2, :, (i % 2) * L : (i % 2 + 1) * L] for i in range(r)]


def conv_one_kernel(
    x_ref, bits_ref, xrow_ref, xcol_ref, corner_ref, w_ref, c_ref, st_ref, up_ref, down_ref,
    edge_ref, xs, run,
):
    step, steps = (pl.program_id(0), pl.num_programs(0))
    c_ref = part_of(c_ref, step)
    rows, tiles = (x_ref.shape[0], x_ref.shape[2] // L)
    r, t_out = (rows // 2, tiles // 2 + 1)
    low = low_half()

    @pl.when(step == 0)
    def _():
        clear_rows(rows, (r + 1) // 2, xs)

    xs[0, 0, :, L:] = xrow_ref[:, : tiles * L]
    xs[0, 0, :, :L] = corner_ref[...]
    for i in range(r):
        k = 2 * i + 2
        xs[k // 4, k % 4, :, :L] = xcol_ref[i]
        k = 2 * i + 1
        xs[k // 4, k % 4, :, :L] = swap(xcol_ref[i].astype(f32)).astype(bf16)
    wide = 3 * L
    some = lambda a: jnp.concatenate(
        [w_ref[q * wide + a * L : q * wide + (a + 2) * L] for q in range(5)], axis=0
    )
    sums, pilot, first = (None, None, None)
    filled = 0
    for t in range(t_out):
        while filled < min(tiles, 2 * t + 1):
            mask_tile(x_ref, bits_ref, filled, xs, filled + 1)
            filled += 1
        if t == 0:
            blocks = conv_rows(xs, slice(0, 2 * L), some(1), r)
            first = blocks
        elif t == t_out - 1:
            blocks = conv_rows(xs, slice((tiles - 1) * L, (tiles + 1) * L), some(0), r)
        else:
            blocks = conv_rows(xs, slice((2 * t - 1) * L, (2 * t + 2) * L), w_ref[...], r)
        for i, block in enumerate(blocks):
            c_ref[i, :, t * L : (t + 1) * L] = block
        if t == 1:
            pilot = pilot_of(jnp.concatenate(blocks[: r // 2], axis=0))
        if t == t_out - 1:
            blocks = [jnp.where(low, b, pair(c_ref, i, 0)) for i, b in enumerate(blocks)]
            for i in range(r):
                edge_ref[i] = blocks[i].astype(bf16)
        if t > 0:
            sums = added(sums, off_sums(blocks, pilot))
    finish_stats(step, steps, pilot, sums, float(r * (t_out - 1) * S), run, st_ref)
    up_ref[...] = c_ref[0:3].astype(bf16)
    down_ref[...] = c_ref[r - 2 : r].astype(bf16)


def conv_one(x, bits, down, xcol, corner, w, devices):
    rows, scan_count, lanes = x.shape
    r, wide = (rows // 2, lanes // 2 + L)
    shape = lambda dtype, *s: jax.ShapeDtypeStruct(s, dtype)
    return pl.pallas_call(
        conv_one_kernel,
        grid=(scan_count // S,),
        in_specs=[
            scans(rows, lanes),
            scans(bits.shape[0], lanes),
            pl.BlockSpec((S, down.shape[1]), lambda g: (g, 0)),
            scans(r, L),
            pl.BlockSpec((S, L), lambda g: (g, 0)),
            whole(w.shape),
        ],
        out_specs=[held, whole((devices, 2, L)), scans(3, wide), scans(2, wide), scans(r, L)],
        out_shape=[
            resident((r, scan_count, wide), f32),
            shape(f32, devices, 2, L),
            shape(bf16, 3, scan_count, wide),
            shape(bf16, 2, scan_count, wide),
            shape(bf16, r, scan_count, L),
        ],
        scratch_shapes=[
            pltpu.VMEM(((r + 1) // 2 + 1, 4, S, lanes + L), bf16),
            pltpu.VMEM((8, L), f32),
        ],
        compiler_params=params_of(),
        cost_estimate=cost(13),
        name="conv_one",
    )(hbm(x), bits, down, xcol, corner, w)


def pack_kernel(up_ref, edge_ref, down_ref, er_ref, el_ref):
    r, half = (edge_ref.shape[0], er_ref.shape[0])
    last = up_ref.shape[2] // L - 1
    low = low_half()

    def both(row):
        if 2 <= row < r + 2:
            return edge_ref[row - 2].astype(f32)
        src, k = (up_ref, row) if row < 2 else (down_ref, row - r - 2)
        return jnp.where(low, pair(src, k, last).astype(f32), pair(src, k, 0).astype(f32))

    for k in range(half):
        near, far = (both(k), swap(both(k + half)))
        er_ref[k] = jnp.where(low, near, far).astype(bf16)
        el_ref[k] = jnp.where(low, far, near).astype(bf16)


def pack_edges(up, edge, down):
    r, scan_count, _lanes = edge.shape
    wide = up.shape[2]
    return pl.pallas_call(
        pack_kernel,
        grid=(scan_count // S,),
        in_specs=[scans(2, wide), scans(r, L), scans(3, wide)],
        out_specs=[scans((r + 5) // 2, L)] * 2,
        out_shape=[jax.ShapeDtypeStruct(((r + 5) // 2, scan_count, L), bf16)] * 2,
        compiler_params=params_of(),
        cost_estimate=cost(2),
        name="pack_edges",
    )(up, edge, down)


def conv_two_kernel(
    flags, c_ref, up_ref, down_ref, left_ref, right_ref, st_ref, np_ref, w_ref, c2_ref, n1_ref,
    hid_ref, st2_ref, hs, rim, run, *, count,
):
    step, steps = (pl.program_id(0), pl.num_programs(0))
    c_ref, c2_ref, n1_ref = (part_of(a, step) for a in (c_ref, c2_ref, n1_ref))
    r, tiles = (c_ref.shape[0], c_ref.shape[2] // L)
    t_out = tiles - 1
    mean, inv = stats_of(st_ref, count)
    offset = -mean * inv
    scale = 0.5 * np_ref[0:1] * inv
    shift = 0.5 * (np_ref[0:1] * offset + np_ref[1:2])
    f_up, f_down, f_left, f_right = (flags[k].astype(f32) for k in range(4))
    low = low_half()
    left = jnp.where(low, f_left, 1.0)
    right = jnp.where(low, 1.0, f_right)
    for row in range(r + 5):
        rim[row] = rim_of(left_ref, right_ref, row, low)

    def act(row, t):
        if row < 2:
            c, flag = (pair(up_ref, row, t), f_up)
        elif row < r + 2:
            c, flag = (pair(c_ref, row - 2, t), None)
        else:
            c, flag = (pair(down_ref, row - r - 2, t), f_down)
        c = c.astype(f32)
        if t == 0:
            c = jnp.where(low, rim[row], c)
        if t == tiles - 1:
            c = jnp.where(low, c, rim[row])
        h = c * scale + shift
        out = h + h * jnp.tanh(h)
        if t == 0:
            out = out * left
        if t == tiles - 1:
            out = out * right
        if flag is not None:
            out = out * flag
        out = out.astype(bf16)
        hs[row // 2, row % 2, :, t * L : (t + 1) * L] = out
        if 1 <= row < r + 3:
            hid_ref[row - 1, :, t * L : (t + 1) * L] = out
        if 2 <= row < r + 3:
            n1_ref[row - 2, :, t * L : (t + 1) * L] = (c * inv + offset).astype(bf16)

    pairs = (r + 3) // 2
    sums, pilot = (None, None)
    for t in range(tiles):
        for row in range(r + 5):
            act(row, t)
        k = t - 1
        if k < 0:
            continue
        lanes = slice(k * L, (k + 2) * L)
        pieces = [hs[a : a + pairs, b, :, lanes] for a in range(2) for b in range(2)]
        lhs = jnp.concatenate([p.reshape(pairs * S, 2 * L) for p in pieces], axis=1)
        acc = jnp.dot(lhs, w_ref[...], preferred_element_type=f32).reshape(pairs, S, 2 * L)
        if pilot is None:
            pilot = pilot_of(acc[1 : r // 2, :, :L])
        blocks = []
        for row in range(r + 3):
            block = acc[row // 2, :, (row % 2) * L : (row % 2 + 1) * L]
            c2_ref[row, :, k * L : (k + 1) * L] = block
            if 0 < row <= r:
                blocks.append(block)
        sums = added(sums, off_sums(blocks, pilot))
    finish_stats(step, steps, pilot, sums, float(r * t_out * S), run, st2_ref)


def conv_two(flags, c1, up, down, left, right, st, np2, w, count):
    r, scan_count, wide = c1.shape
    lanes = wide - L
    devices = st.shape[0]
    return pl.pallas_call(
        functools.partial(conv_two_kernel, count=count),
        grid=(scan_count // S,),
        in_specs=[
            pl.BlockSpec(memory_space=pltpu.SMEM),
            held,
            scans(2, wide),
            scans(3, wide),
            scans(left.shape[0], L),
            scans(right.shape[0], L),
            whole(st.shape),
            whole(np2.shape),
            whole(w.shape),
        ],
        out_specs=[held, held, scans(r + 2, wide), whole((devices, 2, L))],
        out_shape=[
            resident((r + 3, scan_count, lanes), f32),
            resident((r + 1, scan_count, wide), bf16),
            pltpu.HBM((r + 2, scan_count, wide), bf16),
            jax.ShapeDtypeStruct((devices, 2, L), f32),
        ],
        scratch_shapes=[
            pltpu.VMEM(((r + 5) // 2, 2, S, wide), bf16),
            pltpu.VMEM((r + 5, S, L), f32),
            pltpu.VMEM((8, L), f32),
        ],
        compiler_params=params_of(),
        cost_estimate=cost(14),
        name="conv_two",
    )(flags, c1, up, down, left, right, st, np2, w)


def output_kernel(
    c2_ref, st_ref, np_ref, cot_ref, up_ref, down_ref, feat_ref, d_ref, sum_ref, run, *, count,
):
    step, steps = (pl.program_id(0), pl.num_programs(0))
    c2_ref, d_ref = (part_of(a, step) for a in (c2_ref, d_ref))
    r, tiles = (cot_ref.shape[0], cot_ref.shape[2] // L)
    mean, inv = stats_of(st_ref, count)
    offset = -mean * inv
    scale = 0.5 * np_ref[2:3] * inv
    shift = 0.5 * (np_ref[2:3] * offset + np_ref[3:4])
    above = 2 * tiles

    def slope(c, cot):
        h = c * scale + shift
        t = jnp.tanh(h)
        plus = 1.0 + t
        return (h * plus, (0.5 * cot.astype(f32)) * (plus * (1.0 + h * (1.0 - t))))

    def own(i, sums):
        for t in range(tiles):
            c = pair(c2_ref, i + 1, t)
            f, d = slope(c, pair(cot_ref, i, t))
            feat_ref[i, :, t * L : (t + 1) * L] = f.astype(bf16)
            d_ref[i + 1, :, t * L : (t + 1) * L] = d
            sums = (sums[0] + halves(d), sums[1] + halves(d * (c * inv + offset)))
        return sums

    zero = jnp.zeros((8, L), f32)
    sums = lax.fori_loop(0, r, own, (zero, zero))
    for t in range(tiles):
        lanes = slice(t * L, (t + 1) * L)
        cot = up_ref[:, (above + t) * L : (above + t + 1) * L]
        d_ref[0, :, lanes] = slope(pair(c2_ref, 0, t), cot)[1]
        for k in range(2):
            row = r + 1 + k
            d_ref[row, :, lanes] = slope(pair(c2_ref, row, t), pair(down_ref, k, t))[1]
    add_sums(step, steps, sums, run, sum_ref)


def add_sums(step, steps, sums, run, sum_ref):
    rows = jnp.concatenate([jnp.sum(s, axis=0, keepdims=True) for s in sums], axis=0)

    @pl.when(step == 0)
    def _():
        run[0:2] = rows

    @pl.when(step > 0)
    def _():
        run[0:2] = run[0:2] + rows

    @pl.when(step == steps - 1)
    def _():
        sum_ref[...] = jnp.broadcast_to(run[0:2][None], sum_ref.shape)


def output(c2, st, np2, cot, up, down, count):
    r, scan_count, lanes = cot.shape
    devices = st.shape[0]
    return pl.pallas_call(
        functools.partial(output_kernel, count=count),
        grid=(scan_count // S,),
        in_specs=[
            held,
            whole(st.shape),
            whole(np2.shape),
            scans(r, lanes),
            pl.BlockSpec((S, up.shape[1]), lambda g: (g, 0)),
            scans(2, lanes),
        ],
        out_specs=[scans(r, lanes), held, whole((devices, 2, L))],
        out_shape=[
            jax.ShapeDtypeStruct((r, scan_count, lanes), bf16),
            resident((r + 3, scan_count, lanes), f32),
            jax.ShapeDtypeStruct((devices, 2, L), f32),
        ],
        scratch_shapes=[pltpu.VMEM((8, L), f32)],
        compiler_params=params_of(),
        cost_estimate=cost(12),
        name="output",
    )(c2, st, np2, hbm(cot), up, down)


def norm_back_two(flags, st_ref, sum_ref, np_ref, count, rows):
    cells = 2.0 * count * st_ref.shape[0]
    mean, inv = stats_of(st_ref, count)
    shift_sum, gain_sum = sums_of(sum_ref)
    gain = np_ref[2:3] * inv
    c_n = -gain * inv * gain_sum / cells
    c_0 = -gain * shift_sum / cells - c_n * mean
    f_up, f_down = (flags[k].astype(f32) for k in range(2))

    def back(row, d, c):
        d = d * gain + (c * c_n + c_0)
        if isinstance(row, int):
            if row == 0:
                d = d * f_up
            if row > rows:
                d = d * f_down
        return d

    return back


def rim_two_kernel(
    flags, d_ref, c_ref, st_ref, sum_ref, np_ref, er_ref, el_ref, *, count
):
    d_ref, c_ref = (part_of(a, pl.program_id(0)) for a in (d_ref, c_ref))
    rows, last = (d_ref.shape[0], d_ref.shape[2] // L - 1)
    back = norm_back_two(flags, st_ref, sum_ref, np_ref, count, rows - 3)
    low = low_half()
    half = rows // 2
    column = lambda row, t: back(row, pair(d_ref, row, t), pair(c_ref, row, t))
    both = lambda row: jnp.where(low, column(row, 0), column(row, last))
    for k in range(half):
        near, far = (both(k), swap(both(k + half)))
        el_ref[k] = jnp.where(low, near, far).astype(bf16)
        er_ref[k] = jnp.where(low, far, near).astype(bf16)


def rim_two(flags, d, c2, st, sums, np2, count):
    rows, scan_count, lanes = d.shape
    return pl.pallas_call(
        functools.partial(rim_two_kernel, count=count),
        grid=(scan_count // S,),
        in_specs=[
            pl.BlockSpec(memory_space=pltpu.SMEM), held, held, whole(st.shape),
            whole(sums.shape), whole(np2.shape),
        ],
        out_specs=[scans(rows // 2, L)] * 2,
        out_shape=[jax.ShapeDtypeStruct((rows // 2, scan_count, L), bf16)] * 2,
        compiler_params=params_of(),
        cost_estimate=cost(3),
        name="rim_two",
    )(flags, d, c2, st, sums, np2)


def back_two_kernel(
    flags, d_ref, c2_ref, hid_ref, st_ref, sum_ref, np_ref, ds_ref, kg_ref, grad, *, count
):
    step, steps = (pl.program_id(0), pl.num_programs(0))
    d_ref, c2_ref, ds_ref = (part_of(a, step) for a in (d_ref, c2_ref, ds_ref))
    r, tiles = (c2_ref.shape[0] - 3, c2_ref.shape[2] // L)
    back = norm_back_two(flags, st_ref, sum_ref, np_ref, count, r)

    @pl.when(step == 0)
    def _():
        grad[...] = jnp.zeros_like(grad)

    total = None
    for t in range(tiles):
        for row in range(r + 3):
            d = back(row, pair(d_ref, row, t), pair(c2_ref, row, t))
            ds_ref[row, :, t * L : (t + 1) * L] = d.astype(bf16)
        lanes = slice(t * L, (t + 2) * L)
        rhs = jnp.concatenate(
            [hid_ref[p : p + r, :, lanes].reshape(r * S, 2 * L) for p in range(3)], axis=1
        )
        lhs = ds_ref[1 : r + 1, :, t * L : (t + 1) * L].reshape(r * S, L)
        part = lax.dot_general(lhs, rhs, (((0,), (0,)), ((), ())), preferred_element_type=f32)
        total = part if total is None else total + part
    grad[...] += total

    @pl.when(step == steps - 1)
    def _():
        for p in range(3):
            for q in range(3):
                block = None
                for w in range(2):
                    at = 4 * p * C + (w + q) * C
                    part = grad[w * C : (w + 1) * C, at : at + C]
                    block = part if block is None else block + part
                kg_ref[3 * p + q] = block


def back_two(flags, d, c2, hid, st, sums, np2, count):
    r, scan_count, wide = hid.shape
    r, lanes = (r - 2, wide - L)
    return pl.pallas_call(
        functools.partial(back_two_kernel, count=count),
        grid=(scan_count // S,),
        in_specs=[
            pl.BlockSpec(memory_space=pltpu.SMEM),
            held,
            held,
            scans(r + 2, wide),
            whole(st.shape),
            whole(sums.shape),
            whole(np2.shape),
        ],
        out_specs=[held, whole((9, C, C))],
        out_shape=[
            resident((r + 3, scan_count, lanes), bf16),
            jax.ShapeDtypeStruct((9, C, C), f32),
        ],
        scratch_shapes=[pltpu.VMEM((L, 12 * C), f32)],
        compiler_params=params_of(),
        cost_estimate=cost(12),
        name="back_two",
    )(flags, d, c2, hbm(hid), st, sums, np2)


def hidden_kernel(
    ds_ref, left_ref, right_ref, n1_ref, np_ref, w_ref, dp_ref, edge_ref, sum1_ref, rim, run
):
    step, steps = (pl.program_id(0), pl.num_programs(0))
    ds_ref, n1_ref, dp_ref = (part_of(a, step) for a in (ds_ref, n1_ref, dp_ref))
    r, tiles = (n1_ref.shape[0] - 1, n1_ref.shape[2] // L)
    pairs = (r + 1) // 2
    low = low_half()
    for row in range(r + 3):
        rim[row] = rim_of(right_ref, left_ref, row, low).astype(bf16)
    sums = None
    for t in range(tiles):
        parts = []
        for k in (t - 1, t):
            part = ds_ref[:, :, k * L : (k + 1) * L] if 0 <= k < tiles - 1 else rim[...]
            parts.append(part.reshape(pairs + 1, 2, S, L))
        pieces = [p[a : a + pairs, b] for a in range(2) for b in range(2) for p in parts]
        lhs = jnp.concatenate([p.reshape(pairs * S, L) for p in pieces], axis=1)
        acc = jnp.dot(lhs, w_ref[...], preferred_element_type=f32).reshape(pairs, S, 2 * L)
        part = [jnp.zeros((8, L), f32), jnp.zeros((8, L), f32)]
        for i in range(r + 1):
            n = pair(n1_ref, i, t).astype(f32)
            h = 0.5 * (n * np_ref[0:1] + np_ref[1:2])
            tan = jnp.tanh(h)
            d = acc[i // 2, :, (i % 2) * L : (i % 2 + 1) * L]
            d = (0.5 * d) * ((1.0 + tan) * (1.0 + h * (1.0 - tan)))
            dp_ref[i, :, t * L : (t + 1) * L] = d
            if i < r:
                if t == 0:
                    d = jnp.where(low, 0.0, d)
                if t == tiles - 1:
                    d = jnp.where(low, d, 0.0)
                part = [part[0] + halves(d), part[1] + halves(d * n)]
        sums = added(sums, part)
    add_sums(step, steps, sums, run, sum1_ref)
    for i in range(pairs):
        both = jnp.where(low, swap(pair(dp_ref, pairs + i, 0)), pair(dp_ref, i, 0))
        edge_ref[i] = both.astype(bf16)


def hidden_gradient(ds, left, right, n1, np2, w, devices):
    r, scan_count, wide = n1.shape
    r, lanes = (r - 1, wide - L)
    half = left.shape[0]
    return pl.pallas_call(
        hidden_kernel,
        grid=(scan_count // S,),
        in_specs=[
            held,
            scans(half, L),
            scans(half, L),
            held,
            whole(np2.shape),
            whole(w.shape),
        ],
        out_specs=[
            held,
            scans((r + 1) // 2, L),
            whole((devices, 2, L)),
        ],
        out_shape=[
            resident((r + 1, scan_count, wide), f32),
            jax.ShapeDtypeStruct(((r + 1) // 2, scan_count, L), bf16),
            jax.ShapeDtypeStruct((devices, 2, L), f32),
        ],
        scratch_shapes=[pltpu.VMEM((r + 3, S, L), bf16), pltpu.VMEM((8, L), f32)],
        compiler_params=params_of(),
        cost_estimate=cost(12),
        name="hidden_gradient",
    )(ds, left, right, n1, np2, w)


def back_one_kernel(
    flags, dp_ref, edge_ref, n1_ref, x_ref, bits_ref, st_ref, sum_ref, np_ref, kg2_ref, ds, kg_ref,
    xm, grad, *, count,
):
    step, steps = (pl.program_id(0), pl.num_programs(0))
    dp_ref, n1_ref = (part_of(a, step) for a in (dp_ref, n1_ref))
    r, tiles = (n1_ref.shape[0] - 1, n1_ref.shape[2] // L - 1)
    cells = 2.0 * count * st_ref.shape[0]
    _mean, inv = stats_of(st_ref, count)
    shift_sum, gain_sum = sums_of(sum_ref)
    gain = np_ref[0:1] * inv
    c_n = -gain * gain_sum / cells
    c_0 = -gain * shift_sum / cells
    f_down, f_right = (flags[1].astype(f32), flags[3].astype(f32))
    packed = edge_ref.shape[0]
    low = low_half()
    right = jnp.where(low, 1.0, f_right)

    @pl.when(step == 0)
    def _():
        grad[...] = jnp.zeros_like(grad)

    def line(i, t):
        d = pair(dp_ref, i, t)
        if t == tiles:
            beyond = edge_ref[i % packed].astype(f32)
            d = jnp.where(low, d, swap(beyond) if i >= packed else beyond)
        d = d * gain + (pair(n1_ref, i, t).astype(f32) * c_n + c_0)
        if t == tiles:
            d = d * right
        if i == r:
            d = d * f_down
        ds[i, :, t * L : (t + 1) * L] = d.astype(bf16)

    turned = (((0,), (0,)), ((), ()))
    totals = [None, None, None]
    done = 0
    for t in range(tiles):
        while done < t + 2:
            for i in range(r + 1):
                line(i, done)
            done += 1
        for k in (2 * t, 2 * t + 1):
            for g in range(bits_ref.shape[0]):
                word = bits_ref[g, :, k * L : (k + 1) * L]
                for row in range(g * BITS, min(2 * r, (g + 1) * BITS)):
                    x = live(word, row, pair(x_ref, row, k))
                    xm[row % 2, row // 2, :, k * L : (k + 1) * L] = x
        lanes = slice(t * L, (t + 2) * L)
        xl = slice(2 * t * L, 2 * (t + 1) * L)
        rows = [ds[a : a + r, :, lanes].reshape(r * S, 2 * L) for a in range(2)]
        xe, xo = (xm[a, :, :, xl].reshape(r * S, 2 * L) for a in range(2))
        for k, (a, b) in enumerate(((xe, rows[0]), (xo, rows[0]), (xo, rows[1]))):
            part = lax.dot_general(a, b, turned, preferred_element_type=f32)
            totals[k] = part if totals[k] is None else totals[k] + part
    for k in range(3):
        grad[k] += totals[k]

    @pl.when(step == steps - 1)
    def _():
        blocks = []
        for p in range(3):
            g = (2, 0, 1)[p]
            for q in range(3):
                block = None
                for v in range(1, 4):
                    u = q - 3 + 2 * v
                    if 0 <= u < 4:
                        part = grad[g, u * C : (u + 1) * C, v * C : (v + 1) * C]
                        block = part if block is None else block + part
                blocks.append(jnp.transpose(block))
        blocks += [kg2_ref[8]] + [kg2_ref[k] for k in range(8)]
        for a in range(9):
            kg_ref[a * C : (a + 1) * C] = jnp.concatenate(blocks[2 * a : 2 * a + 2], axis=1)
        if kg_ref.shape[0] > 9 * C:
            kg_ref[9 * C :] = jnp.zeros((kg_ref.shape[0] - 9 * C, L), f32)


def back_one(flags, dp, edge, n1, x, bits, st, sums, np2, kg2, count):
    rows, scan_count, lanes = x.shape
    r, tiles = (rows // 2, lanes // L // 2)
    devices = st.shape[0]
    share = 8 * -(-9 * C // (8 * devices))
    wide = (tiles + 1) * L
    return pl.pallas_call(
        functools.partial(back_one_kernel, count=count),
        grid=(scan_count // S,),
        in_specs=[
            pl.BlockSpec(memory_space=pltpu.SMEM),
            held,
            scans(edge.shape[0], L),
            held,
            scans(rows, lanes),
            scans(bits.shape[0], lanes),
            whole(st.shape),
            whole(sums.shape),
            whole(np2.shape),
            whole(kg2.shape),
        ],
        out_specs=[scans(r + 1, wide), whole((devices * share, L))],
        out_shape=[
            pltpu.HBM((r + 1, scan_count, wide), bf16),
            jax.ShapeDtypeStruct((devices * share, L), f32),
        ],
        scratch_shapes=[
            pltpu.VMEM((2, r, S, lanes), bf16),
            pltpu.VMEM((3, 4 * C, 4 * C), f32),
        ],
        compiler_params=params_of(),
        cost_estimate=cost(16),
        name="back_one",
    )(flags, dp, edge, n1, hbm(x), bits, st, sums, np2, kg2)


def input_grad_kernel(ds, bits_ref, w_ref, *rest):
    ig_ref = rest[-1]
    r, tiles = (ds.shape[0] - 1, ds.shape[2] // L - 1)
    for t in range(tiles):
        lanes = slice(t * L, (t + 2) * L)
        rows = [ds[a : a + r, :, lanes].reshape(r * S, 2 * L) for a in range(2)]
        even = jnp.dot(rows[0], w_ref[: 4 * C], preferred_element_type=f32)
        odd = jnp.dot(
            jnp.concatenate(rows, axis=1), w_ref[4 * C :], preferred_element_type=f32
        )
        for k, block in enumerate((even, odd)):
            block = block.reshape(r, S, 2 * L)
            for h in range(2):
                xl = slice((2 * t + h) * L, (2 * t + h + 1) * L)
                for i in range(r):
                    row = 2 * i + k
                    d = block[i, :, h * L : (h + 1) * L].astype(bf16)
                    ig_ref[row, :, xl] = live(bits_ref[row // BITS, :, xl], row, d)


def input_gradient(d, bits, w, part, before):
    r, scan_count, wide = d.shape
    rows, lanes = (2 * (r - 1), 2 * (wide - L))
    steps = scan_count // S // 2
    at = lambda n, m: pl.BlockSpec((n, S, m), lambda g: (0, g + part * steps, 0))
    earlier = () if before is None else (before,)
    return pl.pallas_call(
        input_grad_kernel,
        grid=(steps,),
        in_specs=[at(r, wide), at(bits.shape[0], lanes), whole(w.shape)]
        + [pl.BlockSpec(memory_space=pl.ANY)] * len(earlier),
        out_specs=at(rows, lanes),
        out_shape=jax.ShapeDtypeStruct((rows, scan_count, lanes), bf16),
        input_output_aliases={3: 0} if earlier else {},
        compiler_params=params_of(),
        cost_estimate=cost(7),
        name="input_gradient",
    )(hbm(d), hbm(bits), w, *earlier)


def share_kernel(g_ref, out_ref):
    devices, share, _lanes = g_ref.shape
    total = g_ref[0]
    for k in range(1, devices):
        total = total + g_ref[k]
    for k in range(devices):
        out_ref[k] = total


def sum_share(grads, share):
    shape = (grads.shape[0] // share, share, L)
    return pl.pallas_call(
        share_kernel,
        in_specs=[held],
        out_specs=held,
        out_shape=jax.ShapeDtypeStruct(shape, f32),
        compiler_params=pltpu.CompilerParams(vmem_limit_bytes=8 << 20),
        cost_estimate=cost(1),
        name="sum_share",
    )(grads.reshape(shape)).reshape(grads.shape)


def adam_step(weight_now, gradient, moment_one, moment_two, step_rate, decay_rate):
    first_new = adam_beta * moment_one + (1.0 - adam_beta) * gradient
    second_new = adam_beta * moment_two + (1.0 - adam_beta) * gradient * gradient
    correction = 1.0 - adam_beta**step_count
    update = first_new / correction / (jnp.sqrt(second_new / correction) + adam_eps)
    return (weight_now - step_rate * (update + decay_rate * weight_now), first_new, second_new)


def update_kernel(
    g_ref, s1_ref, s2_ref, k_ref, km_ref, kv_ref, n_ref, nm_ref, nv_ref, gn_ref, ok_ref, okm_ref,
    okv_ref, olow_ref, on_ref, onm_ref, onv_ref,
):
    norm_rows = []
    for ref in (s1_ref, s2_ref):
        shift_sum, gain_sum = sums_of(ref)
        norm_rows += [gain_sum[:, :C], shift_sum[:, :C]]
    g_norm = jnp.concatenate(norm_rows, axis=0)
    squares = jnp.sum(jnp.sum(g_ref[: 9 * C] ** 2, axis=0, keepdims=True), axis=1, keepdims=True)
    squares = squares + jnp.sum(
        jnp.sum(g_norm * g_norm, axis=0, keepdims=True), axis=1, keepdims=True
    )
    norm = jnp.sqrt(squares)
    gn_ref[...] = norm
    factor = jnp.minimum(1.0, clip_limit / norm)
    on, onm, onv = adam_step(
        n_ref[...], g_norm * factor, nm_ref[...], nv_ref[...], norm_rate, 0.0
    )
    on_ref[...] = on
    onm_ref[...] = onm
    onv_ref[...] = onv
    for layer in range(2):
        for a in range(5):
            width = L if a < 4 else C
            at = slice(a * L, a * L + width)
            if a == 4:
                g = g_ref[4 * C : 5 * C, layer * C : (layer + 1) * C]
            else:
                first = (a + 5 * layer) * C
                g = g_ref[first : first + C, :]
            k, km, kv = adam_step(
                k_ref[layer, :, at], g * factor, km_ref[layer, :, at], kv_ref[layer, :, at],
                kernel_rate, kernel_decay,
            )
            ok_ref[layer, :, at] = k
            okm_ref[layer, :, at] = km
            okv_ref[layer, :, at] = kv
            olow_ref[layer, :, at] = k.astype(bf16)


def update(grads, sums1, sums2, kt, kmt, kvt, norm_params, norm_m, norm_v):
    flat = lambda a: a.reshape(4, C)
    big = jax.ShapeDtypeStruct(kt.shape, f32)
    small = jax.ShapeDtypeStruct((4, C), f32)
    outs = [
        jax.ShapeDtypeStruct((1, 1), f32), big, big, big,
        jax.ShapeDtypeStruct(kt.shape, bf16), small, small, small,
    ]
    args = [grads, sums1, sums2, kt, kmt, kvt, flat(norm_params), flat(norm_m), flat(norm_v)]
    return pl.pallas_call(
        update_kernel,
        grid=(1,),
        in_specs=[whole(a.shape) for a in args],
        out_specs=[whole(o.shape) for o in outs],
        out_shape=outs,
        compiler_params=params_of(),
        cost_estimate=cost(3),
        name="update",
    )(*args)


def shifted(block, axis, distance):
    devices = range(lax.axis_size(axis))
    route = [(i - distance, i) for i in devices if i - distance in devices]
    return lax.ppermute(block, axis, route)


def exchange(rows):
    return lax.all_to_all(rows, BOTH, 0, 0, tiled=True)


def per_device(
    scan_features, occupancy, kernels, kernel_m, kernel_v, norm_params, norm_m, norm_v, cotangent
):
    x = jnp.transpose(scan_features, (1, 0, 2))
    cot = jnp.transpose(cotangent, (1, 0, 2))
    occ = jnp.transpose(occupancy, (2, 0, 1))
    kt, kmt, kvt = (jnp.transpose(a, (0, 2, 1)) for a in (kernels, kernel_m, kernel_v))
    gy, gx = (lax.axis_size("gy"), lax.axis_size("gx"))
    devices = gy * gx
    y, z = (lax.axis_index("gy"), lax.axis_index("gx"))
    flags = jnp.stack([y > 0, y < gy - 1, z > 0, z < gx - 1]).astype(jnp.int32)
    rows, scan_count, lanes = x.shape
    r, tiles = (rows // 2, lanes // L // 2)
    count = float(scan_count * r * tiles)
    last = (tiles - 1) * L

    down, cot_down, corner, xcol = edges(x, occ, cot)
    xcol = shifted(xcol, "gx", 1)
    down = shifted(down, "gy", 1)
    cot_down = shifted(cot_down, "gy", -1)
    corner = lax.ppermute(
        corner, BOTH, [(i, i + gx + 1) for i in range(devices - gx) if (i + 1) % gx]
    )
    bits, w1, w2, w2b, w1b, np2 = prepare(occ, kt, norm_params)

    xcol, cot_down, flags = lax.optimization_barrier((xcol, cot_down, flags))
    c1, st1, up, low_rows, edge = conv_one(x, bits, down, xcol, corner, w1, devices)
    down_in = shifted(up, "gy", -1)
    up_in = shifted(low_rows, "gy", 1)
    going_right, going_left = pack_edges(up_in, edge, down_in)
    left_in = shifted(going_right, "gx", 1)
    right_in = shifted(going_left, "gx", -1)
    st1 = exchange(st1)

    c2, n1, hid, st2 = conv_two(
        flags, c1, up_in, down_in, left_in, right_in, st1, np2, w2, count
    )
    st2 = exchange(st2)
    features, d2, sums2 = output(c2, st2, np2, cot, down, cot_down, count)
    sums2 = exchange(sums2)
    going_right, going_left = rim_two(flags, d2, c2, st2, sums2, np2, count)
    left_in = shifted(going_right, "gx", 1)
    right_in = shifted(going_left, "gx", -1)
    ds, kg2 = back_two(flags, d2, c2, hid, st2, sums2, np2, count)
    d1, edge, sums1 = hidden_gradient(ds, left_in, right_in, n1, np2, w2b, devices)
    edge = shifted(edge, "gx", -1)
    sums1 = exchange(sums1)
    d1, grads = back_one(flags, d1, edge, n1, x, bits, st1, sums1, np2, kg2, count)
    share = grads.shape[0] // devices
    grads = exchange(grads)
    input_grad = input_gradient(d1, bits, w1b, 0, None)
    grads = exchange(sum_share(grads, share))
    input_grad = input_gradient(d1, bits, w1b, 1, input_grad)
    norm, k, km, kv, low, n, nm, nv = update(
        grads, sums1, sums2, kt, kmt, kvt, norm_params, norm_m, norm_v
    )
    back = lambda a: jnp.transpose(a, (0, 2, 1))
    deep = lambda a: a.reshape(norm_params.shape)
    return (
        jnp.transpose(features, (1, 0, 2)),
        jnp.transpose(input_grad, (1, 0, 2)),
        norm.reshape(()),
        back(k),
        back(km),
        back(kv),
        back(low),
        deep(n),
        deep(nm),
        deep(nv),
    )


def solution(mesh):
    split = P(None, "gy", "gx")
    return jax.shard_map(
        per_device,
        mesh=mesh,
        in_specs=(split, split) + (P(),) * 6 + (split,),
        out_specs=(split, split) + (P(),) * 8,
        check_vma=False,
    )
```

```python
import functools
import math

import jax
import jax.numpy as jnp
from jax import lax
from jax.experimental import pallas as pl
from jax.experimental.pallas import tpu as pltpu
from jax.sharding import PartitionSpec as P

norm_eps = 1e-05
adam_beta = 0.5
adam_eps = 1e-08
step_count = 5
clip_limit = 1.0
kernel_rate = 0.04
norm_rate = 0.25
kernel_decay = 0.01

f32, bf16 = (jnp.float32, jnp.bfloat16)
BOTH = ("gy", "gx")
S, S2, C, L, BITS = (16, 32, 64, 128, 13)


def params_of(limit=20):
    return pltpu.CompilerParams(
        dimension_semantics=("arbitrary",), vmem_limit_bytes=limit << 20
    )


def cost(microseconds):
    return pl.CostEstimate(
        flops=0, bytes_accessed=int(microseconds * 3.6e6), transcendentals=0
    )


def whole(shape):
    return pl.BlockSpec(shape, lambda g: (0,) * len(shape))


def scans(rows, lanes, n=S):
    return pl.BlockSpec((rows, n, lanes), lambda g: (0, g, 0))


def more(rows, lanes):
    return scans(rows, lanes, S2)


def resident(shape, dtype):
    return pltpu.VMEM(shape, dtype)


held = pl.BlockSpec(memory_space=pltpu.VMEM)


def hbm(array):
    return pltpu.with_memory_space_constraint(array, pltpu.HBM)


def part_of(ref, step, n=S):
    return ref.at[:, pl.ds(pl.multiple_of(step * n, n), n), :]


def low_half(rows=S):
    return lax.broadcasted_iota(jnp.int32, (rows, L), 1) < C


def swap(x):
    return pltpu.roll(x, C, 1)


def fold(x):
    x = jnp.broadcast_to(x, (8, L))
    return (x + swap(x))[:1]


def live(word, row, x):
    bit = 1 << (row % BITS)
    if x.dtype == bf16:
        return jnp.where((word & jnp.int16(bit)) != 0, x, jnp.zeros_like(x))
    return jnp.where((word.astype(jnp.int32) & bit) != 0, x, 0.0)


def pair(ref, row, t):
    return ref[row, :, t * L : (t + 1) * L]


def stats_of(st_ref, count):
    groups = 2 * st_ref.shape[0]
    means = st_ref[:, 0, :]
    mean = fold(jnp.sum(means, axis=0, keepdims=True)) / groups
    spread = st_ref[:, 1, :] + count * (means - mean) ** 2
    spread = fold(jnp.sum(spread, axis=0, keepdims=True)) / (groups * count)
    return (mean, lax.rsqrt(spread + norm_eps))


def sums_of(st_ref):
    return tuple(fold(jnp.sum(st_ref[:, k, :], axis=0, keepdims=True)) for k in range(2))


def pilot_of(block):
    flat = block.reshape(-1, L)
    return jnp.sum(flat, axis=0, keepdims=True) / flat.shape[0]


def finish_stats(step, steps, pilot, sums, count, run_ref, st_ref):
    off, squares = (jnp.sum(s, axis=0, keepdims=True) for s in sums)
    mean = pilot + off / count
    squares = squares - off * off / count

    @pl.when(step == 0)
    def _():
        run_ref[0:1] = mean
        run_ref[1:2] = squares

    @pl.when(step > 0)
    def _():
        before = step.astype(f32)
        share = 1.0 / (before + 1.0)
        delta = mean - run_ref[0:1]
        run_ref[0:1] = run_ref[0:1] + delta * share
        run_ref[1:2] = run_ref[1:2] + squares + delta * delta * (count * before * share)

    @pl.when(step == steps - 1)
    def _():
        st_ref[...] = jnp.broadcast_to(run_ref[0:2][None], st_ref.shape)


def off_sums(blocks, pilot):
    sums = [jnp.zeros((8, L), f32), jnp.zeros((8, L), f32)]
    for block in blocks:
        d = block - pilot
        sums = [sums[0] + halves(d), sums[1] + halves(d * d)]
    return sums


def added(a, b):
    return b if a is None else [x + y for x, y in zip(a, b)]


def rim_of(first, second, row, low):
    half = first.shape[0]
    if row < half:
        return jnp.where(low, first[row].astype(f32), second[row].astype(f32))
    row = row - half
    return swap(jnp.where(low, second[row].astype(f32), first[row].astype(f32)))


def halves(x):
    total = x[:8]
    for k in range(8, x.shape[0], 8):
        total = total + x[k : k + 8]
    return total


def occupancy_words(occ, groups, first):
    rows = occ.shape[1]
    shape = (rows, groups * L)
    group_of = lax.broadcasted_iota(jnp.int32, shape, 1) // L + first
    inner = lax.broadcasted_iota(jnp.int32, shape, 0) - group_of * BITS
    power = jnp.where(
        (inner >= 0) & (inner < BITS), (1 << jnp.clip(inner, 0, BITS)), 0
    ).astype(bf16)
    low = occ.astype(f32).astype(bf16)
    return jnp.dot(low, power, preferred_element_type=f32).astype(jnp.int32)


def edges_kernel(
    row_ref, col_ref, occ_ref, cot_last_ref, cot_first_ref, down_ref, up_ref, corner_ref, xcol_ref
):
    cols, scan_count, rows = occ_ref.shape
    lanes = row_ref.shape[2]
    groups = -(-rows // BITS)
    low = low_half(scan_count)
    words = occupancy_words(occ_ref[...].reshape(cols * scan_count, rows), 1, groups - 1)
    words = words.reshape(cols // 2, 2, scan_count, L)
    for t in range(cols // 2):
        word = jnp.where(low, words[t, 0], words[t, 1])
        x = live(word, rows - 1, row_ref[0, :, t * L : (t + 1) * L].astype(f32)).astype(bf16)
        down_ref[:, t * L : (t + 1) * L] = x
    corner_ref[...] = x
    down_ref[:, lanes:] = cot_last_ref[0]
    up_ref[...] = cot_first_ref[...]
    words = occupancy_words(occ_ref[cols - 1], groups, 0)
    for i in range(rows // 2):
        even, odd = (
            live(
                words[:, row // BITS * L : (row // BITS + 1) * L], row, col_ref[row].astype(f32)
            )
            for row in (2 * i, 2 * i + 1)
        )
        xcol_ref[i] = jnp.where(low, swap(even), odd).astype(bf16)


def edges(x, occ, cot):
    rows, scan_count, lanes = x.shape
    r, wide = (rows // 2, lanes // 2)
    outs = [
        jax.ShapeDtypeStruct((scan_count, lanes + wide), bf16),
        jax.ShapeDtypeStruct((2, scan_count, wide), bf16),
        jax.ShapeDtypeStruct((scan_count, L), bf16),
        jax.ShapeDtypeStruct((r, scan_count, L), bf16),
    ]
    return pl.pallas_call(
        edges_kernel,
        grid=(1,),
        in_specs=[
            pl.BlockSpec((1, scan_count, lanes), lambda g: (rows - 1, 0, 0)),
            pl.BlockSpec((rows, scan_count, L), lambda g: (0, 0, lanes // L - 1)),
            whole(occ.shape),
            pl.BlockSpec((1, scan_count, wide), lambda g: (r - 1, 0, 0)),
            pl.BlockSpec((2, scan_count, wide), lambda g: (0, 0, 0)),
        ],
        out_specs=[whole(o.shape) for o in outs],
        out_shape=outs,
        compiler_params=params_of(),
        cost_estimate=cost(3),
        name="edges",
    )(hbm(x), hbm(x), hbm(occ), hbm(cot), hbm(cot))


def prep_kernel(occ_ref, kt_ref, np_ref, bits_ref, w1_ref, w2_ref, w2b_ref, w1b_ref, np2_ref):
    cols, scan_count, rows = occ_ref.shape
    groups = bits_ref.shape[0]
    words = occupancy_words(occ_ref[...].reshape(cols * scan_count, rows), groups, 0)
    words = words.reshape(cols // 2, 2, scan_count, groups * L)
    low = low_half(scan_count)
    for g in range(groups):
        for t in range(cols // 2):
            lanes = slice(g * L, (g + 1) * L)
            word = jnp.where(low, words[t, 0, :, lanes], words[t, 1, :, lanes])
            bits_ref[g, :, t * L : (t + 1) * L] = word.astype(jnp.int16)
    back = [[kt_ref[l, :, k * C : (k + 1) * C] for k in range(9)] for l in range(2)]
    fore = [[jnp.transpose(b) for b in layer] for layer in back]
    none = jnp.zeros((C, C), f32)

    def put(ref, rows_of, cols_of, pick):
        for a in range(rows_of):
            blocks = [pick(a, b) for b in range(cols_of)]
            for k in range(0, cols_of, 2):
                two = jnp.concatenate(blocks[k : k + 2], axis=1).astype(bf16)
                ref[a * C : (a + 1) * C, k * C : (k + 2) * C] = two

    def tap(table, p, q):
        return table[3 * p + q] if 0 <= p < 3 and 0 <= q < 3 else none

    put(w1_ref, 30, 4, lambda a, b: tap(fore[0], a // 6 - 2 * (b // 2), a % 6 - 2 * (b % 2) - 1))
    put(w2_ref, 16, 4, lambda a, b: tap(fore[1], a // 4 - b // 2, a % 4 - b % 2))
    put(w2b_ref, 16, 4, lambda a, b: tap(back[1], b // 2 + 2 - a // 4, b % 2 + 2 - a % 4))
    put(w1b_ref, 12, 4, lambda a, b: tap(back[0], (1, 2, 0)[a // 4], b + 3 - 2 * (a % 4)))
    np2_ref[...] = jnp.concatenate([np_ref[...], np_ref[...]], axis=1)


def prepare(occ, kt, norm_params):
    cols, scan_count, rows = occ.shape
    full = lambda *shape: jax.ShapeDtypeStruct(shape, bf16)
    outs = [
        jax.ShapeDtypeStruct((-(-rows // BITS), scan_count, cols * C), jnp.int16),
        full(30 * C, 4 * C),
        full(16 * C, 4 * C),
        full(16 * C, 4 * C),
        full(12 * C, 4 * C),
        jax.ShapeDtypeStruct((4, L), f32),
    ]
    return pl.pallas_call(
        prep_kernel,
        grid=(1,),
        in_specs=[whole(occ.shape), whole(kt.shape), whole((4, C))],
        out_specs=[whole(o.shape) for o in outs],
        out_shape=outs,
        compiler_params=params_of(),
        cost_estimate=cost(4),
        name="prepare",
    )(hbm(occ), kt, norm_params.reshape(4, C))


def mask_tile(x_ref, bits_ref, t, xs, into):
    rows = x_ref.shape[0]
    for g in range(bits_ref.shape[0]):
        word = bits_ref[g, :, t * L : (t + 1) * L]
        for row in range(g * BITS, min(rows, (g + 1) * BITS)):
            x = live(word, row, pair(x_ref, row, t))
            xs[(row + 1) // 4, (row + 1) % 4, :, into * L : (into + 1) * L] = x


def clear_rows(rows, pairs, xs):
    for k in range(rows + 1, 4 * pairs + 1):
        xs[k // 4, k % 4] = jnp.zeros_like(xs[0, 0])


def conv_rows(xs, lanes, w, r, before=()):
    pairs = (r + 1) // 2
    pieces = [xs[0:pairs, q, :, lanes] for q in range(4)] + [xs[1 : pairs + 1, 0, :, lanes]]
    pieces = [p.reshape(pairs * S, p.shape[2]) for p in pieces]
    lhs = jnp.concatenate(list(before) + pieces, axis=1)
    acc = jnp.dot(lhs, w, preferred_element_type=f32).reshape(pairs, S, 2 * L)
    return [acc[i // 2, :, (i % 2) * L : (i % 2 + 1) * L] for i in range(r)]


def first_last_kernel(
    xa_ref, xb_ref, ba_ref, bb_ref, xrow_ref, xcol_ref, corner_ref, w_ref, c_ref, st_ref, er_ref,
    el_ref, edge_ref, xs, run,
):
    step, steps = (pl.program_id(0), pl.num_programs(0))
    c_ref = part_of(c_ref, step)
    rows, lanes = (xa_ref.shape[0], xrow_ref.shape[1] * 2 // 3)
    r = rows // 2
    low = low_half()

    @pl.when(step == 0)
    def _():
        clear_rows(rows, (r + 1) // 2, xs)

    xs[0, 0, :, :L] = xrow_ref[:, :L]
    xs[0, 0, :, L:] = xrow_ref[:, lanes - 2 * L : lanes]
    mask_tile(xa_ref, ba_ref, 0, xs, 0)
    mask_tile(xb_ref, bb_ref, 0, xs, 1)
    mask_tile(xb_ref, bb_ref, 1, xs, 2)
    wide = 3 * L
    rows_of = lambda q, a, b: w_ref[q * wide + a * C : q * wide + b * C]
    w = jnp.concatenate([rows_of(q, 0, 4) for q in range(5)], axis=0)
    last = conv_rows(xs, slice(L, 3 * L), w, r)
    pairs = (r + 1) // 2
    none = jnp.zeros((S, L), bf16)
    beside = [corner_ref[...]] + [xcol_ref[i] for i in range(r)] + [none]
    w = [jnp.zeros((C, 2 * L), bf16)] + [rows_of(q, 3, 4) for q in range(5)]
    w = jnp.concatenate(w + [rows_of(q, 4, 6) for q in range(5)], axis=0)
    more_lhs = [
        jnp.concatenate([beside[2 * m + k] for m in range(pairs)], axis=0) for k in range(3)
    ]
    first = conv_rows(xs, slice(0, L), w, r, more_lhs)
    edge = [jnp.where(low, b, a) for a, b in zip(first, last)]
    pilot = pilot_of(jnp.concatenate(edge[: r // 2], axis=0))
    for i in range(r):
        c_ref[i, :, :L] = first[i]
        c_ref[i, :, L:] = last[i]
        edge_ref[i] = edge[i].astype(bf16)
    finish_stats(step, steps, pilot, off_sums(edge, pilot), float(r * S), run, st_ref)
    half = er_ref.shape[0]
    for k in range(half):
        far = swap(edge[k + half]) if k + half < r else jnp.zeros((S, L), f32)
        er_ref[k] = jnp.where(low, edge[k], far).astype(bf16)
        el_ref[k] = jnp.where(low, far, edge[k]).astype(bf16)


def first_last(x, bits, down, xcol, corner, w):
    rows, scan_count, lanes = x.shape
    r = rows // 2
    shape = lambda dtype, *s: jax.ShapeDtypeStruct(s, dtype)
    at = lambda n, width, k: pl.BlockSpec((n, S, width), lambda g: (0, g, k))
    end = lanes // (2 * L) - 1
    return pl.pallas_call(
        first_last_kernel,
        grid=(scan_count // S,),
        in_specs=[
            at(rows, L, 0),
            at(rows, 2 * L, end),
            at(bits.shape[0], L, 0),
            at(bits.shape[0], 2 * L, end),
            pl.BlockSpec((S, down.shape[1]), lambda g: (g, 0)),
            scans(r, L),
            pl.BlockSpec((S, L), lambda g: (g, 0)),
            whole(w.shape),
        ],
        out_specs=[
            held,
            whole((1, 2, L)),
            scans((r + 1) // 2, L),
            scans((r + 1) // 2, L),
            scans(r, L),
        ],
        out_shape=[
            resident((r, scan_count, 2 * L), f32),
            shape(f32, 1, 2, L),
            shape(bf16, (r + 1) // 2, scan_count, L),
            shape(bf16, (r + 1) // 2, scan_count, L),
            shape(bf16, r, scan_count, L),
        ],
        scratch_shapes=[
            pltpu.VMEM(((r + 1) // 2 + 1, 4, S, 3 * L), bf16),
            pltpu.VMEM((8, L), f32),
        ],
        compiler_params=params_of(),
        cost_estimate=cost(4),
        name="conv_one_ends",
    )(hbm(x), hbm(x), hbm(bits), hbm(bits), down, xcol, corner, w)


def conv_one_kernel(
    x_ref, bits_ref, xrow_ref, ends_ref, w_ref, c_ref, st_ref, up_ref, down_ref, xs, run
):
    step, steps = (pl.program_id(0), pl.num_programs(0))
    c_ref = part_of(c_ref, step)
    rows, tiles = (x_ref.shape[0], x_ref.shape[2] // L)
    r, inner = (rows // 2, tiles // 2 - 1)

    @pl.when(step == 0)
    def _():
        clear_rows(rows, (r + 1) // 2, xs)

    xs[0, 0] = xrow_ref[:, : tiles * L]
    sums, pilot = (None, None)
    filled = 0
    for t in range(inner):
        while filled < 2 * t + 3:
            mask_tile(x_ref, bits_ref, filled, xs, filled)
            filled += 1
        blocks = conv_rows(xs, slice(2 * t * L, (2 * t + 3) * L), w_ref[...], r)
        if pilot is None:
            pilot = pilot_of(jnp.concatenate(blocks[: r // 2], axis=0))
        sums = added(sums, off_sums(blocks, pilot))
        for i, block in enumerate(blocks):
            c_ref[i, :, t * L : (t + 1) * L] = block
    finish_stats(step, steps, pilot, sums, float(r * inner * S), run, st_ref)
    up_ref[...] = c_ref[0:3].astype(bf16)
    down_ref[...] = c_ref[r - 2 : r].astype(bf16)

    @pl.when(step == steps - 1)
    def _():
        own, more = (float(r * S) * steps * n for n in (inner, 1))
        delta = ends_ref[0, 0:1] - run[0:1]
        mean = run[0:1] + delta * (more / (own + more))
        squares = run[1:2] + ends_ref[0, 1:2] + delta * delta * (own * more / (own + more))
        row = jnp.concatenate([mean, squares], axis=0)
        st_ref[...] = jnp.broadcast_to(row[None], st_ref.shape)


def conv_one(x, bits, down, ends, w, devices):
    rows, scan_count, lanes = x.shape
    r, wide = (rows // 2, lanes // 2 - L)
    shape = lambda dtype, *s: jax.ShapeDtypeStruct(s, dtype)
    return pl.pallas_call(
        conv_one_kernel,
        grid=(scan_count // S,),
        in_specs=[
            scans(rows, lanes),
            scans(bits.shape[0], lanes),
            pl.BlockSpec((S, down.shape[1]), lambda g: (g, 0)),
            whole(ends.shape),
            whole(w.shape),
        ],
        out_specs=[held, whole((devices, 2, L)), scans(3, wide), scans(2, wide)],
        out_shape=[
            resident((r, scan_count, wide), f32),
            shape(f32, devices, 2, L),
            shape(bf16, 3, scan_count, wide),
            shape(bf16, 2, scan_count, wide),
        ],
        scratch_shapes=[
            pltpu.VMEM(((r + 1) // 2 + 1, 4, S, lanes), bf16),
            pltpu.VMEM((8, L), f32),
        ],
        compiler_params=params_of(),
        cost_estimate=cost(11),
        name="conv_one",
    )(hbm(x), hbm(bits), down, ends, w)


def pack_kernel(up_ref, down_ref, edge_ref, left_ref, right_ref, up_out, down_out):
    r, wide = (edge_ref.shape[0], up_ref.shape[2])
    low = low_half()
    for src, out, first in ((up_ref, up_out, 0), (down_ref, down_out, r - 2)):
        out[:, :, :wide] = src[...]
        for k in range(src.shape[0]):
            out[k, :, wide : wide + L] = edge_ref[first + k]
            out[k, :, wide + L :] = rim_of(left_ref, right_ref, first + k, low).astype(bf16)


def pack_rows(up, down, edge, left, right):
    r, scan_count, _lanes = edge.shape
    wide = up.shape[2]
    return pl.pallas_call(
        pack_kernel,
        grid=(scan_count // S,),
        in_specs=[
            scans(3, wide), scans(2, wide), scans(r, L), scans(left.shape[0], L),
            scans(right.shape[0], L),
        ],
        out_specs=[scans(3, wide + 2 * L), scans(2, wide + 2 * L)],
        out_shape=[
            jax.ShapeDtypeStruct((n, scan_count, wide + 2 * L), bf16) for n in (3, 2)
        ],
        compiler_params=params_of(),
        cost_estimate=cost(1),
        name="pack_rows",
    )(up, down, edge, left, right)


def conv_two_kernel(
    flags, c_ref, ends_ref, up_ref, down_ref, left_ref, right_ref, st_ref, np_ref, w_ref, c2_ref,
    n1_ref, hid_ref, st2_ref, rim, run, *, count,
):
    step, steps = (pl.program_id(0), pl.num_programs(0))
    c_ref, ends_ref, c2_ref, n1_ref = (
        part_of(a, step, S2) for a in (c_ref, ends_ref, c2_ref, n1_ref)
    )
    r, tiles = (c_ref.shape[0], c_ref.shape[2] // L + 2)
    t_out = tiles - 1
    mean, inv = stats_of(st_ref, count)
    offset = -mean * inv
    scale = 0.5 * np_ref[0:1] * inv
    shift = 0.5 * (np_ref[0:1] * offset + np_ref[1:2])
    f_up, f_down, f_left, f_right = (flags[k].astype(f32) for k in range(4))
    low = low_half(S2)
    left = jnp.where(low, f_left, 1.0)
    right = jnp.where(low, 1.0, f_right)
    for row in range(r):
        rim[row] = rim_of(left_ref, right_ref, row, low)

    def act(row, t):
        at_end = t in (0, tiles - 1)
        if 2 <= row < r + 2:
            flag = None
            c = pair(ends_ref, row - 2, min(t, 1)) if at_end else pair(c_ref, row - 2, t - 1)
            beyond = rim[row - 2] if at_end else None
        else:
            src, k, flag = (up_ref, row, f_up) if row < 2 else (down_ref, row - r - 2, f_down)
            c = pair(src, k, tiles - 2 if at_end else t - 1).astype(f32)
            beyond = pair(src, k, tiles - 1).astype(f32) if at_end else None
        if t == 0:
            c = jnp.where(low, beyond, c)
        if t == tiles - 1:
            c = jnp.where(low, c, beyond)
        h = c * scale + shift
        out = h + h * jnp.tanh(h)
        if t == 0:
            out = out * left
        if t == tiles - 1:
            out = out * right
        if flag is not None:
            out = out * flag
        out = out.astype(bf16)
        hid_ref[row, :, t * L : (t + 1) * L] = out
        if 2 <= row < r + 3:
            n1_ref[row - 2, :, t * L : (t + 1) * L] = (c * inv + offset).astype(bf16)

    pairs = (r + 3) // 2
    sums, pilot = (None, None)
    for t in range(tiles):
        for row in range(r + 5):
            act(row, t)
        k = t - 1
        if k < 0:
            continue
        lanes = slice(k * L, (k + 2) * L)
        pieces = [
            jnp.concatenate([hid_ref[2 * m + a, :, lanes] for m in range(pairs)], axis=0)
            for a in range(4)
        ]
        lhs = jnp.concatenate(pieces, axis=1)
        acc = jnp.dot(lhs, w_ref[...], preferred_element_type=f32).reshape(pairs, S2, 2 * L)
        if pilot is None:
            pilot = pilot_of(acc[1 : r // 2, :, :L])
        blocks = []
        for row in range(r + 3):
            block = acc[row // 2, :, (row % 2) * L : (row % 2 + 1) * L]
            c2_ref[row, :, k * L : (k + 1) * L] = block
            if 0 < row <= r:
                blocks.append(block)
        sums = added(sums, off_sums(blocks, pilot))
    finish_stats(step, steps, pilot, sums, float(r * t_out * S2), run, st2_ref)


def conv_two(flags, c1, ends, up, down, left, right, st, np2, w, count):
    r, scan_count, wide = c1.shape
    wide = wide + 2 * L
    lanes = wide - L
    devices = st.shape[0]
    return pl.pallas_call(
        functools.partial(conv_two_kernel, count=count),
        grid=(scan_count // S2,),
        in_specs=[
            pl.BlockSpec(memory_space=pltpu.SMEM),
            held,
            held,
            more(2, wide),
            more(3, wide),
            more(left.shape[0], L),
            more(right.shape[0], L),
            whole(st.shape),
            whole(np2.shape),
            whole(w.shape),
        ],
        out_specs=[held, held, more(r + 5, wide), whole((devices, 2, L))],
        out_shape=[
            resident((r + 3, scan_count, lanes), f32),
            resident((r + 1, scan_count, wide), bf16),
            pltpu.HBM((r + 5, scan_count, wide), bf16),
            jax.ShapeDtypeStruct((devices, 2, L), f32),
        ],
        scratch_shapes=[
            pltpu.VMEM((r, S2, L), f32),
            pltpu.VMEM((8, L), f32),
        ],
        compiler_params=params_of(),
        cost_estimate=cost(14),
        name="conv_two",
    )(flags, c1, ends, up, down, left, right, st, np2, w)


def output_kernel(
    c2_ref, st_ref, np_ref, cot_ref, up_ref, down_ref, feat_ref, d_ref, sum_ref, run, *, count,
):
    step, steps = (pl.program_id(0), pl.num_programs(0))
    c2_ref, d_ref = (part_of(a, step, S2) for a in (c2_ref, d_ref))
    r, tiles = (cot_ref.shape[0], cot_ref.shape[2] // L)
    mean, inv = stats_of(st_ref, count)
    offset = -mean * inv
    scale = 0.5 * np_ref[2:3] * inv
    shift = 0.5 * (np_ref[2:3] * offset + np_ref[3:4])
    above = 2 * tiles

    def slope(c, cot):
        h = c * scale + shift
        s = 1.0 + jnp.tanh(h)
        f = h * s
        return (f, cot.astype(f32) * (s + f * (2.0 - s)))

    sums = None
    for t in range(tiles):
        part = [jnp.zeros((8, L), f32), jnp.zeros((8, L), f32)]
        for i in range(r):
            c = pair(c2_ref, i + 1, t)
            f, d = slope(c, pair(cot_ref, i, t))
            feat_ref[i, :, t * L : (t + 1) * L] = f.astype(bf16)
            d_ref[i + 1, :, t * L : (t + 1) * L] = d
            part = [part[0] + halves(d), part[1] + halves(d * c)]
        sums = added(sums, part)
    for t in range(tiles):
        lanes = slice(t * L, (t + 1) * L)
        cot = up_ref[:, (above + t) * L : (above + t + 1) * L]
        d_ref[0, :, lanes] = slope(pair(c2_ref, 0, t), cot)[1]
        for k in range(2):
            row = r + 1 + k
            d_ref[row, :, lanes] = slope(pair(c2_ref, row, t), pair(down_ref, k, t))[1]
    sums = (0.5 * sums[0], (0.5 * inv) * (sums[1] - mean * sums[0]))
    add_sums(step, steps, sums, run, sum_ref)


def add_sums(step, steps, sums, run, sum_ref):
    rows = jnp.concatenate([jnp.sum(s, axis=0, keepdims=True) for s in sums], axis=0)

    @pl.when(step == 0)
    def _():
        run[0:2] = rows

    @pl.when(step > 0)
    def _():
        run[0:2] = run[0:2] + rows

    @pl.when(step == steps - 1)
    def _():
        sum_ref[...] = jnp.broadcast_to(run[0:2][None], sum_ref.shape)


def output(c2, st, np2, cot, up, down, count):
    r, scan_count, lanes = cot.shape
    devices = st.shape[0]
    return pl.pallas_call(
        functools.partial(output_kernel, count=count),
        grid=(scan_count // S2,),
        in_specs=[
            held,
            whole(st.shape),
            whole(np2.shape),
            more(r, lanes),
            pl.BlockSpec((S2, up.shape[1]), lambda g: (g, 0)),
            more(2, lanes),
        ],
        out_specs=[more(r, lanes), held, whole((devices, 2, L))],
        out_shape=[
            jax.ShapeDtypeStruct((r, scan_count, lanes), bf16),
            resident((r + 3, scan_count, lanes), f32),
            jax.ShapeDtypeStruct((devices, 2, L), f32),
        ],
        scratch_shapes=[pltpu.VMEM((8, L), f32)],
        compiler_params=params_of(),
        cost_estimate=cost(12),
        name="output",
    )(c2, st, np2, hbm(cot), up, down)


def norm_back_two(flags, st_ref, sum_ref, np_ref, count, rows):
    cells = 2.0 * count * st_ref.shape[0]
    mean, inv = stats_of(st_ref, count)
    shift_sum, gain_sum = sums_of(sum_ref)
    gain = np_ref[2:3] * inv
    c_n = -gain * inv * gain_sum / cells
    c_0 = -gain * shift_sum / cells - c_n * mean
    gain = 0.5 * gain
    f_up, f_down = (flags[k].astype(f32) for k in range(2))

    def back(row, d, c):
        d = d * gain + (c * c_n + c_0)
        if isinstance(row, int):
            if row == 0:
                d = d * f_up
            if row > rows:
                d = d * f_down
        return d

    return back


def rim_two_kernel(
    flags, d_ref, c_ref, st_ref, sum_ref, np_ref, er_ref, el_ref, *, count
):
    d_ref, c_ref = (part_of(a, pl.program_id(0), S2) for a in (d_ref, c_ref))
    rows, last = (d_ref.shape[0], d_ref.shape[2] // L - 1)
    back = norm_back_two(flags, st_ref, sum_ref, np_ref, count, rows - 3)
    low = low_half(S2)
    half = rows // 2
    column = lambda row, t: back(row, pair(d_ref, row, t), pair(c_ref, row, t))
    both = lambda row: jnp.where(low, column(row, 0), column(row, last))
    for k in range(half):
        near, far = (both(k), swap(both(k + half)))
        el_ref[k] = jnp.where(low, near, far).astype(bf16)
        er_ref[k] = jnp.where(low, far, near).astype(bf16)


def rim_two(flags, d, c2, st, sums, np2, count):
    rows, scan_count, lanes = d.shape
    return pl.pallas_call(
        functools.partial(rim_two_kernel, count=count),
        grid=(scan_count // S2,),
        in_specs=[
            pl.BlockSpec(memory_space=pltpu.SMEM), held, held, whole(st.shape),
            whole(sums.shape), whole(np2.shape),
        ],
        out_specs=[more(rows // 2, L)] * 2,
        out_shape=[jax.ShapeDtypeStruct((rows // 2, scan_count, L), bf16)] * 2,
        compiler_params=params_of(),
        cost_estimate=cost(3),
        name="rim_two",
    )(flags, d, c2, st, sums, np2)


def back_two_kernel(
    flags, d_ref, c2_ref, hid_ref, st_ref, sum_ref, np_ref, ds_ref, kg_ref, grad, *, count
):
    step, steps = (pl.program_id(0), pl.num_programs(0))
    d_ref, c2_ref, ds_ref = (part_of(a, step) for a in (d_ref, c2_ref, ds_ref))
    r, tiles = (c2_ref.shape[0] - 3, c2_ref.shape[2] // L)
    back = norm_back_two(flags, st_ref, sum_ref, np_ref, count, r)

    @pl.when(step == 0)
    def _():
        grad[...] = jnp.zeros_like(grad)

    total = None
    for t in range(tiles):
        for row in range(r + 3):
            d = back(row, pair(d_ref, row, t), pair(c2_ref, row, t))
            ds_ref[row, :, t * L : (t + 1) * L] = d.astype(bf16)
        lanes = slice(t * L, (t + 2) * L)
        rhs = jnp.concatenate(
            [hid_ref[p + 1 : p + 1 + r, :, lanes].reshape(r * S, 2 * L) for p in range(3)], axis=1
        )
        lhs = ds_ref[1 : r + 1, :, t * L : (t + 1) * L].reshape(r * S, L)
        part = lax.dot_general(lhs, rhs, (((0,), (0,)), ((), ())), preferred_element_type=f32)
        total = part if total is None else total + part
    grad[...] += total

    @pl.when(step == steps - 1)
    def _():
        for p in range(3):
            for q in range(3):
                block = None
                for w in range(2):
                    at = 4 * p * C + (w + q) * C
                    part = grad[w * C : (w + 1) * C, at : at + C]
                    block = part if block is None else block + part
                kg_ref[3 * p + q] = block


def back_two(flags, d, c2, hid, st, sums, np2, count):
    r, scan_count, wide = hid.shape
    r, lanes = (r - 5, wide - L)
    return pl.pallas_call(
        functools.partial(back_two_kernel, count=count),
        grid=(scan_count // S,),
        in_specs=[
            pl.BlockSpec(memory_space=pltpu.SMEM),
            held,
            held,
            scans(r + 5, wide),
            whole(st.shape),
            whole(sums.shape),
            whole(np2.shape),
        ],
        out_specs=[held, whole((9, C, C))],
        out_shape=[
            resident((r + 3, scan_count, lanes), bf16),
            jax.ShapeDtypeStruct((9, C, C), f32),
        ],
        scratch_shapes=[pltpu.VMEM((L, 12 * C), f32)],
        compiler_params=params_of(),
        cost_estimate=cost(12),
        name="back_two",
    )(flags, d, c2, hbm(hid), st, sums, np2)


def hidden_kernel(
    ds_ref, left_ref, right_ref, n1_ref, np_ref, w_ref, dp_ref, edge_ref, sum1_ref, rim, run
):
    step, steps = (pl.program_id(0), pl.num_programs(0))
    ds_ref, n1_ref, dp_ref = (part_of(a, step) for a in (ds_ref, n1_ref, dp_ref))
    r, tiles = (n1_ref.shape[0] - 1, n1_ref.shape[2] // L)
    pairs = (r + 1) // 2
    low = low_half()
    for row in range(r + 3):
        rim[row] = rim_of(right_ref, left_ref, row, low).astype(bf16)
    scale, shift = (0.5 * np_ref[0:1], 0.5 * np_ref[1:2])
    sums = None
    for t in range(tiles):
        parts = []
        for k in (t - 1, t):
            part = ds_ref[:, :, k * L : (k + 1) * L] if 0 <= k < tiles - 1 else rim[...]
            parts.append(part.reshape(pairs + 1, 2, S, L))
        pieces = [p[a : a + pairs, b] for a in range(2) for b in range(2) for p in parts]
        lhs = jnp.concatenate([p.reshape(pairs * S, L) for p in pieces], axis=1)
        acc = jnp.dot(lhs, w_ref[...], preferred_element_type=f32).reshape(pairs, S, 2 * L)
        part = [jnp.zeros((8, L), f32), jnp.zeros((8, L), f32)]
        for i in range(r + 1):
            n = pair(n1_ref, i, t).astype(f32)
            h = n * scale + shift
            s = 1.0 + jnp.tanh(h)
            d = acc[i // 2, :, (i % 2) * L : (i % 2 + 1) * L] * (s + h * s * (2.0 - s))
            dp_ref[i, :, t * L : (t + 1) * L] = d
            if i < r:
                if t == 0:
                    d = jnp.where(low, 0.0, d)
                if t == tiles - 1:
                    d = jnp.where(low, d, 0.0)
                part = [part[0] + halves(d), part[1] + halves(d * n)]
        sums = added(sums, part)
    add_sums(step, steps, [0.5 * x for x in sums], run, sum1_ref)
    for i in range(pairs):
        both = jnp.where(low, swap(pair(dp_ref, pairs + i, 0)), pair(dp_ref, i, 0))
        edge_ref[i] = both.astype(bf16)


def hidden_gradient(ds, left, right, n1, np2, w, devices):
    r, scan_count, wide = n1.shape
    r, lanes = (r - 1, wide - L)
    half = left.shape[0]
    return pl.pallas_call(
        hidden_kernel,
        grid=(scan_count // S,),
        in_specs=[
            held,
            scans(half, L),
            scans(half, L),
            held,
            whole(np2.shape),
            whole(w.shape),
        ],
        out_specs=[
            held,
            scans((r + 1) // 2, L),
            whole((devices, 2, L)),
        ],
        out_shape=[
            resident((r + 1, scan_count, wide), f32),
            jax.ShapeDtypeStruct(((r + 1) // 2, scan_count, L), bf16),
            jax.ShapeDtypeStruct((devices, 2, L), f32),
        ],
        scratch_shapes=[pltpu.VMEM((r + 3, S, L), bf16), pltpu.VMEM((8, L), f32)],
        compiler_params=params_of(),
        cost_estimate=cost(12),
        name="hidden_gradient",
    )(ds, left, right, n1, np2, w)


def back_one_kernel(
    flags, dp_ref, edge_ref, n1_ref, x_ref, bits_ref, st_ref, sum_ref, np_ref, kg2_ref, ds, kg_ref,
    xm, grad, flat, *, count,
):
    step, steps = (pl.program_id(0), pl.num_programs(0))
    dp_ref, n1_ref = (part_of(a, step) for a in (dp_ref, n1_ref))
    r, tiles = (n1_ref.shape[0] - 1, n1_ref.shape[2] // L - 1)
    cells = 2.0 * count * st_ref.shape[0]
    _mean, inv = stats_of(st_ref, count)
    shift_sum, gain_sum = sums_of(sum_ref)
    gain = np_ref[0:1] * inv
    c_n = -gain * gain_sum / cells
    c_0 = -gain * shift_sum / cells
    gain = 0.5 * gain
    f_down, f_right = (flags[1].astype(f32), flags[3].astype(f32))
    packed = edge_ref.shape[0]
    low = low_half()
    right = jnp.where(low, 1.0, f_right)

    @pl.when(step == 0)
    def _():
        grad[...] = jnp.zeros_like(grad)

    def line(i, t):
        d = pair(dp_ref, i, t)
        if t == tiles:
            beyond = edge_ref[i % packed].astype(f32)
            d = jnp.where(low, d, swap(beyond) if i >= packed else beyond)
        d = d * gain + (pair(n1_ref, i, t).astype(f32) * c_n + c_0)
        if t == tiles:
            d = d * right
        if i == r:
            d = d * f_down
        ds[i, :, t * L : (t + 1) * L] = d.astype(bf16)

    turned = (((0,), (0,)), ((), ()))
    totals = [None, None, None]
    done = 0
    for t in range(tiles):
        while done < t + 2:
            for i in range(r + 1):
                line(i, done)
            done += 1
        for k in (2 * t, 2 * t + 1):
            for g in range(bits_ref.shape[0]):
                word = bits_ref[g, :, k * L : (k + 1) * L]
                for row in range(g * BITS, min(2 * r, (g + 1) * BITS)):
                    x = live(word, row, pair(x_ref, row, k))
                    xm[row % 2, row // 2, :, k * L : (k + 1) * L] = x
        lanes = slice(t * L, (t + 2) * L)
        xl = slice(2 * t * L, 2 * (t + 1) * L)
        rows = [ds[a : a + r, :, lanes].reshape(r * S, 2 * L) for a in range(2)]
        xe, xo = (xm[a, :, :, xl].reshape(r * S, 2 * L) for a in range(2))
        for k, (a, b) in enumerate(((xe, rows[0]), (xo, rows[0]), (xo, rows[1]))):
            part = lax.dot_general(a, b, turned, preferred_element_type=f32)
            totals[k] = part if totals[k] is None else totals[k] + part
    for k in range(3):
        grad[k] += totals[k]

    @pl.when(step == steps - 1)
    def _():
        blocks = []
        for p in range(3):
            g = (2, 0, 1)[p]
            for q in range(3):
                block = None
                for v in range(1, 4):
                    u = q - 3 + 2 * v
                    if 0 <= u < 4:
                        part = grad[g, u * C : (u + 1) * C, v * C : (v + 1) * C]
                        block = part if block is None else block + part
                blocks.append(jnp.transpose(block))
        blocks += [kg2_ref[8]] + [kg2_ref[k] for k in range(8)]
        for a in range(9):
            flat[a * C : (a + 1) * C] = jnp.concatenate(blocks[2 * a : 2 * a + 2], axis=1)
        if flat.shape[0] > 9 * C:
            flat[9 * C :] = jnp.zeros((flat.shape[0] - 9 * C, L), f32)
        devices, share, _lanes = kg_ref.shape
        for k in range(devices):
            kg_ref[k] = flat[k * share : (k + 1) * share].astype(bf16)


def back_one(flags, dp, edge, n1, x, bits, st, sums, np2, kg2, count):
    rows, scan_count, lanes = x.shape
    r, tiles = (rows // 2, lanes // L // 2)
    devices = st.shape[0]
    share = 8 * -(-9 * C // (8 * devices))
    wide = (tiles + 1) * L
    return pl.pallas_call(
        functools.partial(back_one_kernel, count=count),
        grid=(scan_count // S,),
        in_specs=[
            pl.BlockSpec(memory_space=pltpu.SMEM),
            held,
            scans(edge.shape[0], L),
            held,
            scans(rows, lanes),
            scans(bits.shape[0], lanes),
            whole(st.shape),
            whole(sums.shape),
            whole(np2.shape),
            whole(kg2.shape),
        ],
        out_specs=[scans(r + 1, wide), whole((devices, share, L))],
        out_shape=[
            pltpu.HBM((r + 1, scan_count, wide), bf16),
            jax.ShapeDtypeStruct((devices, share, L), bf16),
        ],
        scratch_shapes=[
            pltpu.VMEM((2, r, S, lanes), bf16),
            pltpu.VMEM((3, 4 * C, 4 * C), f32),
            pltpu.VMEM((devices * share, L), f32),
        ],
        compiler_params=params_of(),
        cost_estimate=cost(16),
        name="back_one",
    )(flags, dp, edge, n1, hbm(x), hbm(bits), st, sums, np2, kg2)


def input_grad_kernel(ds, bits_ref, w_ref, *rest):
    ig_ref = rest[-1]
    r, tiles = (ds.shape[0] - 1, ds.shape[2] // L - 1)
    for t in range(tiles):
        lanes = slice(t * L, (t + 2) * L)
        rows = [ds[a : a + r, :, lanes].reshape(r * S, 2 * L) for a in range(2)]
        even = jnp.dot(rows[0], w_ref[: 4 * C], preferred_element_type=f32)
        odd = jnp.dot(
            jnp.concatenate(rows, axis=1), w_ref[4 * C :], preferred_element_type=f32
        )
        for k, block in enumerate((even, odd)):
            block = block.reshape(r, S, 2 * L)
            for h in range(2):
                xl = slice((2 * t + h) * L, (2 * t + h + 1) * L)
                for i in range(r):
                    row = 2 * i + k
                    d = block[i, :, h * L : (h + 1) * L].astype(bf16)
                    ig_ref[row, :, xl] = live(bits_ref[row // BITS, :, xl], row, d)


def input_gradient(d, bits, w, part, before):
    r, scan_count, wide = d.shape
    rows, lanes = (2 * (r - 1), 2 * (wide - L))
    steps = scan_count // S // 2
    at = lambda n, m: pl.BlockSpec((n, S, m), lambda g: (0, g + part * steps, 0))
    earlier = () if before is None else (before,)
    return pl.pallas_call(
        input_grad_kernel,
        grid=(steps,),
        in_specs=[at(r, wide), at(bits.shape[0], lanes), whole(w.shape)]
        + [pl.BlockSpec(memory_space=pl.ANY)] * len(earlier),
        out_specs=at(rows, lanes),
        out_shape=jax.ShapeDtypeStruct((rows, scan_count, lanes), bf16),
        input_output_aliases={3: 0} if earlier else {},
        compiler_params=params_of(),
        cost_estimate=cost(7),
        name="input_gradient",
    )(hbm(d), hbm(bits), w, *earlier)


def share_kernel(g_ref, out_ref):
    devices = g_ref.shape[0]
    total = g_ref[0].astype(f32)
    for k in range(1, devices):
        total = total + g_ref[k].astype(f32)
    total = total.astype(bf16)
    for k in range(devices):
        out_ref[k] = total


def sum_share(grads):
    return pl.pallas_call(
        share_kernel,
        in_specs=[held],
        out_specs=held,
        out_shape=jax.ShapeDtypeStruct(grads.shape, bf16),
        compiler_params=pltpu.CompilerParams(vmem_limit_bytes=8 << 20),
        cost_estimate=cost(1),
        name="sum_share",
    )(grads)


def adam_step(weight_now, gradient, moment_one, moment_two, step_rate, decay_rate):
    first_new = adam_beta * moment_one + (1.0 - adam_beta) * gradient
    second_new = adam_beta * moment_two + (1.0 - adam_beta) * gradient * gradient
    correction = 1.0 - adam_beta**step_count
    update = first_new / correction / (jnp.sqrt(second_new / correction) + adam_eps)
    return (weight_now - step_rate * (update + decay_rate * weight_now), first_new, second_new)


def update_kernel(
    g_ref, s1_ref, s2_ref, k_ref, km_ref, kv_ref, n_ref, nm_ref, nv_ref, gn_ref, ok_ref, okm_ref,
    okv_ref, olow_ref, on_ref, onm_ref, onv_ref, flat,
):
    devices, share, _lanes = g_ref.shape
    for k in range(devices):
        flat[k * share : (k + 1) * share] = g_ref[k].astype(f32)
    norm_rows = []
    for ref in (s1_ref, s2_ref):
        shift_sum, gain_sum = sums_of(ref)
        norm_rows += [gain_sum[:, :C], shift_sum[:, :C]]
    g_norm = jnp.concatenate(norm_rows, axis=0)
    squares = jnp.sum(jnp.sum(flat[: 9 * C] ** 2, axis=0, keepdims=True), axis=1, keepdims=True)
    squares = squares + jnp.sum(
        jnp.sum(g_norm * g_norm, axis=0, keepdims=True), axis=1, keepdims=True
    )
    norm = jnp.sqrt(squares)
    gn_ref[...] = norm
    factor = jnp.minimum(1.0, clip_limit / norm)
    on, onm, onv = adam_step(
        n_ref[...], g_norm * factor, nm_ref[...], nv_ref[...], norm_rate, 0.0
    )
    on_ref[...] = on
    onm_ref[...] = onm
    onv_ref[...] = onv
    for layer in range(2):
        for a in range(5):
            width = L if a < 4 else C
            at = slice(a * L, a * L + width)
            if a == 4:
                g = flat[4 * C : 5 * C, layer * C : (layer + 1) * C]
            else:
                first = (a + 5 * layer) * C
                g = flat[first : first + C, :]
            k, km, kv = adam_step(
                k_ref[layer, :, at], g * factor, km_ref[layer, :, at], kv_ref[layer, :, at],
                kernel_rate, kernel_decay,
            )
            ok_ref[layer, :, at] = k
            okm_ref[layer, :, at] = km
            okv_ref[layer, :, at] = kv
            olow_ref[layer, :, at] = k.astype(bf16)


def update(grads, sums1, sums2, kt, kmt, kvt, norm_params, norm_m, norm_v):
    flat = lambda a: a.reshape(4, C)
    big = jax.ShapeDtypeStruct(kt.shape, f32)
    small = jax.ShapeDtypeStruct((4, C), f32)
    outs = [
        jax.ShapeDtypeStruct((1, 1), f32), big, big, big,
        jax.ShapeDtypeStruct(kt.shape, bf16), small, small, small,
    ]
    args = [grads, sums1, sums2, kt, kmt, kvt, flat(norm_params), flat(norm_m), flat(norm_v)]
    return pl.pallas_call(
        update_kernel,
        grid=(1,),
        in_specs=[whole(a.shape) for a in args],
        out_specs=[whole(o.shape) for o in outs],
        out_shape=outs,
        scratch_shapes=[pltpu.VMEM((grads.shape[0] * grads.shape[1], L), f32)],
        compiler_params=params_of(),
        cost_estimate=cost(3),
        name="update",
    )(*args)


def shifted(block, axis, distance):
    devices = range(lax.axis_size(axis))
    route = [(i - distance, i) for i in devices if i - distance in devices]
    return lax.ppermute(block, axis, route)


def exchange(rows):
    return lax.all_to_all(rows, BOTH, 0, 0, tiled=True)


def per_device(
    scan_features, occupancy, kernels, kernel_m, kernel_v, norm_params, norm_m, norm_v, cotangent
):
    x = jnp.transpose(scan_features, (1, 0, 2))
    cot = jnp.transpose(cotangent, (1, 0, 2))
    occ = jnp.transpose(occupancy, (2, 0, 1))
    kt, kmt, kvt = (jnp.transpose(a, (0, 2, 1)) for a in (kernels, kernel_m, kernel_v))
    gy, gx = (lax.axis_size("gy"), lax.axis_size("gx"))
    devices = gy * gx
    y, z = (lax.axis_index("gy"), lax.axis_index("gx"))
    flags = jnp.stack([y > 0, y < gy - 1, z > 0, z < gx - 1]).astype(jnp.int32)
    rows, scan_count, lanes = x.shape
    r, tiles = (rows // 2, lanes // L // 2)
    count = float(scan_count * r * tiles)
    last = (tiles - 1) * L

    down, cot_down, corner, xcol = edges(x, occ, cot)
    xcol = shifted(xcol, "gx", 1)
    down = shifted(down, "gy", 1)
    cot_down = shifted(cot_down, "gy", -1)
    corner = lax.ppermute(
        corner, BOTH, [(i, i + gx + 1) for i in range(devices - gx) if (i + 1) % gx]
    )
    bits, w1, w2, w2b, w1b, np2 = prepare(occ, kt, norm_params)

    xcol, cot_down, flags = lax.optimization_barrier((xcol, cot_down, flags))
    ends, st1, going_right, going_left, edge = first_last(x, bits, down, xcol, corner, w1)
    left_in = shifted(going_right, "gx", 1)
    right_in = shifted(going_left, "gx", -1)
    c1, st1, up, low_rows = conv_one(x, bits, down, st1, w1, devices)
    up, low_rows = pack_rows(up, low_rows, edge, left_in, right_in)
    down_in = shifted(up, "gy", -1)
    up_in = shifted(low_rows, "gy", 1)
    st1 = exchange(st1)

    c2, n1, hid, st2 = conv_two(
        flags, c1, ends, up_in, down_in, left_in, right_in, st1, np2, w2, count
    )
    st2 = exchange(st2)
    features, d2, sums2 = output(c2, st2, np2, cot, down, cot_down, count)
    sums2 = exchange(sums2)
    going_right, going_left = rim_two(flags, d2, c2, st2, sums2, np2, count)
    left_in = shifted(going_right, "gx", 1)
    right_in = shifted(going_left, "gx", -1)
    ds, kg2 = back_two(flags, d2, c2, hid, st2, sums2, np2, count)
    d1, edge, sums1 = hidden_gradient(ds, left_in, right_in, n1, np2, w2b, devices)
    edge = shifted(edge, "gx", -1)
    sums1 = exchange(sums1)
    d1, grads = back_one(flags, d1, edge, n1, x, bits, st1, sums1, np2, kg2, count)
    grads = exchange(grads)
    input_grad = input_gradient(d1, bits, w1b, 0, None)
    grads, input_grad = lax.optimization_barrier((sum_share(grads), input_grad))
    grads = exchange(grads)
    input_grad = input_gradient(d1, bits, w1b, 1, input_grad)
    norm, k, km, kv, low, n, nm, nv = update(
        grads, sums1, sums2, kt, kmt, kvt, norm_params, norm_m, norm_v
    )
    back = lambda a: jnp.transpose(a, (0, 2, 1))
    deep = lambda a: a.reshape(norm_params.shape)
    return (
        jnp.transpose(features, (1, 0, 2)),
        jnp.transpose(input_grad, (1, 0, 2)),
        norm.reshape(()),
        back(k),
        back(km),
        back(kv),
        back(low),
        deep(n),
        deep(nm),
        deep(nv),
    )


def solution(mesh):
    split = P(None, "gy", "gx")
    return jax.shard_map(
        per_device,
        mesh=mesh,
        in_specs=(split, split) + (P(),) * 6 + (split,),
        out_specs=(split, split) + (P(),) * 8,
        check_vma=False,
    )
```

```python
import functools
import math

import jax
import jax.numpy as jnp
from jax import lax
from jax.experimental import pallas as pl
from jax.experimental.pallas import tpu as pltpu
from jax.sharding import PartitionSpec as P

norm_eps = 1e-05
adam_beta = 0.5
adam_eps = 1e-08
step_count = 5
clip_limit = 1.0
kernel_rate = 0.04
norm_rate = 0.25
kernel_decay = 0.01

f32, bf16 = (jnp.float32, jnp.bfloat16)
BOTH = ("gy", "gx")
S, S2, C, L, BITS = (16, 32, 64, 128, 13)


def params_of(limit=20):
    return pltpu.CompilerParams(
        dimension_semantics=("arbitrary",), vmem_limit_bytes=limit << 20
    )


def cost(microseconds):
    return pl.CostEstimate(
        flops=0, bytes_accessed=int(microseconds * 3.6e6), transcendentals=0
    )


def whole(shape):
    return pl.BlockSpec(shape, lambda g: (0,) * len(shape))


def scans(rows, lanes, n=S):
    return pl.BlockSpec((rows, n, lanes), lambda g: (0, g, 0))


def more(rows, lanes):
    return scans(rows, lanes, S2)


def resident(shape, dtype):
    return pltpu.VMEM(shape, dtype)


held = pl.BlockSpec(memory_space=pltpu.VMEM)


def vmem(array):
    return pltpu.with_memory_space_constraint(array, pltpu.VMEM)


def hbm(array):
    return pltpu.with_memory_space_constraint(array, pltpu.HBM)


def inside():
    flags = []
    for axis in BOTH:
        at = lax.axis_index(axis)
        flags += [at > 0, at < lax.axis_size(axis) - 1]
    return [jnp.where(flag, 1.0, 0.0) for flag in flags]


def part_of(ref, step, n=S):
    return ref.at[:, pl.ds(pl.multiple_of(step * n, n), n), :]


def low_half(rows=S):
    return lax.broadcasted_iota(jnp.int32, (rows, L), 1) < C


def swap(x):
    return pltpu.roll(x, C, 1)


def fold(x):
    x = jnp.broadcast_to(x, (8, L))
    return (x + swap(x))[:1]


def live(word, row, x):
    bit = 1 << (row % BITS)
    if x.dtype == bf16:
        return jnp.where((word & jnp.int16(bit)) != 0, x, jnp.zeros_like(x))
    return jnp.where((word.astype(jnp.int32) & bit) != 0, x, 0.0)


def pair(ref, row, t):
    return ref[row, :, t * L : (t + 1) * L]


def stats_of(st_ref, count):
    groups = 2 * st_ref.shape[0]
    means = st_ref[:, 0, :]
    mean = fold(jnp.sum(means, axis=0, keepdims=True)) / groups
    spread = st_ref[:, 1, :] + count * (means - mean) ** 2
    spread = fold(jnp.sum(spread, axis=0, keepdims=True)) / (groups * count)
    return (mean, lax.rsqrt(spread + norm_eps))


def sums_of(st_ref):
    return tuple(fold(jnp.sum(st_ref[:, k, :], axis=0, keepdims=True)) for k in range(2))


def pilot_of(block):
    flat = block.reshape(-1, L)
    return jnp.sum(flat, axis=0, keepdims=True) / flat.shape[0]


def finish_stats(step, steps, pilot, sums, count, run_ref, st_ref):
    off, squares = (jnp.sum(s, axis=0, keepdims=True) for s in sums)
    mean = pilot + off / count
    squares = squares - off * off / count

    @pl.when(step == 0)
    def _():
        run_ref[0:1] = mean
        run_ref[1:2] = squares

    @pl.when(step > 0)
    def _():
        before = step.astype(f32)
        share = 1.0 / (before + 1.0)
        delta = mean - run_ref[0:1]
        run_ref[0:1] = run_ref[0:1] + delta * share
        run_ref[1:2] = run_ref[1:2] + squares + delta * delta * (count * before * share)

    @pl.when(step == steps - 1)
    def _():
        st_ref[...] = jnp.broadcast_to(run_ref[0:2][None], st_ref.shape)


def off_sums(blocks, pilot):
    sums = [jnp.zeros((8, L), f32), jnp.zeros((8, L), f32)]
    for block in blocks:
        d = block - pilot
        sums = [sums[0] + halves(d), sums[1] + halves(d * d)]
    return sums


def added(a, b):
    return b if a is None else [x + y for x, y in zip(a, b)]


def rim_of(first, second, row, low):
    half = first.shape[0]
    if row < half:
        return jnp.where(low, first[row].astype(f32), second[row].astype(f32))
    row = row - half
    return swap(jnp.where(low, second[row].astype(f32), first[row].astype(f32)))


def halves(x):
    total = x[:8]
    for k in range(8, x.shape[0], 8):
        total = total + x[k : k + 8]
    return total


def occupancy_words(occ, groups, first):
    rows = occ.shape[1]
    shape = (rows, groups * L)
    group_of = lax.broadcasted_iota(jnp.int32, shape, 1) // L + first
    inner = lax.broadcasted_iota(jnp.int32, shape, 0) - group_of * BITS
    power = jnp.where(
        (inner >= 0) & (inner < BITS), (1 << jnp.clip(inner, 0, BITS)), 0
    ).astype(bf16)
    low = occ.astype(f32).astype(bf16)
    return jnp.dot(low, power, preferred_element_type=f32).astype(jnp.int32)


def edges_kernel(
    row_ref, col_ref, occ_ref, cot_last_ref, cot_first_ref, down_ref, up_ref, corner_ref, xcol_ref
):
    cols, scan_count, rows = occ_ref.shape
    lanes = row_ref.shape[2]
    groups = -(-rows // BITS)
    low = low_half(scan_count)
    words = occupancy_words(occ_ref[...].reshape(cols * scan_count, rows), 1, groups - 1)
    words = words.reshape(cols // 2, 2, scan_count, L)
    for t in range(cols // 2):
        word = jnp.where(low, words[t, 0], words[t, 1])
        x = live(word, rows - 1, row_ref[0, :, t * L : (t + 1) * L].astype(f32)).astype(bf16)
        down_ref[:, t * L : (t + 1) * L] = x
    corner_ref[...] = x
    down_ref[:, lanes:] = cot_last_ref[0]
    up_ref[...] = cot_first_ref[...]
    words = occupancy_words(occ_ref[cols - 1], groups, 0)
    for i in range(rows // 2):
        even, odd = (
            live(
                words[:, row // BITS * L : (row // BITS + 1) * L], row, col_ref[row].astype(f32)
            )
            for row in (2 * i, 2 * i + 1)
        )
        xcol_ref[i] = jnp.where(low, swap(even), odd).astype(bf16)


def edges(x, occ, cot):
    rows, scan_count, lanes = x.shape
    r, wide = (rows // 2, lanes // 2)
    outs = [
        jax.ShapeDtypeStruct((scan_count, lanes + wide), bf16),
        jax.ShapeDtypeStruct((2, scan_count, wide), bf16),
        jax.ShapeDtypeStruct((scan_count, L), bf16),
        jax.ShapeDtypeStruct((r, scan_count, L), bf16),
    ]
    return pl.pallas_call(
        edges_kernel,
        grid=(1,),
        in_specs=[
            pl.BlockSpec((1, scan_count, lanes), lambda g: (rows - 1, 0, 0)),
            pl.BlockSpec((rows, scan_count, L), lambda g: (0, 0, lanes // L - 1)),
            whole(occ.shape),
            pl.BlockSpec((1, scan_count, wide), lambda g: (r - 1, 0, 0)),
            pl.BlockSpec((2, scan_count, wide), lambda g: (0, 0, 0)),
        ],
        out_specs=[whole(o.shape) for o in outs],
        out_shape=outs,
        compiler_params=params_of(),
        cost_estimate=cost(3),
        name="edges",
    )(hbm(x), hbm(x), hbm(occ), hbm(cot), hbm(cot))


def prep_kernel(occ_ref, kt_ref, np_ref, bits_ref, w1_ref, w2_ref, w2b_ref, w1b_ref, np2_ref):
    cols, scan_count, rows = occ_ref.shape
    groups = bits_ref.shape[0]
    words = occupancy_words(occ_ref[...].reshape(cols * scan_count, rows), groups, 0)
    words = words.reshape(cols // 2, 2, scan_count, groups * L)
    low = low_half(scan_count)
    for g in range(groups):
        for t in range(cols // 2):
            lanes = slice(g * L, (g + 1) * L)
            word = jnp.where(low, words[t, 0, :, lanes], words[t, 1, :, lanes])
            bits_ref[g, :, t * L : (t + 1) * L] = word.astype(jnp.int16)
    back = [[kt_ref[l, :, k * C : (k + 1) * C] for k in range(9)] for l in range(2)]
    fore = [[jnp.transpose(b) for b in layer] for layer in back]
    none = jnp.zeros((C, C), f32)

    def put(ref, rows_of, cols_of, pick):
        for a in range(rows_of):
            blocks = [pick(a, b) for b in range(cols_of)]
            for k in range(0, cols_of, 2):
                two = jnp.concatenate(blocks[k : k + 2], axis=1).astype(bf16)
                ref[a * C : (a + 1) * C, k * C : (k + 2) * C] = two

    def tap(table, p, q):
        return table[3 * p + q] if 0 <= p < 3 and 0 <= q < 3 else none

    put(w1_ref, 30, 4, lambda a, b: tap(fore[0], a // 6 - 2 * (b // 2), a % 6 - 2 * (b % 2) - 1))
    put(w2_ref, 16, 4, lambda a, b: tap(fore[1], a // 4 - b // 2, a % 4 - b % 2))
    put(w2b_ref, 16, 4, lambda a, b: tap(back[1], b // 2 + 2 - a // 4, b % 2 + 2 - a % 4))
    put(w1b_ref, 12, 4, lambda a, b: tap(back[0], (1, 2, 0)[a // 4], b + 3 - 2 * (a % 4)))
    np2_ref[...] = jnp.concatenate([np_ref[...], np_ref[...]], axis=1)


def prepare(occ, kt, norm_params):
    cols, scan_count, rows = occ.shape
    full = lambda *shape: jax.ShapeDtypeStruct(shape, bf16)
    outs = [
        jax.ShapeDtypeStruct((-(-rows // BITS), scan_count, cols * C), jnp.int16),
        full(30 * C, 4 * C),
        full(16 * C, 4 * C),
        full(16 * C, 4 * C),
        full(12 * C, 4 * C),
        jax.ShapeDtypeStruct((4, L), f32),
    ]
    return pl.pallas_call(
        prep_kernel,
        grid=(1,),
        in_specs=[whole(occ.shape), whole(kt.shape), whole((4, C))],
        out_specs=[whole(o.shape) for o in outs],
        out_shape=outs,
        compiler_params=params_of(),
        cost_estimate=cost(4),
        name="prepare",
    )(hbm(occ), kt, norm_params.reshape(4, C))


def mask_tile(x_ref, bits_ref, t, xs, into):
    rows = x_ref.shape[0]
    for g in range(bits_ref.shape[0]):
        word = bits_ref[g, :, t * L : (t + 1) * L]
        for row in range(g * BITS, min(rows, (g + 1) * BITS)):
            x = live(word, row, pair(x_ref, row, t))
            xs[(row + 1) // 4, (row + 1) % 4, :, into * L : (into + 1) * L] = x


def clear_rows(rows, pairs, xs):
    for k in range(rows + 1, 4 * pairs + 1):
        xs[k // 4, k % 4] = jnp.zeros_like(xs[0, 0])


def conv_rows(xs, lanes, w, r, before=()):
    pairs = (r + 1) // 2
    pieces = [xs[0:pairs, q, :, lanes] for q in range(4)] + [xs[1 : pairs + 1, 0, :, lanes]]
    pieces = [p.reshape(pairs * S, p.shape[2]) for p in pieces]
    lhs = jnp.concatenate(list(before) + pieces, axis=1)
    acc = jnp.dot(lhs, w, preferred_element_type=f32).reshape(pairs, S, 2 * L)
    return [acc[i // 2, :, (i % 2) * L : (i % 2 + 1) * L] for i in range(r)]


def first_last_kernel(
    x_ref, bits_ref, xrow_ref, xcol_ref, corner_ref, w_ref, c_ref, st_ref, er_ref, el_ref,
    edge_ref, xs, run,
):
    step, steps = (pl.program_id(0), pl.num_programs(0))
    c_ref, x_ref, bits_ref = (part_of(a, step) for a in (c_ref, x_ref, bits_ref))
    rows, lanes = (x_ref.shape[0], x_ref.shape[2])
    r = rows // 2
    low = low_half()

    @pl.when(step == 0)
    def _():
        clear_rows(rows, (r + 1) // 2, xs)

    xs[0, 0, :, :L] = xrow_ref[:, :L]
    xs[0, 0, :, L:] = xrow_ref[:, lanes - 2 * L : lanes]
    mask_tile(x_ref, bits_ref, 0, xs, 0)
    mask_tile(x_ref, bits_ref, lanes // L - 2, xs, 1)
    mask_tile(x_ref, bits_ref, lanes // L - 1, xs, 2)
    wide = 3 * L
    rows_of = lambda q, a, b: w_ref[q * wide + a * C : q * wide + b * C]
    w = jnp.concatenate([rows_of(q, 0, 4) for q in range(5)], axis=0)
    last = conv_rows(xs, slice(L, 3 * L), w, r)
    pairs = (r + 1) // 2
    none = jnp.zeros((S, L), bf16)
    beside = [corner_ref[...]] + [xcol_ref[i] for i in range(r)] + [none]
    w = [jnp.zeros((C, 2 * L), bf16)] + [rows_of(q, 3, 4) for q in range(5)]
    w = jnp.concatenate(w + [rows_of(q, 4, 6) for q in range(5)], axis=0)
    more_lhs = [
        jnp.concatenate([beside[2 * m + k] for m in range(pairs)], axis=0) for k in range(3)
    ]
    first = conv_rows(xs, slice(0, L), w, r, more_lhs)
    edge = [jnp.where(low, b, a) for a, b in zip(first, last)]
    pilot = pilot_of(jnp.concatenate(edge[: r // 2], axis=0))
    for i in range(r):
        c_ref[i, :, :L] = first[i]
        c_ref[i, :, L:] = last[i]
        edge_ref[i] = edge[i].astype(bf16)
    finish_stats(step, steps, pilot, off_sums(edge, pilot), float(r * S), run, st_ref)
    half = er_ref.shape[0]
    for k in range(half):
        far = swap(edge[k + half]) if k + half < r else jnp.zeros((S, L), f32)
        er_ref[k] = jnp.where(low, edge[k], far).astype(bf16)
        el_ref[k] = jnp.where(low, far, edge[k]).astype(bf16)


def first_last(x, bits, down, xcol, corner, w):
    rows, scan_count, lanes = x.shape
    r = rows // 2
    shape = lambda dtype, *s: jax.ShapeDtypeStruct(s, dtype)
    return pl.pallas_call(
        first_last_kernel,
        grid=(scan_count // S,),
        in_specs=[
            held,
            held,
            pl.BlockSpec((S, down.shape[1]), lambda g: (g, 0)),
            scans(r, L),
            pl.BlockSpec((S, L), lambda g: (g, 0)),
            whole(w.shape),
        ],
        out_specs=[
            held,
            whole((1, 2, L)),
            scans((r + 1) // 2, L),
            scans((r + 1) // 2, L),
            scans(r, L),
        ],
        out_shape=[
            resident((r, scan_count, 2 * L), f32),
            shape(f32, 1, 2, L),
            shape(bf16, (r + 1) // 2, scan_count, L),
            shape(bf16, (r + 1) // 2, scan_count, L),
            shape(bf16, r, scan_count, L),
        ],
        scratch_shapes=[
            pltpu.VMEM(((r + 1) // 2 + 1, 4, S, 3 * L), bf16),
            pltpu.VMEM((8, L), f32),
        ],
        compiler_params=params_of(),
        cost_estimate=cost(4),
        name="conv_one_ends",
    )(vmem(x), vmem(bits), down, xcol, corner, w)


def conv_one_kernel(
    x_ref, bits_ref, xrow_ref, ends_ref, w_ref, c_ref, st_ref, up_ref, down_ref, xs, run
):
    step, steps = (pl.program_id(0), pl.num_programs(0))
    c_ref, x_ref, bits_ref = (part_of(a, step) for a in (c_ref, x_ref, bits_ref))
    rows, tiles = (x_ref.shape[0], x_ref.shape[2] // L)
    r, inner = (rows // 2, tiles // 2 - 1)

    @pl.when(step == 0)
    def _():
        clear_rows(rows, (r + 1) // 2, xs)

    xs[0, 0] = xrow_ref[:, : tiles * L]
    sums, pilot = (None, None)
    filled = 0
    for t in range(inner):
        while filled < 2 * t + 3:
            mask_tile(x_ref, bits_ref, filled, xs, filled)
            filled += 1
        blocks = conv_rows(xs, slice(2 * t * L, (2 * t + 3) * L), w_ref[...], r)
        if pilot is None:
            pilot = pilot_of(jnp.concatenate(blocks[: r // 2], axis=0))
        sums = added(sums, off_sums(blocks, pilot))
        for i, block in enumerate(blocks):
            c_ref[i, :, t * L : (t + 1) * L] = block
    finish_stats(step, steps, pilot, sums, float(r * inner * S), run, st_ref)
    up_ref[...] = c_ref[0:3].astype(bf16)
    down_ref[...] = c_ref[r - 2 : r].astype(bf16)

    @pl.when(step == steps - 1)
    def _():
        own, more = (float(r * S) * steps * n for n in (inner, 1))
        delta = ends_ref[0, 0:1] - run[0:1]
        mean = run[0:1] + delta * (more / (own + more))
        squares = run[1:2] + ends_ref[0, 1:2] + delta * delta * (own * more / (own + more))
        row = jnp.concatenate([mean, squares], axis=0)
        st_ref[...] = jnp.broadcast_to(row[None], st_ref.shape)


def conv_one(x, bits, down, ends, w, devices):
    rows, scan_count, lanes = x.shape
    r, wide = (rows // 2, lanes // 2 - L)
    shape = lambda dtype, *s: jax.ShapeDtypeStruct(s, dtype)
    return pl.pallas_call(
        conv_one_kernel,
        grid=(scan_count // S,),
        in_specs=[
            held,
            held,
            pl.BlockSpec((S, down.shape[1]), lambda g: (g, 0)),
            whole(ends.shape),
            whole(w.shape),
        ],
        out_specs=[held, whole((devices, 2, L)), scans(3, wide), scans(2, wide)],
        out_shape=[
            resident((r, scan_count, wide), f32),
            shape(f32, devices, 2, L),
            shape(bf16, 3, scan_count, wide),
            shape(bf16, 2, scan_count, wide),
        ],
        scratch_shapes=[
            pltpu.VMEM(((r + 1) // 2 + 1, 4, S, lanes), bf16),
            pltpu.VMEM((8, L), f32),
        ],
        compiler_params=params_of(),
        cost_estimate=cost(11),
        name="conv_one",
    )(vmem(x), vmem(bits), down, ends, w)


def pack_kernel(up_ref, down_ref, edge_ref, left_ref, right_ref, up_out, down_out):
    r, wide = (edge_ref.shape[0], up_ref.shape[2])
    low = low_half()
    for src, out, first in ((up_ref, up_out, 0), (down_ref, down_out, r - 2)):
        out[:, :, :wide] = src[...]
        for k in range(src.shape[0]):
            out[k, :, wide : wide + L] = edge_ref[first + k]
            out[k, :, wide + L :] = rim_of(left_ref, right_ref, first + k, low).astype(bf16)


def pack_rows(up, down, edge, left, right):
    r, scan_count, _lanes = edge.shape
    wide = up.shape[2]
    return pl.pallas_call(
        pack_kernel,
        grid=(scan_count // S,),
        in_specs=[
            scans(3, wide), scans(2, wide), scans(r, L), scans(left.shape[0], L),
            scans(right.shape[0], L),
        ],
        out_specs=[scans(3, wide + 2 * L), scans(2, wide + 2 * L)],
        out_shape=[
            jax.ShapeDtypeStruct((n, scan_count, wide + 2 * L), bf16) for n in (3, 2)
        ],
        compiler_params=params_of(),
        cost_estimate=cost(1),
        name="pack_rows",
    )(up, down, edge, left, right)


def conv_two_kernel(
    c_ref, ends_ref, up_ref, down_ref, left_ref, right_ref, st_ref, np_ref, w_ref, c2_ref,
    n1_ref, hid_ref, st2_ref, rim, run, *, count,
):
    step, steps = (pl.program_id(0), pl.num_programs(0))
    c_ref, ends_ref, c2_ref, n1_ref = (
        part_of(a, step, S2) for a in (c_ref, ends_ref, c2_ref, n1_ref)
    )
    r, tiles = (c_ref.shape[0], c_ref.shape[2] // L + 2)
    t_out = tiles - 1
    mean, inv = stats_of(st_ref, count)
    offset = -mean * inv
    scale = 0.5 * np_ref[0:1] * inv
    shift = 0.5 * (np_ref[0:1] * offset + np_ref[1:2])
    f_up, f_down, f_left, f_right = inside()
    low = low_half(S2)
    left = jnp.where(low, f_left, 1.0)
    right = jnp.where(low, 1.0, f_right)
    for row in range(r):
        rim[row] = rim_of(left_ref, right_ref, row, low)

    def act(row, t):
        at_end = t in (0, tiles - 1)
        if 2 <= row < r + 2:
            flag = None
            c = pair(ends_ref, row - 2, min(t, 1)) if at_end else pair(c_ref, row - 2, t - 1)
            beyond = rim[row - 2] if at_end else None
        else:
            src, k, flag = (up_ref, row, f_up) if row < 2 else (down_ref, row - r - 2, f_down)
            c = pair(src, k, tiles - 2 if at_end else t - 1).astype(f32)
            beyond = pair(src, k, tiles - 1).astype(f32) if at_end else None
        if t == 0:
            c = jnp.where(low, beyond, c)
        if t == tiles - 1:
            c = jnp.where(low, c, beyond)
        h = c * scale + shift
        out = h + h * jnp.tanh(h)
        if t == 0:
            out = out * left
        if t == tiles - 1:
            out = out * right
        if flag is not None:
            out = out * flag
        out = out.astype(bf16)
        hid_ref[row, :, t * L : (t + 1) * L] = out
        if 2 <= row < r + 3:
            n1_ref[row - 2, :, t * L : (t + 1) * L] = (c * inv + offset).astype(bf16)

    pairs = (r + 3) // 2
    sums, pilot = (None, None)
    for t in range(tiles):
        for row in range(r + 5):
            act(row, t)
        k = t - 1
        if k < 0:
            continue
        lanes = slice(k * L, (k + 2) * L)
        pieces = [
            jnp.concatenate([hid_ref[2 * m + a, :, lanes] for m in range(pairs)], axis=0)
            for a in range(4)
        ]
        lhs = jnp.concatenate(pieces, axis=1)
        acc = jnp.dot(lhs, w_ref[...], preferred_element_type=f32).reshape(pairs, S2, 2 * L)
        if pilot is None:
            pilot = pilot_of(acc[1 : r // 2, :, :L])
        blocks = []
        for row in range(r + 3):
            block = acc[row // 2, :, (row % 2) * L : (row % 2 + 1) * L]
            c2_ref[row, :, k * L : (k + 1) * L] = block
            if 0 < row <= r:
                blocks.append(block)
        sums = added(sums, off_sums(blocks, pilot))
    finish_stats(step, steps, pilot, sums, float(r * t_out * S2), run, st2_ref)


def conv_two(c1, ends, up, down, left, right, st, np2, w, count):
    r, scan_count, wide = c1.shape
    wide = wide + 2 * L
    lanes = wide - L
    devices = st.shape[0]
    return pl.pallas_call(
        functools.partial(conv_two_kernel, count=count),
        grid=(scan_count // S2,),
        in_specs=[
            held,
            held,
            more(2, wide),
            more(3, wide),
            more(left.shape[0], L),
            more(right.shape[0], L),
            whole(st.shape),
            whole(np2.shape),
            whole(w.shape),
        ],
        out_specs=[held, held, more(r + 5, wide), whole((devices, 2, L))],
        out_shape=[
            resident((r + 3, scan_count, lanes), f32),
            resident((r + 1, scan_count, wide), bf16),
            pltpu.HBM((r + 5, scan_count, wide), bf16),
            jax.ShapeDtypeStruct((devices, 2, L), f32),
        ],
        scratch_shapes=[
            pltpu.VMEM((r, S2, L), f32),
            pltpu.VMEM((8, L), f32),
        ],
        compiler_params=params_of(),
        cost_estimate=cost(14),
        name="conv_two",
    )(c1, ends, up, down, left, right, st, np2, w)


def output_kernel(
    c2_ref, st_ref, np_ref, cot_ref, up_ref, down_ref, feat_ref, d_ref, sum_ref, run, *, count,
):
    step, steps = (pl.program_id(0), pl.num_programs(0))
    c2_ref, d_ref, cot_ref = (part_of(a, step, S2) for a in (c2_ref, d_ref, cot_ref))
    r, tiles = (cot_ref.shape[0], cot_ref.shape[2] // L)
    mean, inv = stats_of(st_ref, count)
    offset = -mean * inv
    scale = 0.5 * np_ref[2:3] * inv
    shift = 0.5 * (np_ref[2:3] * offset + np_ref[3:4])
    above = 2 * tiles

    def slope(c, cot):
        h = c * scale + shift
        s = 1.0 + jnp.tanh(h)
        f = h * s
        return (f, cot.astype(f32) * (s + f * (2.0 - s)))

    sums = None
    for t in range(tiles):
        part = [jnp.zeros((8, L), f32), jnp.zeros((8, L), f32)]
        for i in range(r):
            c = pair(c2_ref, i + 1, t)
            f, d = slope(c, pair(cot_ref, i, t))
            feat_ref[i, :, t * L : (t + 1) * L] = f.astype(bf16)
            d_ref[i + 1, :, t * L : (t + 1) * L] = d
            part = [part[0] + halves(d), part[1] + halves(d * c)]
        sums = added(sums, part)
    for t in range(tiles):
        lanes = slice(t * L, (t + 1) * L)
        cot = up_ref[:, (above + t) * L : (above + t + 1) * L]
        d_ref[0, :, lanes] = slope(pair(c2_ref, 0, t), cot)[1]
        for k in range(2):
            row = r + 1 + k
            d_ref[row, :, lanes] = slope(pair(c2_ref, row, t), pair(down_ref, k, t))[1]
    sums = (0.5 * sums[0], (0.5 * inv) * (sums[1] - mean * sums[0]))
    add_sums(step, steps, sums, run, sum_ref)


def add_sums(step, steps, sums, run, sum_ref):
    rows = jnp.concatenate([jnp.sum(s, axis=0, keepdims=True) for s in sums], axis=0)

    @pl.when(step == 0)
    def _():
        run[0:2] = rows

    @pl.when(step > 0)
    def _():
        run[0:2] = run[0:2] + rows

    @pl.when(step == steps - 1)
    def _():
        sum_ref[...] = jnp.broadcast_to(run[0:2][None], sum_ref.shape)


def output(c2, st, np2, cot, up, down, count):
    r, scan_count, lanes = cot.shape
    devices = st.shape[0]
    return pl.pallas_call(
        functools.partial(output_kernel, count=count),
        grid=(scan_count // S2,),
        in_specs=[
            held,
            whole(st.shape),
            whole(np2.shape),
            held,
            pl.BlockSpec((S2, up.shape[1]), lambda g: (g, 0)),
            more(2, lanes),
        ],
        out_specs=[more(r, lanes), held, whole((devices, 2, L))],
        out_shape=[
            jax.ShapeDtypeStruct((r, scan_count, lanes), bf16),
            resident((r + 3, scan_count, lanes), f32),
            jax.ShapeDtypeStruct((devices, 2, L), f32),
        ],
        scratch_shapes=[pltpu.VMEM((8, L), f32)],
        compiler_params=params_of(),
        cost_estimate=cost(12),
        name="output",
    )(c2, st, np2, vmem(cot), up, down)


def norm_back_two(st_ref, sum_ref, np_ref, count, rows):
    cells = 2.0 * count * st_ref.shape[0]
    mean, inv = stats_of(st_ref, count)
    shift_sum, gain_sum = sums_of(sum_ref)
    gain = np_ref[2:3] * inv
    c_n = -gain * inv * gain_sum / cells
    c_0 = -gain * shift_sum / cells - c_n * mean
    gain = 0.5 * gain
    f_up, f_down = inside()[:2]

    def back(row, d, c):
        d = d * gain + (c * c_n + c_0)
        if isinstance(row, int):
            if row == 0:
                d = d * f_up
            if row > rows:
                d = d * f_down
        return d

    return back


def rim_two_kernel(
    d_ref, c_ref, st_ref, sum_ref, np_ref, er_ref, el_ref, *, count
):
    d_ref, c_ref = (part_of(a, pl.program_id(0), S2) for a in (d_ref, c_ref))
    rows, last = (d_ref.shape[0], d_ref.shape[2] // L - 1)
    back = norm_back_two(st_ref, sum_ref, np_ref, count, rows - 3)
    low = low_half(S2)
    half = rows // 2
    column = lambda row, t: back(row, pair(d_ref, row, t), pair(c_ref, row, t))
    both = lambda row: jnp.where(low, column(row, 0), column(row, last))
    for k in range(half):
        near, far = (both(k), swap(both(k + half)))
        el_ref[k] = jnp.where(low, near, far).astype(bf16)
        er_ref[k] = jnp.where(low, far, near).astype(bf16)


def rim_two(d, c2, st, sums, np2, count):
    rows, scan_count, lanes = d.shape
    return pl.pallas_call(
        functools.partial(rim_two_kernel, count=count),
        grid=(scan_count // S2,),
        in_specs=[
            held, held, whole(st.shape),
            whole(sums.shape), whole(np2.shape),
        ],
        out_specs=[more(rows // 2, L)] * 2,
        out_shape=[jax.ShapeDtypeStruct((rows // 2, scan_count, L), bf16)] * 2,
        compiler_params=params_of(),
        cost_estimate=cost(3),
        name="rim_two",
    )(d, c2, st, sums, np2)


def back_two_kernel(
    d_ref, c2_ref, hid_ref, st_ref, sum_ref, np_ref, ds_ref, kg_ref, grad, *, count
):
    step, steps = (pl.program_id(0), pl.num_programs(0))
    d_ref, c2_ref, ds_ref = (part_of(a, step, S2) for a in (d_ref, c2_ref, ds_ref))
    r, tiles = (c2_ref.shape[0] - 3, c2_ref.shape[2] // L)
    back = norm_back_two(st_ref, sum_ref, np_ref, count, r)

    @pl.when(step == 0)
    def _():
        grad[...] = jnp.zeros_like(grad)

    total = None
    for t in range(tiles):
        for row in range(r + 3):
            d = back(row, pair(d_ref, row, t), pair(c2_ref, row, t))
            ds_ref[row, :, t * L : (t + 1) * L] = d.astype(bf16)
        own = [ds_ref[i + 1, :, t * L : (t + 1) * L] for i in range(r)]
        none = jnp.zeros_like(own[0])
        lhs = jnp.concatenate(
            [
                jnp.transpose(jnp.concatenate([none] * p + own + [none] * (2 - p), axis=0))
                for p in range(3)
            ],
            axis=0,
        )
        rhs = hid_ref[1 : r + 3, :, t * L : (t + 2) * L].reshape((r + 2) * S2, 2 * L)
        part = jnp.dot(lhs, rhs, preferred_element_type=f32)
        total = part if total is None else total + part
    grad[...] += total

    @pl.when(step == steps - 1)
    def _():
        for p in range(3):
            for q in range(3):
                block = None
                for w in range(2):
                    at = (2 * p + w) * C
                    part = grad[at : at + C, (w + q) * C : (w + q + 1) * C]
                    block = part if block is None else block + part
                kg_ref[3 * p + q] = block


def back_two(d, c2, hid, st, sums, np2, count):
    r, scan_count, wide = hid.shape
    r, lanes = (r - 5, wide - L)
    return pl.pallas_call(
        functools.partial(back_two_kernel, count=count),
        grid=(scan_count // S2,),
        in_specs=[
            held,
            held,
            more(r + 5, wide),
            whole(st.shape),
            whole(sums.shape),
            whole(np2.shape),
        ],
        out_specs=[held, whole((9, C, C))],
        out_shape=[
            resident((r + 3, scan_count, lanes), bf16),
            jax.ShapeDtypeStruct((9, C, C), f32),
        ],
        scratch_shapes=[pltpu.VMEM((6 * C, 4 * C), f32)],
        compiler_params=params_of(),
        cost_estimate=cost(12),
        name="back_two",
    )(d, c2, hbm(hid), st, sums, np2)


def hidden_tile(t, parts, n1_ref, np_ref, w_ref, dp_ref, into, first, last):
    r = n1_ref.shape[0] - 1
    pairs, n_scans = ((r + 1) // 2, n1_ref.shape[1])
    low = low_half(n_scans)
    scale, shift = (0.5 * np_ref[0:1], 0.5 * np_ref[1:2])
    parts = [p.reshape(pairs + 1, 2, n_scans, L) for p in parts]
    pieces = [p[a : a + pairs, b] for a in range(2) for b in range(2) for p in parts]
    lhs = jnp.concatenate([p.reshape(pairs * n_scans, L) for p in pieces], axis=1)
    acc = jnp.dot(lhs, w_ref[...], preferred_element_type=f32).reshape(pairs, n_scans, 2 * L)
    sums = [jnp.zeros((8, L), f32), jnp.zeros((8, L), f32)]
    for i in range(r + 1):
        n = pair(n1_ref, i, t).astype(f32)
        h = n * scale + shift
        s = 1.0 + jnp.tanh(h)
        d = acc[i // 2, :, (i % 2) * L : (i % 2 + 1) * L] * (s + h * s * (2.0 - s))
        dp_ref[i, :, into * L : (into + 1) * L] = d
        if i < r:
            if first:
                d = jnp.where(low, 0.0, d)
            if last:
                d = jnp.where(low, d, 0.0)
            sums = [sums[0] + halves(d), sums[1] + halves(d * n)]
    return sums


def hidden_kernel(ds_ref, n1_ref, np_ref, w_ref, dp_ref, sum_ref, run):
    step, steps = (pl.program_id(0), pl.num_programs(0))
    ds_ref, n1_ref, dp_ref = (part_of(a, step) for a in (ds_ref, n1_ref, dp_ref))
    sums = None
    for t in range(1, n1_ref.shape[2] // L - 1):
        parts = [ds_ref[:, :, k * L : (k + 1) * L] for k in (t - 1, t)]
        sums = added(
            sums, hidden_tile(t, parts, n1_ref, np_ref, w_ref, dp_ref, t - 1, False, False)
        )
    add_sums(step, steps, [0.5 * x for x in sums], run, sum_ref)


def hidden_gradient(ds, n1, np2, w):
    r, scan_count, wide = n1.shape
    return pl.pallas_call(
        hidden_kernel,
        grid=(scan_count // S,),
        in_specs=[held, held, whole(np2.shape), whole(w.shape)],
        out_specs=[held, whole((1, 2, L))],
        out_shape=[
            resident((r, scan_count, wide - 2 * L), f32),
            jax.ShapeDtypeStruct((1, 2, L), f32),
        ],
        scratch_shapes=[pltpu.VMEM((8, L), f32)],
        compiler_params=params_of(),
        cost_estimate=cost(6),
        name="hidden_gradient",
    )(ds, n1, np2, w)


def hidden_ends_kernel(
    ds_ref, left_ref, right_ref, n1_ref, np_ref, w_ref, inner_ref, dp_ref, edge_ref, sum_ref, rim,
    run,
):
    step, steps = (pl.program_id(0), pl.num_programs(0))
    ds_ref, n1_ref, dp_ref = (part_of(a, step, S2) for a in (ds_ref, n1_ref, dp_ref))
    r, tiles = (n1_ref.shape[0] - 1, n1_ref.shape[2] // L)
    low = low_half(S2)
    for row in range(r + 3):
        rim[row] = rim_of(right_ref, left_ref, row, low).astype(bf16)
    first, last = (ds_ref[:, :, k * L : (k + 1) * L] for k in (0, tiles - 2))
    args = (n1_ref, np_ref, w_ref, dp_ref)
    sums = hidden_tile(0, [rim[...], first], *args, 0, True, False)
    sums = added(sums, hidden_tile(tiles - 1, [last, rim[...]], *args, 1, False, True))
    sums = [0.5 * jnp.sum(x, axis=0, keepdims=True) for x in sums]
    sums = [x + inner_ref[0, k : k + 1] / steps for k, x in enumerate(sums)]
    add_sums(step, steps, sums, run, sum_ref)
    half = edge_ref.shape[0]
    for i in range(half):
        both = jnp.where(low, swap(pair(dp_ref, half + i, 0)), pair(dp_ref, i, 0))
        edge_ref[i] = both.astype(bf16)


def hidden_ends(ds, left, right, n1, np2, w, inner, devices):
    r, scan_count, _wide = n1.shape
    half = left.shape[0]
    return pl.pallas_call(
        hidden_ends_kernel,
        grid=(scan_count // S2,),
        in_specs=[
            held,
            more(half, L),
            more(half, L),
            held,
            whole(np2.shape),
            whole(w.shape),
            whole(inner.shape),
        ],
        out_specs=[held, more(r // 2, L), whole((devices, 2, L))],
        out_shape=[
            resident((r, scan_count, 2 * L), f32),
            jax.ShapeDtypeStruct((r // 2, scan_count, L), bf16),
            jax.ShapeDtypeStruct((devices, 2, L), f32),
        ],
        scratch_shapes=[pltpu.VMEM((r + 2, S2, L), bf16), pltpu.VMEM((8, L), f32)],
        compiler_params=params_of(),
        cost_estimate=cost(3),
        name="hidden_gradient_ends",
    )(ds, left, right, n1, np2, w, inner)


def back_one_kernel(
    dp_ref, ends_ref, edge_ref, n1_ref, x_ref, bits_ref, st_ref, sum_ref, np_ref, kg2_ref, ds, kg_ref,
    xm, grad, flat, *, count,
):
    step, steps = (pl.program_id(0), pl.num_programs(0))
    dp_ref, ends_ref, n1_ref = (part_of(a, step) for a in (dp_ref, ends_ref, n1_ref))
    r, tiles = (n1_ref.shape[0] - 1, n1_ref.shape[2] // L - 1)
    cells = 2.0 * count * st_ref.shape[0]
    _mean, inv = stats_of(st_ref, count)
    shift_sum, gain_sum = sums_of(sum_ref)
    gain = np_ref[0:1] * inv
    c_n = -gain * gain_sum / cells
    c_0 = -gain * shift_sum / cells
    gain = 0.5 * gain
    f_down, f_right = inside()[1::2]
    packed = edge_ref.shape[0]
    low = low_half()
    right = jnp.where(low, 1.0, f_right)

    @pl.when(step == 0)
    def _():
        grad[...] = jnp.zeros_like(grad)

    def line(i, t):
        d = pair(ends_ref, i, min(t, 1)) if t in (0, tiles) else pair(dp_ref, i, t - 1)
        if t == tiles:
            beyond = edge_ref[i % packed].astype(f32)
            d = jnp.where(low, d, swap(beyond) if i >= packed else beyond)
        d = d * gain + (pair(n1_ref, i, t).astype(f32) * c_n + c_0)
        if t == tiles:
            d = d * right
        if i == r:
            d = d * f_down
        ds[i, :, t * L : (t + 1) * L] = d.astype(bf16)

    def turned(t, first):
        return jnp.transpose(ds[first : first + r, :, t * L : (t + 1) * L].reshape(r * S, L))

    columns = []
    total_even, total_odd = (None, None)
    for t in range(tiles + 1):
        for i in range(r + 1):
            line(i, t)
        columns.append([turned(t, 0), turned(t, 1)])
        if t == 0:
            continue
        k = t - 1
        for a in (2 * k, 2 * k + 1):
            for g in range(bits_ref.shape[0]):
                word = bits_ref[g, :, a * L : (a + 1) * L]
                for row in range(g * BITS, min(2 * r, (g + 1) * BITS)):
                    x = live(word, row, pair(x_ref, row, a))
                    xm[row % 2, row // 2, :, a * L : (a + 1) * L] = x
        xl = slice(2 * k * L, 2 * (k + 1) * L)
        xe, xo = (xm[a, :, :, xl].reshape(r * S, 2 * L) for a in range(2))
        here, below = (
            jnp.concatenate([columns[k][a][C:], columns[t][a]], axis=0) for a in range(2)
        )
        even = jnp.dot(here, xe, preferred_element_type=f32)
        odd = jnp.dot(
            jnp.concatenate([here, below], axis=0), xo, preferred_element_type=f32
        )
        total_even = even if total_even is None else total_even + even
        total_odd = odd if total_odd is None else total_odd + odd
    grad[: 3 * C] += total_even
    grad[3 * C :] += total_odd

    @pl.when(step == steps - 1)
    def _():
        blocks = []
        for p in range(3):
            first = (6, 0, 3)[p] * C
            for q in range(3):
                block = None
                for v in range(1, 4):
                    u = q - 3 + 2 * v
                    if 0 <= u < 4:
                        at = first + (v - 1) * C
                        part = grad[at : at + C, u * C : (u + 1) * C]
                        block = part if block is None else block + part
                blocks.append(block)
        blocks += [kg2_ref[8]] + [kg2_ref[k] for k in range(8)]
        for a in range(9):
            flat[a * C : (a + 1) * C] = jnp.concatenate(blocks[2 * a : 2 * a + 2], axis=1)
        if flat.shape[0] > 9 * C:
            flat[9 * C :] = jnp.zeros((flat.shape[0] - 9 * C, L), f32)
        devices, share, _lanes = kg_ref.shape
        for k in range(devices):
            kg_ref[k] = flat[k * share : (k + 1) * share].astype(bf16)


def back_one(dp, ends, edge, n1, x, bits, st, sums, np2, kg2, count):
    rows, scan_count, lanes = x.shape
    r, tiles = (rows // 2, lanes // L // 2)
    devices = st.shape[0]
    share = 8 * -(-9 * C // (8 * devices))
    wide = (tiles + 1) * L
    return pl.pallas_call(
        functools.partial(back_one_kernel, count=count),
        grid=(scan_count // S,),
        in_specs=[
            held,
            held,
            scans(edge.shape[0], L),
            held,
            scans(rows, lanes),
            scans(bits.shape[0], lanes),
            whole(st.shape),
            whole(sums.shape),
            whole(np2.shape),
            whole(kg2.shape),
        ],
        out_specs=[scans(r + 1, wide), whole((devices, share, L))],
        out_shape=[
            pltpu.HBM((r + 1, scan_count, wide), bf16),
            jax.ShapeDtypeStruct((devices, share, L), bf16),
        ],
        scratch_shapes=[
            pltpu.VMEM((2, r, S, lanes), bf16),
            pltpu.VMEM((9 * C, 4 * C), f32),
            pltpu.VMEM((devices * share, L), f32),
        ],
        compiler_params=params_of(),
        cost_estimate=cost(16),
        name="back_one",
    )(dp, ends, edge, n1, hbm(x), hbm(bits), st, sums, np2, kg2)


def input_grad_kernel(ds, bits_ref, w_ref, *rest):
    ig_ref = rest[-1]
    r, tiles = (ds.shape[0] - 1, ds.shape[2] // L - 1)
    for t in range(tiles):
        lanes = slice(t * L, (t + 2) * L)
        rows = [ds[a : a + r, :, lanes].reshape(r * S, 2 * L) for a in range(2)]
        even = jnp.dot(rows[0], w_ref[: 4 * C], preferred_element_type=f32)
        odd = jnp.dot(
            jnp.concatenate(rows, axis=1), w_ref[4 * C :], preferred_element_type=f32
        )
        for k, block in enumerate((even, odd)):
            block = block.reshape(r, S, 2 * L)
            for h in range(2):
                xl = slice((2 * t + h) * L, (2 * t + h + 1) * L)
                for i in range(r):
                    row = 2 * i + k
                    d = block[i, :, h * L : (h + 1) * L].astype(bf16)
                    ig_ref[row, :, xl] = live(bits_ref[row // BITS, :, xl], row, d)


def input_gradient(d, bits, w, part, before):
    r, scan_count, wide = d.shape
    rows, lanes = (2 * (r - 1), 2 * (wide - L))
    steps = scan_count // S // 2
    at = lambda n, m: pl.BlockSpec((n, S, m), lambda g: (0, g + part * steps, 0))
    earlier = () if before is None else (before,)
    return pl.pallas_call(
        input_grad_kernel,
        grid=(steps,),
        in_specs=[at(r, wide), at(bits.shape[0], lanes), whole(w.shape)]
        + [pl.BlockSpec(memory_space=pl.ANY)] * len(earlier),
        out_specs=at(rows, lanes),
        out_shape=jax.ShapeDtypeStruct((rows, scan_count, lanes), bf16),
        input_output_aliases={3: 0} if earlier else {},
        compiler_params=params_of(),
        cost_estimate=cost(7),
        name="input_gradient",
    )(hbm(d), hbm(bits), w, *earlier)


def share_kernel(g_ref, out_ref):
    devices = g_ref.shape[0]
    total = g_ref[0].astype(f32)
    for k in range(1, devices):
        total = total + g_ref[k].astype(f32)
    total = total.astype(bf16)
    for k in range(devices):
        out_ref[k] = total


def sum_share(grads):
    return pl.pallas_call(
        share_kernel,
        in_specs=[held],
        out_specs=held,
        out_shape=jax.ShapeDtypeStruct(grads.shape, bf16),
        compiler_params=pltpu.CompilerParams(vmem_limit_bytes=8 << 20),
        cost_estimate=cost(1),
        name="sum_share",
    )(grads)


def adam_step(weight_now, gradient, moment_one, moment_two, step_rate, decay_rate):
    first_new = adam_beta * moment_one + (1.0 - adam_beta) * gradient
    second_new = adam_beta * moment_two + (1.0 - adam_beta) * gradient * gradient
    correction = 1.0 - adam_beta**step_count
    update = first_new / correction / (jnp.sqrt(second_new / correction) + adam_eps)
    return (weight_now - step_rate * (update + decay_rate * weight_now), first_new, second_new)


def update_kernel(
    g_ref, s1_ref, s2_ref, k_ref, km_ref, kv_ref, n_ref, nm_ref, nv_ref, gn_ref, ok_ref, okm_ref,
    okv_ref, olow_ref, on_ref, onm_ref, onv_ref, flat,
):
    devices, share, _lanes = g_ref.shape
    for k in range(devices):
        flat[k * share : (k + 1) * share] = g_ref[k].astype(f32)
    norm_rows = []
    for ref in (s1_ref, s2_ref):
        shift_sum, gain_sum = sums_of(ref)
        norm_rows += [gain_sum[:, :C], shift_sum[:, :C]]
    g_norm = jnp.concatenate(norm_rows, axis=0)
    squares = jnp.sum(jnp.sum(flat[: 9 * C] ** 2, axis=0, keepdims=True), axis=1, keepdims=True)
    squares = squares + jnp.sum(
        jnp.sum(g_norm * g_norm, axis=0, keepdims=True), axis=1, keepdims=True
    )
    norm = jnp.sqrt(squares)
    gn_ref[...] = norm
    factor = jnp.minimum(1.0, clip_limit / norm)
    on, onm, onv = adam_step(
        n_ref[...], g_norm * factor, nm_ref[...], nv_ref[...], norm_rate, 0.0
    )
    on_ref[...] = on
    onm_ref[...] = onm
    onv_ref[...] = onv
    for layer in range(2):
        for a in range(5):
            width = L if a < 4 else C
            at = slice(a * L, a * L + width)
            if a == 4:
                g = flat[4 * C : 5 * C, layer * C : (layer + 1) * C]
            else:
                first = (a + 5 * layer) * C
                g = flat[first : first + C, :]
            k, km, kv = adam_step(
                k_ref[layer, :, at], g * factor, km_ref[layer, :, at], kv_ref[layer, :, at],
                kernel_rate, kernel_decay,
            )
            ok_ref[layer, :, at] = k
            okm_ref[layer, :, at] = km
            okv_ref[layer, :, at] = kv
            olow_ref[layer, :, at] = k.astype(bf16)


def update(grads, sums1, sums2, kt, kmt, kvt, norm_params, norm_m, norm_v):
    flat = lambda a: a.reshape(4, C)
    big = jax.ShapeDtypeStruct(kt.shape, f32)
    small = jax.ShapeDtypeStruct((4, C), f32)
    outs = [
        jax.ShapeDtypeStruct((1, 1), f32), big, big, big,
        jax.ShapeDtypeStruct(kt.shape, bf16), small, small, small,
    ]
    args = [grads, sums1, sums2, kt, kmt, kvt, flat(norm_params), flat(norm_m), flat(norm_v)]
    return pl.pallas_call(
        update_kernel,
        grid=(1,),
        in_specs=[whole(a.shape) for a in args],
        out_specs=[whole(o.shape) for o in outs],
        out_shape=outs,
        scratch_shapes=[pltpu.VMEM((grads.shape[0] * grads.shape[1], L), f32)],
        compiler_params=params_of(),
        cost_estimate=cost(3),
        name="update",
    )(*args)


def shifted(block, axis, distance):
    devices = range(lax.axis_size(axis))
    route = [(i - distance, i) for i in devices if i - distance in devices]
    return lax.ppermute(block, axis, route)


def exchange(rows):
    return lax.all_to_all(rows, BOTH, 0, 0, tiled=True)


def per_device(
    scan_features, occupancy, kernels, kernel_m, kernel_v, norm_params, norm_m, norm_v, cotangent
):
    x = jnp.transpose(scan_features, (1, 0, 2))
    cot = jnp.transpose(cotangent, (1, 0, 2))
    occ = jnp.transpose(occupancy, (2, 0, 1))
    kt, kmt, kvt = (jnp.transpose(a, (0, 2, 1)) for a in (kernels, kernel_m, kernel_v))
    gy, gx = (lax.axis_size("gy"), lax.axis_size("gx"))
    devices = gy * gx
    rows, scan_count, lanes = x.shape
    r, tiles = (rows // 2, lanes // L // 2)
    count = float(scan_count * r * tiles)
    last = (tiles - 1) * L

    down, cot_down, corner, xcol = edges(x, occ, cot)
    xcol = shifted(xcol, "gx", 1)
    down = shifted(down, "gy", 1)
    cot_down = shifted(cot_down, "gy", -1)
    corner = lax.ppermute(
        corner, BOTH, [(i, i + gx + 1) for i in range(devices - gx) if (i + 1) % gx]
    )
    bits, w1, w2, w2b, w1b, np2 = prepare(occ, kt, norm_params)

    xcol, cot_down = lax.optimization_barrier((xcol, cot_down))
    ends, st1, going_right, going_left, edge = first_last(x, bits, down, xcol, corner, w1)
    left_in = shifted(going_right, "gx", 1)
    right_in = shifted(going_left, "gx", -1)
    c1, st1, up, low_rows = conv_one(x, bits, down, st1, w1, devices)
    up, low_rows = pack_rows(up, low_rows, edge, left_in, right_in)
    down_in = shifted(up, "gy", -1)
    up_in = shifted(low_rows, "gy", 1)
    st1 = exchange(st1)

    c2, n1, hid, st2 = conv_two(
        c1, ends, up_in, down_in, left_in, right_in, st1, np2, w2, count
    )
    st2 = exchange(st2)
    features, d2, sums2 = output(c2, st2, np2, cot, down, cot_down, count)
    sums2 = exchange(sums2)
    going_right, going_left = rim_two(d2, c2, st2, sums2, np2, count)
    left_in = shifted(going_right, "gx", 1)
    right_in = shifted(going_left, "gx", -1)
    ds, kg2 = back_two(d2, c2, hid, st2, sums2, np2, count)
    d1, sums1 = hidden_gradient(ds, n1, np2, w2b)
    d1_ends, edge, sums1 = hidden_ends(ds, left_in, right_in, n1, np2, w2b, sums1, devices)
    edge = shifted(edge, "gx", -1)
    sums1 = exchange(sums1)
    d1, grads = back_one(d1, d1_ends, edge, n1, x, bits, st1, sums1, np2, kg2, count)
    grads = exchange(grads)
    input_grad = input_gradient(d1, bits, w1b, 0, None)
    grads, input_grad = lax.optimization_barrier((sum_share(grads), input_grad))
    grads = exchange(grads)
    input_grad = input_gradient(d1, bits, w1b, 1, input_grad)
    norm, k, km, kv, low, n, nm, nv = update(
        grads, sums1, sums2, kt, kmt, kvt, norm_params, norm_m, norm_v
    )
    back = lambda a: jnp.transpose(a, (0, 2, 1))
    deep = lambda a: a.reshape(norm_params.shape)
    return (
        jnp.transpose(features, (1, 0, 2)),
        jnp.transpose(input_grad, (1, 0, 2)),
        norm.reshape(()),
        back(k),
        back(km),
        back(kv),
        back(low),
        deep(n),
        deep(nm),
        deep(nv),
    )


def solution(mesh):
    split = P(None, "gy", "gx")
    return jax.shard_map(
        per_device,
        mesh=mesh,
        in_specs=(split, split) + (P(),) * 6 + (split,),
        out_specs=(split, split) + (P(),) * 8,
        check_vma=False,
    )
```

```python
import functools
import math

import jax
import jax.numpy as jnp
from jax import lax
from jax.experimental import pallas as pl
from jax.experimental.pallas import tpu as pltpu
from jax.sharding import PartitionSpec as P

norm_eps = 1e-05
adam_beta = 0.5
adam_eps = 1e-08
step_count = 5
clip_limit = 1.0
kernel_rate = 0.04
norm_rate = 0.25
kernel_decay = 0.01

f32, bf16 = (jnp.float32, jnp.bfloat16)
BOTH = ("gy", "gx")
S, S2, C, L, BITS = (16, 32, 64, 128, 13)


def params_of(limit=20):
    return pltpu.CompilerParams(
        dimension_semantics=("arbitrary",), vmem_limit_bytes=limit << 20
    )


def cost(microseconds):
    return pl.CostEstimate(
        flops=0, bytes_accessed=int(microseconds * 3.6e6), transcendentals=0
    )


def whole(shape):
    return pl.BlockSpec(shape, lambda g: (0,) * len(shape))


def scans(rows, lanes, n=S):
    return pl.BlockSpec((rows, n, lanes), lambda g: (0, g, 0))


def more(rows, lanes):
    return scans(rows, lanes, S2)


def resident(shape, dtype):
    return pltpu.VMEM(shape, dtype)


held = pl.BlockSpec(memory_space=pltpu.VMEM)


def vmem(array):
    return pltpu.with_memory_space_constraint(array, pltpu.VMEM)


def hbm(array):
    return pltpu.with_memory_space_constraint(array, pltpu.HBM)


def inside():
    flags = []
    for axis in BOTH:
        at = lax.axis_index(axis)
        flags += [at > 0, at < lax.axis_size(axis) - 1]
    return [jnp.where(flag, 1.0, 0.0) for flag in flags]


def part_of(ref, step, n=S):
    return ref.at[:, pl.ds(pl.multiple_of(step * n, n), n), :]


def low_half(rows=S):
    return lax.broadcasted_iota(jnp.int32, (rows, L), 1) < C


def swap(x):
    return pltpu.roll(x, C, 1)


def fold(x):
    x = jnp.broadcast_to(x, (8, L))
    return (x + swap(x))[:1]


def live(word, row, x):
    bit = 1 << (row % BITS)
    if x.dtype == bf16:
        return jnp.where((word & jnp.int16(bit)) != 0, x, jnp.zeros_like(x))
    return jnp.where((word.astype(jnp.int32) & bit) != 0, x, 0.0)


def pair(ref, row, t):
    return ref[row, :, t * L : (t + 1) * L]


def stats_of(st_ref, count):
    groups = 2 * st_ref.shape[0]
    means = st_ref[:, 0, :]
    mean = fold(jnp.sum(means, axis=0, keepdims=True)) / groups
    spread = st_ref[:, 1, :] + count * (means - mean) ** 2
    spread = fold(jnp.sum(spread, axis=0, keepdims=True)) / (groups * count)
    return (mean, lax.rsqrt(spread + norm_eps))


def sums_of(st_ref):
    return tuple(fold(jnp.sum(st_ref[:, k, :], axis=0, keepdims=True)) for k in range(2))


def pilot_of(block):
    flat = block.reshape(-1, L)
    return jnp.sum(flat, axis=0, keepdims=True) / flat.shape[0]


def finish_stats(step, steps, pilot, sums, count, run_ref, st_ref):
    off, squares = (jnp.sum(s, axis=0, keepdims=True) for s in sums)
    mean = pilot + off / count
    squares = squares - off * off / count

    @pl.when(step == 0)
    def _():
        run_ref[0:1] = mean
        run_ref[1:2] = squares

    @pl.when(step > 0)
    def _():
        before = step.astype(f32)
        share = 1.0 / (before + 1.0)
        delta = mean - run_ref[0:1]
        run_ref[0:1] = run_ref[0:1] + delta * share
        run_ref[1:2] = run_ref[1:2] + squares + delta * delta * (count * before * share)

    @pl.when(step == steps - 1)
    def _():
        st_ref[...] = jnp.broadcast_to(run_ref[0:2][None], st_ref.shape)


def off_sums(blocks, pilot):
    sums = [jnp.zeros((8, L), f32), jnp.zeros((8, L), f32)]
    for block in blocks:
        d = block - pilot
        sums = [sums[0] + halves(d), sums[1] + halves(d * d)]
    return sums


def added(a, b):
    return b if a is None else [x + y for x, y in zip(a, b)]


def rim_of(first, second, row, low):
    half = first.shape[0]
    if row < half:
        return jnp.where(low, first[row].astype(f32), second[row].astype(f32))
    row = row - half
    return swap(jnp.where(low, second[row].astype(f32), first[row].astype(f32)))


def halves(x):
    total = x[:8]
    for k in range(8, x.shape[0], 8):
        total = total + x[k : k + 8]
    return total


def occupancy_words(occ, groups, first):
    rows = occ.shape[1]
    shape = (rows, groups * L)
    group_of = lax.broadcasted_iota(jnp.int32, shape, 1) // L + first
    inner = lax.broadcasted_iota(jnp.int32, shape, 0) - group_of * BITS
    power = jnp.where(
        (inner >= 0) & (inner < BITS), (1 << jnp.clip(inner, 0, BITS)), 0
    ).astype(bf16)
    low = occ.astype(f32).astype(bf16)
    return jnp.dot(low, power, preferred_element_type=f32).astype(jnp.int32)


def edges_kernel(
    row_ref, col_ref, occ_ref, cot_last_ref, cot_first_ref, down_ref, up_ref, corner_ref, xcol_ref
):
    cols, scan_count, rows = occ_ref.shape
    lanes = row_ref.shape[2]
    groups = -(-rows // BITS)
    low = low_half(scan_count)
    words = occupancy_words(occ_ref[...].reshape(cols * scan_count, rows), 1, groups - 1)
    words = words.reshape(cols // 2, 2, scan_count, L)
    for t in range(cols // 2):
        word = jnp.where(low, words[t, 0], words[t, 1])
        x = live(word, rows - 1, row_ref[0, :, t * L : (t + 1) * L].astype(f32)).astype(bf16)
        down_ref[:, t * L : (t + 1) * L] = x
    corner_ref[...] = x
    down_ref[:, lanes:] = cot_last_ref[0]
    up_ref[...] = cot_first_ref[...]
    words = occupancy_words(occ_ref[cols - 1], groups, 0)
    for i in range(rows // 2):
        even, odd = (
            live(
                words[:, row // BITS * L : (row // BITS + 1) * L], row, col_ref[row].astype(f32)
            )
            for row in (2 * i, 2 * i + 1)
        )
        xcol_ref[i] = jnp.where(low, swap(even), odd).astype(bf16)


def edges(x, occ, cot):
    rows, scan_count, lanes = x.shape
    r, wide = (rows // 2, lanes // 2)
    outs = [
        jax.ShapeDtypeStruct((scan_count, lanes + wide), bf16),
        jax.ShapeDtypeStruct((2, scan_count, wide), bf16),
        jax.ShapeDtypeStruct((scan_count, L), bf16),
        jax.ShapeDtypeStruct((r, scan_count, L), bf16),
    ]
    return pl.pallas_call(
        edges_kernel,
        grid=(1,),
        in_specs=[
            pl.BlockSpec((1, scan_count, lanes), lambda g: (rows - 1, 0, 0)),
            pl.BlockSpec((rows, scan_count, L), lambda g: (0, 0, lanes // L - 1)),
            whole(occ.shape),
            pl.BlockSpec((1, scan_count, wide), lambda g: (r - 1, 0, 0)),
            pl.BlockSpec((2, scan_count, wide), lambda g: (0, 0, 0)),
        ],
        out_specs=[whole(o.shape) for o in outs],
        out_shape=outs,
        compiler_params=params_of(),
        cost_estimate=cost(3),
        name="edges",
    )(hbm(x), hbm(x), hbm(occ), hbm(cot), hbm(cot))


def prep_kernel(occ_ref, kt_ref, np_ref, bits_ref, w1_ref, w2_ref, w2b_ref, w1b_ref, np2_ref):
    cols, scan_count, rows = occ_ref.shape
    groups = bits_ref.shape[0]
    words = occupancy_words(occ_ref[...].reshape(cols * scan_count, rows), groups, 0)
    words = words.reshape(cols // 2, 2, scan_count, groups * L)
    low = low_half(scan_count)
    for g in range(groups):
        for t in range(cols // 2):
            lanes = slice(g * L, (g + 1) * L)
            word = jnp.where(low, words[t, 0, :, lanes], words[t, 1, :, lanes])
            bits_ref[g, :, t * L : (t + 1) * L] = word.astype(jnp.int16)
    back = [[kt_ref[l, :, k * C : (k + 1) * C] for k in range(9)] for l in range(2)]
    fore = [[jnp.transpose(b) for b in layer] for layer in back]
    none = jnp.zeros((C, C), f32)

    def put(ref, rows_of, cols_of, pick):
        for a in range(rows_of):
            blocks = [pick(a, b) for b in range(cols_of)]
            for k in range(0, cols_of, 2):
                two = jnp.concatenate(blocks[k : k + 2], axis=1).astype(bf16)
                ref[a * C : (a + 1) * C, k * C : (k + 2) * C] = two

    def tap(table, p, q):
        return table[3 * p + q] if 0 <= p < 3 and 0 <= q < 3 else none

    put(w1_ref, 30, 4, lambda a, b: tap(fore[0], a // 6 - 2 * (b // 2), a % 6 - 2 * (b % 2) - 1))
    put(w2_ref, 16, 4, lambda a, b: tap(fore[1], a // 4 - b // 2, a % 4 - b % 2))
    put(w2b_ref, 16, 4, lambda a, b: tap(back[1], b // 2 + 2 - a // 4, b % 2 + 2 - a % 4))
    put(w1b_ref, 12, 4, lambda a, b: tap(back[0], (1, 2, 0)[a // 4], b + 3 - 2 * (a % 4)))
    np2_ref[...] = jnp.concatenate([np_ref[...], np_ref[...]], axis=1)


def prepare(occ, kt, norm_params):
    cols, scan_count, rows = occ.shape
    full = lambda *shape: jax.ShapeDtypeStruct(shape, bf16)
    outs = [
        jax.ShapeDtypeStruct((-(-rows // BITS), scan_count, cols * C), jnp.int16),
        full(30 * C, 4 * C),
        full(16 * C, 4 * C),
        full(16 * C, 4 * C),
        full(12 * C, 4 * C),
        jax.ShapeDtypeStruct((4, L), f32),
    ]
    return pl.pallas_call(
        prep_kernel,
        grid=(1,),
        in_specs=[whole(occ.shape), whole(kt.shape), whole((4, C))],
        out_specs=[whole(o.shape) for o in outs],
        out_shape=outs,
        compiler_params=params_of(),
        cost_estimate=cost(4),
        name="prepare",
    )(hbm(occ), kt, norm_params.reshape(4, C))


def mask_tile(x_ref, bits_ref, t, xs, into):
    rows = x_ref.shape[0]
    for g in range(bits_ref.shape[0]):
        word = bits_ref[g, :, t * L : (t + 1) * L]
        for row in range(g * BITS, min(rows, (g + 1) * BITS)):
            x = live(word, row, pair(x_ref, row, t))
            xs[(row + 1) // 4, (row + 1) % 4, :, into * L : (into + 1) * L] = x


def clear_rows(rows, pairs, xs):
    for k in range(rows + 1, 4 * pairs + 1):
        xs[k // 4, k % 4] = jnp.zeros_like(xs[0, 0])


def conv_rows(xs, lanes, w, r, before=()):
    pairs = (r + 1) // 2
    pieces = [xs[0:pairs, q, :, lanes] for q in range(4)] + [xs[1 : pairs + 1, 0, :, lanes]]
    pieces = [p.reshape(pairs * S, p.shape[2]) for p in pieces]
    lhs = jnp.concatenate(list(before) + pieces, axis=1)
    acc = jnp.dot(lhs, w, preferred_element_type=f32).reshape(pairs, S, 2 * L)
    return [acc[i // 2, :, (i % 2) * L : (i % 2 + 1) * L] for i in range(r)]


def first_last_kernel(
    x_ref, bits_ref, xrow_ref, xcol_ref, corner_ref, w_ref, c_ref, st_ref, er_ref, el_ref,
    edge_ref, xs, run,
):
    step, steps = (pl.program_id(0), pl.num_programs(0))
    c_ref, x_ref, bits_ref = (part_of(a, step) for a in (c_ref, x_ref, bits_ref))
    rows, lanes = (x_ref.shape[0], x_ref.shape[2])
    r = rows // 2
    low = low_half()

    @pl.when(step == 0)
    def _():
        clear_rows(rows, (r + 1) // 2, xs)

    xs[0, 0, :, :L] = xrow_ref[:, :L]
    xs[0, 0, :, L:] = xrow_ref[:, lanes - 2 * L : lanes]
    mask_tile(x_ref, bits_ref, 0, xs, 0)
    mask_tile(x_ref, bits_ref, lanes // L - 2, xs, 1)
    mask_tile(x_ref, bits_ref, lanes // L - 1, xs, 2)
    wide = 3 * L
    rows_of = lambda q, a, b: w_ref[q * wide + a * C : q * wide + b * C]
    w = jnp.concatenate([rows_of(q, 0, 4) for q in range(5)], axis=0)
    last = conv_rows(xs, slice(L, 3 * L), w, r)
    pairs = (r + 1) // 2
    none = jnp.zeros((S, L), bf16)
    beside = [corner_ref[...]] + [xcol_ref[i] for i in range(r)] + [none]
    w = [jnp.zeros((C, 2 * L), bf16)] + [rows_of(q, 3, 4) for q in range(5)]
    w = jnp.concatenate(w + [rows_of(q, 4, 6) for q in range(5)], axis=0)
    more_lhs = [
        jnp.concatenate([beside[2 * m + k] for m in range(pairs)], axis=0) for k in range(3)
    ]
    first = conv_rows(xs, slice(0, L), w, r, more_lhs)
    edge = [jnp.where(low, b, a) for a, b in zip(first, last)]
    pilot = pilot_of(jnp.concatenate(edge[: r // 2], axis=0))
    for i in range(r):
        c_ref[i, :, :L] = first[i]
        c_ref[i, :, L:] = last[i]
        edge_ref[i] = edge[i].astype(bf16)
    finish_stats(step, steps, pilot, off_sums(edge, pilot), float(r * S), run, st_ref)
    half = er_ref.shape[0]
    for k in range(half):
        far = swap(edge[k + half]) if k + half < r else jnp.zeros((S, L), f32)
        er_ref[k] = jnp.where(low, edge[k], far).astype(bf16)
        el_ref[k] = jnp.where(low, far, edge[k]).astype(bf16)


def first_last(x, bits, down, xcol, corner, w):
    rows, scan_count, lanes = x.shape
    r = rows // 2
    shape = lambda dtype, *s: jax.ShapeDtypeStruct(s, dtype)
    return pl.pallas_call(
        first_last_kernel,
        grid=(scan_count // S,),
        in_specs=[
            held,
            held,
            pl.BlockSpec((S, down.shape[1]), lambda g: (g, 0)),
            scans(r, L),
            pl.BlockSpec((S, L), lambda g: (g, 0)),
            whole(w.shape),
        ],
        out_specs=[
            held,
            whole((1, 2, L)),
            scans((r + 1) // 2, L),
            scans((r + 1) // 2, L),
            scans(r, L),
        ],
        out_shape=[
            resident((r, scan_count, 2 * L), f32),
            shape(f32, 1, 2, L),
            shape(bf16, (r + 1) // 2, scan_count, L),
            shape(bf16, (r + 1) // 2, scan_count, L),
            shape(bf16, r, scan_count, L),
        ],
        scratch_shapes=[
            pltpu.VMEM(((r + 1) // 2 + 1, 4, S, 3 * L), bf16),
            pltpu.VMEM((8, L), f32),
        ],
        compiler_params=params_of(),
        cost_estimate=cost(4),
        name="conv_one_ends",
    )(vmem(x), vmem(bits), down, xcol, corner, w)


def conv_one_kernel(
    x_ref, bits_ref, xrow_ref, ends_ref, w_ref, c_ref, st_ref, up_ref, down_ref, xs, run
):
    step, steps = (pl.program_id(0), pl.num_programs(0))
    c_ref, x_ref, bits_ref = (part_of(a, step) for a in (c_ref, x_ref, bits_ref))
    rows, tiles = (x_ref.shape[0], x_ref.shape[2] // L)
    r, inner = (rows // 2, tiles // 2 - 1)

    @pl.when(step == 0)
    def _():
        clear_rows(rows, (r + 1) // 2, xs)

    xs[0, 0] = xrow_ref[:, : tiles * L]
    sums, pilot = (None, None)
    filled = 0
    for t in range(inner):
        while filled < 2 * t + 3:
            mask_tile(x_ref, bits_ref, filled, xs, filled)
            filled += 1
        blocks = conv_rows(xs, slice(2 * t * L, (2 * t + 3) * L), w_ref[...], r)
        if pilot is None:
            pilot = pilot_of(jnp.concatenate(blocks[: r // 2], axis=0))
        sums = added(sums, off_sums(blocks, pilot))
        for i, block in enumerate(blocks):
            c_ref[i, :, t * L : (t + 1) * L] = block
    finish_stats(step, steps, pilot, sums, float(r * inner * S), run, st_ref)
    up_ref[...] = c_ref[0:3].astype(bf16)
    down_ref[...] = c_ref[r - 2 : r].astype(bf16)

    @pl.when(step == steps - 1)
    def _():
        own, more = (float(r * S) * steps * n for n in (inner, 1))
        delta = ends_ref[0, 0:1] - run[0:1]
        mean = run[0:1] + delta * (more / (own + more))
        squares = run[1:2] + ends_ref[0, 1:2] + delta * delta * (own * more / (own + more))
        row = jnp.concatenate([mean, squares], axis=0)
        st_ref[...] = jnp.broadcast_to(row[None], st_ref.shape)


def conv_one(x, bits, down, ends, w, devices):
    rows, scan_count, lanes = x.shape
    r, wide = (rows // 2, lanes // 2 - L)
    shape = lambda dtype, *s: jax.ShapeDtypeStruct(s, dtype)
    return pl.pallas_call(
        conv_one_kernel,
        grid=(scan_count // S,),
        in_specs=[
            held,
            held,
            pl.BlockSpec((S, down.shape[1]), lambda g: (g, 0)),
            whole(ends.shape),
            whole(w.shape),
        ],
        out_specs=[held, whole((devices, 2, L)), scans(3, wide), scans(2, wide)],
        out_shape=[
            resident((r, scan_count, wide), f32),
            shape(f32, devices, 2, L),
            shape(bf16, 3, scan_count, wide),
            shape(bf16, 2, scan_count, wide),
        ],
        scratch_shapes=[
            pltpu.VMEM(((r + 1) // 2 + 1, 4, S, lanes), bf16),
            pltpu.VMEM((8, L), f32),
        ],
        compiler_params=params_of(),
        cost_estimate=cost(11),
        name="conv_one",
    )(vmem(x), vmem(bits), down, ends, w)


def pack_kernel(up_ref, down_ref, edge_ref, left_ref, right_ref, up_out, down_out):
    r, wide = (edge_ref.shape[0], up_ref.shape[2])
    low = low_half()
    for src, out, first in ((up_ref, up_out, 0), (down_ref, down_out, r - 2)):
        out[:, :, :wide] = src[...]
        for k in range(src.shape[0]):
            out[k, :, wide : wide + L] = edge_ref[first + k]
            out[k, :, wide + L :] = rim_of(left_ref, right_ref, first + k, low).astype(bf16)


def pack_rows(up, down, edge, left, right):
    r, scan_count, _lanes = edge.shape
    wide = up.shape[2]
    return pl.pallas_call(
        pack_kernel,
        grid=(scan_count // S,),
        in_specs=[
            scans(3, wide), scans(2, wide), scans(r, L), scans(left.shape[0], L),
            scans(right.shape[0], L),
        ],
        out_specs=[scans(3, wide + 2 * L), scans(2, wide + 2 * L)],
        out_shape=[
            jax.ShapeDtypeStruct((n, scan_count, wide + 2 * L), bf16) for n in (3, 2)
        ],
        compiler_params=params_of(10),
        cost_estimate=cost(1),
        name="pack_rows",
    )(up, down, edge, left, right)


def conv_two_kernel(
    c_ref, ends_ref, up_ref, down_ref, left_ref, right_ref, st_ref, np_ref, w_ref, c2_ref,
    n1_ref, hid_ref, st2_ref, rim, run, *, count,
):
    step, steps = (pl.program_id(0), pl.num_programs(0))
    c_ref, ends_ref, c2_ref, n1_ref, hid_ref = (
        part_of(a, step, S2) for a in (c_ref, ends_ref, c2_ref, n1_ref, hid_ref)
    )
    r, tiles = (c_ref.shape[0], c_ref.shape[2] // L + 2)
    t_out = tiles - 1
    mean, inv = stats_of(st_ref, count)
    offset = -mean * inv
    scale = 0.5 * np_ref[0:1] * inv
    shift = 0.5 * (np_ref[0:1] * offset + np_ref[1:2])
    f_up, f_down, f_left, f_right = inside()
    low = low_half(S2)
    left = jnp.where(low, f_left, 1.0)
    right = jnp.where(low, 1.0, f_right)
    for row in range(r):
        rim[row] = rim_of(left_ref, right_ref, row, low)

    def act(row, t):
        at_end = t in (0, tiles - 1)
        if 2 <= row < r + 2:
            flag = None
            c = pair(ends_ref, row - 2, min(t, 1)) if at_end else pair(c_ref, row - 2, t - 1)
            beyond = rim[row - 2] if at_end else None
        else:
            src, k, flag = (up_ref, row, f_up) if row < 2 else (down_ref, row - r - 2, f_down)
            c = pair(src, k, tiles - 2 if at_end else t - 1).astype(f32)
            beyond = pair(src, k, tiles - 1).astype(f32) if at_end else None
        if t == 0:
            c = jnp.where(low, beyond, c)
        if t == tiles - 1:
            c = jnp.where(low, c, beyond)
        h = c * scale + shift
        out = h + h * jnp.tanh(h)
        if t == 0:
            out = out * left
        if t == tiles - 1:
            out = out * right
        if flag is not None:
            out = out * flag
        out = out.astype(bf16)
        hid_ref[row, :, t * L : (t + 1) * L] = out
        if 2 <= row < r + 3:
            n1_ref[row - 2, :, t * L : (t + 1) * L] = (c * inv + offset).astype(bf16)

    pairs = (r + 3) // 2
    sums, pilot = (None, None)
    for t in range(tiles):
        for row in range(r + 5):
            act(row, t)
        k = t - 1
        if k < 0:
            continue
        lanes = slice(k * L, (k + 2) * L)
        pieces = [
            jnp.concatenate([hid_ref[2 * m + a, :, lanes] for m in range(pairs)], axis=0)
            for a in range(4)
        ]
        lhs = jnp.concatenate(pieces, axis=1)
        acc = jnp.dot(lhs, w_ref[...], preferred_element_type=f32).reshape(pairs, S2, 2 * L)
        if pilot is None:
            pilot = pilot_of(acc[1 : r // 2, :, :L])
        blocks = []
        for row in range(r + 3):
            block = acc[row // 2, :, (row % 2) * L : (row % 2 + 1) * L]
            c2_ref[row, :, k * L : (k + 1) * L] = block
            if 0 < row <= r:
                blocks.append(block)
        sums = added(sums, off_sums(blocks, pilot))
    finish_stats(step, steps, pilot, sums, float(r * t_out * S2), run, st2_ref)


def conv_two(c1, ends, up, down, left, right, st, np2, w, count):
    r, scan_count, wide = c1.shape
    wide = wide + 2 * L
    lanes = wide - L
    devices = st.shape[0]
    return pl.pallas_call(
        functools.partial(conv_two_kernel, count=count),
        grid=(scan_count // S2,),
        in_specs=[
            held,
            held,
            more(2, wide),
            more(3, wide),
            more(left.shape[0], L),
            more(right.shape[0], L),
            whole(st.shape),
            whole(np2.shape),
            whole(w.shape),
        ],
        out_specs=[held, held, held, whole((devices, 2, L))],
        out_shape=[
            resident((r + 3, scan_count, lanes), f32),
            resident((r + 1, scan_count, wide), bf16),
            resident((r + 5, scan_count, wide), bf16),
            jax.ShapeDtypeStruct((devices, 2, L), f32),
        ],
        scratch_shapes=[
            pltpu.VMEM((r, S2, L), f32),
            pltpu.VMEM((8, L), f32),
        ],
        compiler_params=params_of(10),
        cost_estimate=cost(14),
        name="conv_two",
    )(c1, ends, up, down, left, right, st, np2, w)


def output_kernel(
    c2_ref, st_ref, np_ref, cot_ref, up_ref, down_ref, feat_ref, d_ref, sum_ref, run, *, count,
):
    step, steps = (pl.program_id(0), pl.num_programs(0))
    c2_ref, d_ref, cot_ref = (part_of(a, step, S2) for a in (c2_ref, d_ref, cot_ref))
    r, tiles = (cot_ref.shape[0], cot_ref.shape[2] // L)
    mean, inv = stats_of(st_ref, count)
    offset = -mean * inv
    scale = 0.5 * np_ref[2:3] * inv
    shift = 0.5 * (np_ref[2:3] * offset + np_ref[3:4])
    above = 2 * tiles

    def slope(c, cot):
        h = c * scale + shift
        s = 1.0 + jnp.tanh(h)
        f = h * s
        return (f, cot.astype(f32) * (s + f * (2.0 - s)))

    sums = None
    for t in range(tiles):
        part = [jnp.zeros((8, L), f32), jnp.zeros((8, L), f32)]
        for i in range(r):
            c = pair(c2_ref, i + 1, t)
            f, d = slope(c, pair(cot_ref, i, t))
            feat_ref[i, :, t * L : (t + 1) * L] = f.astype(bf16)
            d_ref[i + 1, :, t * L : (t + 1) * L] = d
            part = [part[0] + halves(d), part[1] + halves(d * c)]
        sums = added(sums, part)
    for t in range(tiles):
        lanes = slice(t * L, (t + 1) * L)
        cot = up_ref[:, (above + t) * L : (above + t + 1) * L]
        d_ref[0, :, lanes] = slope(pair(c2_ref, 0, t), cot)[1]
        for k in range(2):
            row = r + 1 + k
            d_ref[row, :, lanes] = slope(pair(c2_ref, row, t), pair(down_ref, k, t))[1]
    sums = (0.5 * sums[0], (0.5 * inv) * (sums[1] - mean * sums[0]))
    add_sums(step, steps, sums, run, sum_ref)


def add_sums(step, steps, sums, run, sum_ref):
    rows = jnp.concatenate([jnp.sum(s, axis=0, keepdims=True) for s in sums], axis=0)

    @pl.when(step == 0)
    def _():
        run[0:2] = rows

    @pl.when(step > 0)
    def _():
        run[0:2] = run[0:2] + rows

    @pl.when(step == steps - 1)
    def _():
        sum_ref[...] = jnp.broadcast_to(run[0:2][None], sum_ref.shape)


def output(c2, st, np2, cot, up, down, count):
    r, scan_count, lanes = cot.shape
    devices = st.shape[0]
    return pl.pallas_call(
        functools.partial(output_kernel, count=count),
        grid=(scan_count // S2,),
        in_specs=[
            held,
            whole(st.shape),
            whole(np2.shape),
            held,
            pl.BlockSpec((S2, up.shape[1]), lambda g: (g, 0)),
            more(2, lanes),
        ],
        out_specs=[more(r, lanes), held, whole((devices, 2, L))],
        out_shape=[
            jax.ShapeDtypeStruct((r, scan_count, lanes), bf16),
            resident((r + 3, scan_count, lanes), f32),
            jax.ShapeDtypeStruct((devices, 2, L), f32),
        ],
        scratch_shapes=[pltpu.VMEM((8, L), f32)],
        compiler_params=params_of(10),
        cost_estimate=cost(12),
        name="output",
    )(c2, st, np2, vmem(cot), up, down)


def norm_back_two(st_ref, sum_ref, np_ref, count, rows):
    cells = 2.0 * count * st_ref.shape[0]
    mean, inv = stats_of(st_ref, count)
    shift_sum, gain_sum = sums_of(sum_ref)
    gain = np_ref[2:3] * inv
    c_n = -gain * inv * gain_sum / cells
    c_0 = -gain * shift_sum / cells - c_n * mean
    gain = 0.5 * gain
    f_up, f_down = inside()[:2]

    def back(row, d, c):
        d = d * gain + (c * c_n + c_0)
        if isinstance(row, int):
            if row == 0:
                d = d * f_up
            if row > rows:
                d = d * f_down
        return d

    return back


def rim_two_kernel(
    d_ref, c_ref, st_ref, sum_ref, np_ref, er_ref, el_ref, *, count
):
    d_ref, c_ref = (part_of(a, pl.program_id(0), S2) for a in (d_ref, c_ref))
    rows, last = (d_ref.shape[0], d_ref.shape[2] // L - 1)
    back = norm_back_two(st_ref, sum_ref, np_ref, count, rows - 3)
    low = low_half(S2)
    half = rows // 2
    column = lambda row, t: back(row, pair(d_ref, row, t), pair(c_ref, row, t))
    both = lambda row: jnp.where(low, column(row, 0), column(row, last))
    for k in range(half):
        near, far = (both(k), swap(both(k + half)))
        el_ref[k] = jnp.where(low, near, far).astype(bf16)
        er_ref[k] = jnp.where(low, far, near).astype(bf16)


def rim_two(d, c2, st, sums, np2, count):
    rows, scan_count, lanes = d.shape
    return pl.pallas_call(
        functools.partial(rim_two_kernel, count=count),
        grid=(scan_count // S2,),
        in_specs=[
            held, held, whole(st.shape),
            whole(sums.shape), whole(np2.shape),
        ],
        out_specs=[more(rows // 2, L)] * 2,
        out_shape=[jax.ShapeDtypeStruct((rows // 2, scan_count, L), bf16)] * 2,
        compiler_params=params_of(10),
        cost_estimate=cost(3),
        name="rim_two",
    )(d, c2, st, sums, np2)


def back_two_kernel(
    d_ref, c2_ref, hid_ref, st_ref, sum_ref, np_ref, ds_ref, kg_ref, grad, *, count
):
    step, steps = (pl.program_id(0), pl.num_programs(0))
    d_ref, c2_ref, ds_ref, hid_ref = (
        part_of(a, step, S2) for a in (d_ref, c2_ref, ds_ref, hid_ref)
    )
    r, tiles = (c2_ref.shape[0] - 3, c2_ref.shape[2] // L)
    back = norm_back_two(st_ref, sum_ref, np_ref, count, r)

    @pl.when(step == 0)
    def _():
        grad[...] = jnp.zeros_like(grad)

    total = None
    for t in range(tiles):
        for row in range(r + 3):
            d = back(row, pair(d_ref, row, t), pair(c2_ref, row, t))
            ds_ref[row, :, t * L : (t + 1) * L] = d.astype(bf16)
        own = [ds_ref[i + 1, :, t * L : (t + 1) * L] for i in range(r)]
        none = jnp.zeros_like(own[0])
        lhs = jnp.concatenate(
            [
                jnp.transpose(jnp.concatenate([none] * p + own + [none] * (2 - p), axis=0))
                for p in range(3)
            ],
            axis=0,
        )
        rhs = hid_ref[1 : r + 3, :, t * L : (t + 2) * L].reshape((r + 2) * S2, 2 * L)
        part = jnp.dot(lhs, rhs, preferred_element_type=f32)
        total = part if total is None else total + part
    grad[...] += total

    @pl.when(step == steps - 1)
    def _():
        for p in range(3):
            for q in range(3):
                block = None
                for w in range(2):
                    at = (2 * p + w) * C
                    part = grad[at : at + C, (w + q) * C : (w + q + 1) * C]
                    block = part if block is None else block + part
                kg_ref[3 * p + q] = block


def back_two(d, c2, hid, st, sums, np2, count):
    r, scan_count, wide = hid.shape
    r, lanes = (r - 5, wide - L)
    return pl.pallas_call(
        functools.partial(back_two_kernel, count=count),
        grid=(scan_count // S2,),
        in_specs=[
            held,
            held,
            held,
            whole(st.shape),
            whole(sums.shape),
            whole(np2.shape),
        ],
        out_specs=[held, whole((9, C, C))],
        out_shape=[
            resident((r + 3, scan_count, lanes), bf16),
            jax.ShapeDtypeStruct((9, C, C), f32),
        ],
        scratch_shapes=[pltpu.VMEM((6 * C, 4 * C), f32)],
        compiler_params=params_of(10),
        cost_estimate=cost(12),
        name="back_two",
    )(d, c2, hid, st, sums, np2)


def hidden_tile(t, parts, n1_ref, np_ref, w_ref, dp_ref, into, first, last):
    r = n1_ref.shape[0] - 1
    pairs, n_scans = ((r + 1) // 2, n1_ref.shape[1])
    low = low_half(n_scans)
    scale, shift = (0.5 * np_ref[0:1], 0.5 * np_ref[1:2])
    parts = [p.reshape(pairs + 1, 2, n_scans, L) for p in parts]
    pieces = [p[a : a + pairs, b] for a in range(2) for b in range(2) for p in parts]
    lhs = jnp.concatenate([p.reshape(pairs * n_scans, L) for p in pieces], axis=1)
    acc = jnp.dot(lhs, w_ref[...], preferred_element_type=f32).reshape(pairs, n_scans, 2 * L)
    sums = [jnp.zeros((8, L), f32), jnp.zeros((8, L), f32)]
    for i in range(r + 1):
        n = pair(n1_ref, i, t).astype(f32)
        h = n * scale + shift
        s = 1.0 + jnp.tanh(h)
        d = acc[i // 2, :, (i % 2) * L : (i % 2 + 1) * L] * (s + h * s * (2.0 - s))
        dp_ref[i, :, into * L : (into + 1) * L] = d
        if i < r:
            if first:
                d = jnp.where(low, 0.0, d)
            if last:
                d = jnp.where(low, d, 0.0)
            sums = [sums[0] + halves(d), sums[1] + halves(d * n)]
    return sums


def hidden_kernel(ds_ref, n1_ref, np_ref, w_ref, dp_ref, sum_ref, run):
    step, steps = (pl.program_id(0), pl.num_programs(0))
    ds_ref, n1_ref, dp_ref = (part_of(a, step) for a in (ds_ref, n1_ref, dp_ref))
    sums = None
    for t in range(1, n1_ref.shape[2] // L - 1):
        parts = [ds_ref[:, :, k * L : (k + 1) * L] for k in (t - 1, t)]
        sums = added(
            sums, hidden_tile(t, parts, n1_ref, np_ref, w_ref, dp_ref, t - 1, False, False)
        )
    add_sums(step, steps, [0.5 * x for x in sums], run, sum_ref)


def hidden_gradient(ds, n1, np2, w):
    r, scan_count, wide = n1.shape
    return pl.pallas_call(
        hidden_kernel,
        grid=(scan_count // S,),
        in_specs=[held, held, whole(np2.shape), whole(w.shape)],
        out_specs=[held, whole((1, 2, L))],
        out_shape=[
            resident((r, scan_count, wide - 2 * L), f32),
            jax.ShapeDtypeStruct((1, 2, L), f32),
        ],
        scratch_shapes=[pltpu.VMEM((8, L), f32)],
        compiler_params=params_of(10),
        cost_estimate=cost(6),
        name="hidden_gradient",
    )(ds, n1, np2, w)


def hidden_ends_kernel(
    ds_ref, left_ref, right_ref, n1_ref, np_ref, w_ref, inner_ref, dp_ref, edge_ref, sum_ref, rim,
    run,
):
    step, steps = (pl.program_id(0), pl.num_programs(0))
    ds_ref, n1_ref, dp_ref = (part_of(a, step, S2) for a in (ds_ref, n1_ref, dp_ref))
    r, tiles = (n1_ref.shape[0] - 1, n1_ref.shape[2] // L)
    low = low_half(S2)
    for row in range(r + 3):
        rim[row] = rim_of(right_ref, left_ref, row, low).astype(bf16)
    first, last = (ds_ref[:, :, k * L : (k + 1) * L] for k in (0, tiles - 2))
    args = (n1_ref, np_ref, w_ref, dp_ref)
    sums = hidden_tile(0, [rim[...], first], *args, 0, True, False)
    sums = added(sums, hidden_tile(tiles - 1, [last, rim[...]], *args, 1, False, True))
    sums = [0.5 * jnp.sum(x, axis=0, keepdims=True) for x in sums]
    sums = [x + inner_ref[0, k : k + 1] / steps for k, x in enumerate(sums)]
    add_sums(step, steps, sums, run, sum_ref)
    half = edge_ref.shape[0]
    for i in range(half):
        both = jnp.where(low, swap(pair(dp_ref, half + i, 0)), pair(dp_ref, i, 0))
        edge_ref[i] = both.astype(bf16)


def hidden_ends(ds, left, right, n1, np2, w, inner, devices):
    r, scan_count, _wide = n1.shape
    half = left.shape[0]
    return pl.pallas_call(
        hidden_ends_kernel,
        grid=(scan_count // S2,),
        in_specs=[
            held,
            more(half, L),
            more(half, L),
            held,
            whole(np2.shape),
            whole(w.shape),
            whole(inner.shape),
        ],
        out_specs=[held, more(r // 2, L), whole((devices, 2, L))],
        out_shape=[
            resident((r, scan_count, 2 * L), f32),
            jax.ShapeDtypeStruct((r // 2, scan_count, L), bf16),
            jax.ShapeDtypeStruct((devices, 2, L), f32),
        ],
        scratch_shapes=[pltpu.VMEM((r + 2, S2, L), bf16), pltpu.VMEM((8, L), f32)],
        compiler_params=params_of(10),
        cost_estimate=cost(3),
        name="hidden_gradient_ends",
    )(ds, left, right, n1, np2, w, inner)


def back_one_kernel(
    dp_ref, ends_ref, edge_ref, n1_ref, x_ref, bits_ref, st_ref, sum_ref, np_ref, kg2_ref, ds, kg_ref,
    xm, grad, flat, *, count,
):
    step, steps = (pl.program_id(0), pl.num_programs(0))
    dp_ref, ends_ref, n1_ref = (part_of(a, step) for a in (dp_ref, ends_ref, n1_ref))
    r, tiles = (n1_ref.shape[0] - 1, n1_ref.shape[2] // L - 1)
    cells = 2.0 * count * st_ref.shape[0]
    _mean, inv = stats_of(st_ref, count)
    shift_sum, gain_sum = sums_of(sum_ref)
    gain = np_ref[0:1] * inv
    c_n = -gain * gain_sum / cells
    c_0 = -gain * shift_sum / cells
    gain = 0.5 * gain
    f_down, f_right = inside()[1::2]
    packed = edge_ref.shape[0]
    low = low_half()
    right = jnp.where(low, 1.0, f_right)

    @pl.when(step == 0)
    def _():
        grad[...] = jnp.zeros_like(grad)

    def line(i, t):
        d = pair(ends_ref, i, min(t, 1)) if t in (0, tiles) else pair(dp_ref, i, t - 1)
        if t == tiles:
            beyond = edge_ref[i % packed].astype(f32)
            d = jnp.where(low, d, swap(beyond) if i >= packed else beyond)
        d = d * gain + (pair(n1_ref, i, t).astype(f32) * c_n + c_0)
        if t == tiles:
            d = d * right
        if i == r:
            d = d * f_down
        ds[i, :, t * L : (t + 1) * L] = d.astype(bf16)

    def turned(t, first):
        return jnp.transpose(ds[first : first + r, :, t * L : (t + 1) * L].reshape(r * S, L))

    columns = []
    total_even, total_odd = (None, None)
    for t in range(tiles + 1):
        for i in range(r + 1):
            line(i, t)
        columns.append([turned(t, 0), turned(t, 1)])
        if t == 0:
            continue
        k = t - 1
        for a in (2 * k, 2 * k + 1):
            for g in range(bits_ref.shape[0]):
                word = bits_ref[g, :, a * L : (a + 1) * L]
                for row in range(g * BITS, min(2 * r, (g + 1) * BITS)):
                    x = live(word, row, pair(x_ref, row, a))
                    xm[row % 2, row // 2, :, a * L : (a + 1) * L] = x
        xl = slice(2 * k * L, 2 * (k + 1) * L)
        xe, xo = (xm[a, :, :, xl].reshape(r * S, 2 * L) for a in range(2))
        here, below = (
            jnp.concatenate([columns[k][a][C:], columns[t][a]], axis=0) for a in range(2)
        )
        even = jnp.dot(here, xe, preferred_element_type=f32)
        odd = jnp.dot(
            jnp.concatenate([here, below], axis=0), xo, preferred_element_type=f32
        )
        total_even = even if total_even is None else total_even + even
        total_odd = odd if total_odd is None else total_odd + odd
    grad[: 3 * C] += total_even
    grad[3 * C :] += total_odd

    @pl.when(step == steps - 1)
    def _():
        blocks = []
        for p in range(3):
            first = (6, 0, 3)[p] * C
            for q in range(3):
                block = None
                for v in range(1, 4):
                    u = q - 3 + 2 * v
                    if 0 <= u < 4:
                        at = first + (v - 1) * C
                        part = grad[at : at + C, u * C : (u + 1) * C]
                        block = part if block is None else block + part
                blocks.append(block)
        blocks += [kg2_ref[8]] + [kg2_ref[k] for k in range(8)]
        for a in range(9):
            flat[a * C : (a + 1) * C] = jnp.concatenate(blocks[2 * a : 2 * a + 2], axis=1)
        if flat.shape[0] > 9 * C:
            flat[9 * C :] = jnp.zeros((flat.shape[0] - 9 * C, L), f32)
        devices, share, _lanes = kg_ref.shape
        for k in range(devices):
            kg_ref[k] = flat[k * share : (k + 1) * share].astype(bf16)


def back_one(dp, ends, edge, n1, x, bits, st, sums, np2, kg2, count):
    rows, scan_count, lanes = x.shape
    r, tiles = (rows // 2, lanes // L // 2)
    devices = st.shape[0]
    share = 8 * -(-9 * C // (8 * devices))
    wide = (tiles + 1) * L
    return pl.pallas_call(
        functools.partial(back_one_kernel, count=count),
        grid=(scan_count // S,),
        in_specs=[
            held,
            held,
            scans(edge.shape[0], L),
            held,
            scans(rows, lanes),
            scans(bits.shape[0], lanes),
            whole(st.shape),
            whole(sums.shape),
            whole(np2.shape),
            whole(kg2.shape),
        ],
        out_specs=[scans(r + 1, wide), whole((devices, share, L))],
        out_shape=[
            pltpu.HBM((r + 1, scan_count, wide), bf16),
            jax.ShapeDtypeStruct((devices, share, L), bf16),
        ],
        scratch_shapes=[
            pltpu.VMEM((2, r, S, lanes), bf16),
            pltpu.VMEM((9 * C, 4 * C), f32),
            pltpu.VMEM((devices * share, L), f32),
        ],
        compiler_params=params_of(),
        cost_estimate=cost(16),
        name="back_one",
    )(dp, ends, edge, n1, hbm(x), hbm(bits), st, sums, np2, kg2)


def input_grad_kernel(ds, bits_ref, w_ref, *rest):
    ig_ref = rest[-1]
    r, tiles = (ds.shape[0] - 1, ds.shape[2] // L - 1)
    for t in range(tiles):
        lanes = slice(t * L, (t + 2) * L)
        rows = [ds[a : a + r, :, lanes].reshape(r * S, 2 * L) for a in range(2)]
        even = jnp.dot(rows[0], w_ref[: 4 * C], preferred_element_type=f32)
        odd = jnp.dot(
            jnp.concatenate(rows, axis=1), w_ref[4 * C :], preferred_element_type=f32
        )
        for k, block in enumerate((even, odd)):
            block = block.reshape(r, S, 2 * L)
            for h in range(2):
                xl = slice((2 * t + h) * L, (2 * t + h + 1) * L)
                for i in range(r):
                    row = 2 * i + k
                    d = block[i, :, h * L : (h + 1) * L].astype(bf16)
                    ig_ref[row, :, xl] = live(bits_ref[row // BITS, :, xl], row, d)


def input_gradient(d, bits, w, part, before):
    r, scan_count, wide = d.shape
    rows, lanes = (2 * (r - 1), 2 * (wide - L))
    steps = scan_count // S // 2
    at = lambda n, m: pl.BlockSpec((n, S, m), lambda g: (0, g + part * steps, 0))
    earlier = () if before is None else (before,)
    return pl.pallas_call(
        input_grad_kernel,
        grid=(steps,),
        in_specs=[at(r, wide), at(bits.shape[0], lanes), whole(w.shape)]
        + [pl.BlockSpec(memory_space=pl.ANY)] * len(earlier),
        out_specs=at(rows, lanes),
        out_shape=jax.ShapeDtypeStruct((rows, scan_count, lanes), bf16),
        input_output_aliases={3: 0} if earlier else {},
        compiler_params=params_of(),
        cost_estimate=cost(7),
        name="input_gradient",
    )(hbm(d), hbm(bits), w, *earlier)


def share_kernel(g_ref, out_ref):
    devices = g_ref.shape[0]
    total = g_ref[0].astype(f32)
    for k in range(1, devices):
        total = total + g_ref[k].astype(f32)
    total = total.astype(bf16)
    for k in range(devices):
        out_ref[k] = total


def sum_share(grads):
    return pl.pallas_call(
        share_kernel,
        in_specs=[held],
        out_specs=held,
        out_shape=jax.ShapeDtypeStruct(grads.shape, bf16),
        compiler_params=pltpu.CompilerParams(vmem_limit_bytes=8 << 20),
        cost_estimate=cost(1),
        name="sum_share",
    )(grads)


def adam_step(weight_now, gradient, moment_one, moment_two, step_rate, decay_rate):
    first_new = adam_beta * moment_one + (1.0 - adam_beta) * gradient
    second_new = adam_beta * moment_two + (1.0 - adam_beta) * gradient * gradient
    correction = 1.0 - adam_beta**step_count
    update = first_new / correction / (jnp.sqrt(second_new / correction) + adam_eps)
    return (weight_now - step_rate * (update + decay_rate * weight_now), first_new, second_new)


def update_kernel(
    g_ref, s1_ref, s2_ref, k_ref, km_ref, kv_ref, n_ref, nm_ref, nv_ref, gn_ref, ok_ref, okm_ref,
    okv_ref, olow_ref, on_ref, onm_ref, onv_ref, flat,
):
    devices, share, _lanes = g_ref.shape
    for k in range(devices):
        flat[k * share : (k + 1) * share] = g_ref[k].astype(f32)
    norm_rows = []
    for ref in (s1_ref, s2_ref):
        shift_sum, gain_sum = sums_of(ref)
        norm_rows += [gain_sum[:, :C], shift_sum[:, :C]]
    g_norm = jnp.concatenate(norm_rows, axis=0)
    squares = jnp.sum(jnp.sum(flat[: 9 * C] ** 2, axis=0, keepdims=True), axis=1, keepdims=True)
    squares = squares + jnp.sum(
        jnp.sum(g_norm * g_norm, axis=0, keepdims=True), axis=1, keepdims=True
    )
    norm = jnp.sqrt(squares)
    gn_ref[...] = norm
    factor = jnp.minimum(1.0, clip_limit / norm)
    on, onm, onv = adam_step(
        n_ref[...], g_norm * factor, nm_ref[...], nv_ref[...], norm_rate, 0.0
    )
    on_ref[...] = on
    onm_ref[...] = onm
    onv_ref[...] = onv
    for layer in range(2):
        for a in range(5):
            width = L if a < 4 else C
            at = slice(a * L, a * L + width)
            if a == 4:
                g = flat[4 * C : 5 * C, layer * C : (layer + 1) * C]
            else:
                first = (a + 5 * layer) * C
                g = flat[first : first + C, :]
            k, km, kv = adam_step(
                k_ref[layer, :, at], g * factor, km_ref[layer, :, at], kv_ref[layer, :, at],
                kernel_rate, kernel_decay,
            )
            ok_ref[layer, :, at] = k
            okm_ref[layer, :, at] = km
            okv_ref[layer, :, at] = kv
            olow_ref[layer, :, at] = k.astype(bf16)


def update(grads, sums1, sums2, kt, kmt, kvt, norm_params, norm_m, norm_v):
    flat = lambda a: a.reshape(4, C)
    big = jax.ShapeDtypeStruct(kt.shape, f32)
    small = jax.ShapeDtypeStruct((4, C), f32)
    outs = [
        jax.ShapeDtypeStruct((1, 1), f32), big, big, big,
        jax.ShapeDtypeStruct(kt.shape, bf16), small, small, small,
    ]
    args = [grads, sums1, sums2, kt, kmt, kvt, flat(norm_params), flat(norm_m), flat(norm_v)]
    return pl.pallas_call(
        update_kernel,
        grid=(1,),
        in_specs=[whole(a.shape) for a in args],
        out_specs=[whole(o.shape) for o in outs],
        out_shape=outs,
        scratch_shapes=[pltpu.VMEM((grads.shape[0] * grads.shape[1], L), f32)],
        compiler_params=params_of(),
        cost_estimate=cost(3),
        name="update",
    )(*args)


def shifted(block, axis, distance):
    devices = range(lax.axis_size(axis))
    route = [(i - distance, i) for i in devices if i - distance in devices]
    return lax.ppermute(block, axis, route)


def exchange(rows):
    return lax.all_to_all(rows, BOTH, 0, 0, tiled=True)


def per_device(
    scan_features, occupancy, kernels, kernel_m, kernel_v, norm_params, norm_m, norm_v, cotangent
):
    x = jnp.transpose(scan_features, (1, 0, 2))
    cot = jnp.transpose(cotangent, (1, 0, 2))
    occ = jnp.transpose(occupancy, (2, 0, 1))
    kt, kmt, kvt = (jnp.transpose(a, (0, 2, 1)) for a in (kernels, kernel_m, kernel_v))
    gy, gx = (lax.axis_size("gy"), lax.axis_size("gx"))
    devices = gy * gx
    rows, scan_count, lanes = x.shape
    r, tiles = (rows // 2, lanes // L // 2)
    count = float(scan_count * r * tiles)
    last = (tiles - 1) * L

    down, cot_down, corner, xcol = edges(x, occ, cot)
    xcol = shifted(xcol, "gx", 1)
    down = shifted(down, "gy", 1)
    cot_down = shifted(cot_down, "gy", -1)
    corner = lax.ppermute(
        corner, BOTH, [(i, i + gx + 1) for i in range(devices - gx) if (i + 1) % gx]
    )
    bits, w1, w2, w2b, w1b, np2 = prepare(occ, kt, norm_params)

    xcol, cot_down = lax.optimization_barrier((xcol, cot_down))
    ends, st1, going_right, going_left, edge = first_last(x, bits, down, xcol, corner, w1)
    left_in = shifted(going_right, "gx", 1)
    right_in = shifted(going_left, "gx", -1)
    c1, st1, up, low_rows = conv_one(x, bits, down, st1, w1, devices)
    up, low_rows = pack_rows(up, low_rows, edge, left_in, right_in)
    down_in = shifted(up, "gy", -1)
    up_in = shifted(low_rows, "gy", 1)
    st1 = exchange(st1)

    c2, n1, hid, st2 = conv_two(
        c1, ends, up_in, down_in, left_in, right_in, st1, np2, w2, count
    )
    st2 = exchange(st2)
    features, d2, sums2 = output(c2, st2, np2, cot, down, cot_down, count)
    sums2 = exchange(sums2)
    going_right, going_left = rim_two(d2, c2, st2, sums2, np2, count)
    left_in = shifted(going_right, "gx", 1)
    right_in = shifted(going_left, "gx", -1)
    ds, kg2 = back_two(d2, c2, hid, st2, sums2, np2, count)
    d1, sums1 = hidden_gradient(ds, n1, np2, w2b)
    d1_ends, edge, sums1 = hidden_ends(ds, left_in, right_in, n1, np2, w2b, sums1, devices)
    edge = shifted(edge, "gx", -1)
    sums1 = exchange(sums1)
    d1, grads = back_one(d1, d1_ends, edge, n1, x, bits, st1, sums1, np2, kg2, count)
    grads = exchange(grads)
    input_grad = input_gradient(d1, bits, w1b, 0, None)
    grads, input_grad = lax.optimization_barrier((sum_share(grads), input_grad))
    grads = exchange(grads)
    input_grad = input_gradient(d1, bits, w1b, 1, input_grad)
    norm, k, km, kv, low, n, nm, nv = update(
        grads, sums1, sums2, kt, kmt, kvt, norm_params, norm_m, norm_v
    )
    back = lambda a: jnp.transpose(a, (0, 2, 1))
    deep = lambda a: a.reshape(norm_params.shape)
    return (
        jnp.transpose(features, (1, 0, 2)),
        jnp.transpose(input_grad, (1, 0, 2)),
        norm.reshape(()),
        back(k),
        back(km),
        back(kv),
        back(low),
        deep(n),
        deep(nm),
        deep(nv),
    )


def solution(mesh):
    split = P(None, "gy", "gx")
    return jax.shard_map(
        per_device,
        mesh=mesh,
        in_specs=(split, split) + (P(),) * 6 + (split,),
        out_specs=(split, split) + (P(),) * 8,
        check_vma=False,
    )
```

```python
import functools
import math

import jax
import jax.numpy as jnp
from jax import lax
from jax.experimental import pallas as pl
from jax.experimental.pallas import tpu as pltpu
from jax.sharding import PartitionSpec as P

norm_eps = 1e-05
adam_beta = 0.5
adam_eps = 1e-08
step_count = 5
clip_limit = 1.0
kernel_rate = 0.04
norm_rate = 0.25
kernel_decay = 0.01

f32, bf16 = (jnp.float32, jnp.bfloat16)
BOTH = ("gy", "gx")
S, S2, C, L, BITS = (16, 32, 64, 128, 13)


def params_of(limit=20):
    return pltpu.CompilerParams(
        dimension_semantics=("arbitrary",), vmem_limit_bytes=limit << 20
    )


def cost(microseconds):
    return pl.CostEstimate(
        flops=0, bytes_accessed=int(microseconds * 3.6e6), transcendentals=0
    )


def whole(shape):
    return pl.BlockSpec(shape, lambda g: (0,) * len(shape))


def scans(rows, lanes, n=S):
    return pl.BlockSpec((rows, n, lanes), lambda g: (0, g, 0))


def more(rows, lanes):
    return scans(rows, lanes, S2)


def resident(shape, dtype):
    return pltpu.VMEM(shape, dtype)


held = pl.BlockSpec(memory_space=pltpu.VMEM)


def vmem(array):
    return pltpu.with_memory_space_constraint(array, pltpu.VMEM)


def hbm(array):
    return pltpu.with_memory_space_constraint(array, pltpu.HBM)


def inside():
    flags = []
    for axis in BOTH:
        at = lax.axis_index(axis)
        flags += [at > 0, at < lax.axis_size(axis) - 1]
    return [jnp.where(flag, 1.0, 0.0) for flag in flags]


def part_of(ref, step, n=S):
    return ref.at[:, pl.ds(pl.multiple_of(step * n, n), n), :]


def low_half(rows=S):
    return lax.broadcasted_iota(jnp.int32, (rows, L), 1) < C


def swap(x):
    return pltpu.roll(x, C, 1)


def fold(x):
    x = jnp.broadcast_to(x, (8, L))
    return (x + swap(x))[:1]


def live(word, row, x):
    bit = 1 << (row % BITS)
    if x.dtype == bf16:
        return jnp.where((word & jnp.int16(bit)) != 0, x, jnp.zeros_like(x))
    return jnp.where((word.astype(jnp.int32) & bit) != 0, x, 0.0)


def pair(ref, row, t):
    return ref[row, :, t * L : (t + 1) * L]


def stats_of(st_ref, count):
    groups = 2 * st_ref.shape[0]
    means = st_ref[:, 0, :]
    mean = fold(jnp.sum(means, axis=0, keepdims=True)) / groups
    spread = st_ref[:, 1, :] + count * (means - mean) ** 2
    spread = fold(jnp.sum(spread, axis=0, keepdims=True)) / (groups * count)
    return (mean, lax.rsqrt(spread + norm_eps))


def sums_of(st_ref):
    return tuple(fold(jnp.sum(st_ref[:, k, :], axis=0, keepdims=True)) for k in range(2))


def pilot_of(block):
    flat = block.reshape(-1, L)
    return jnp.sum(flat, axis=0, keepdims=True) / flat.shape[0]


def finish_stats(step, steps, pilot, sums, count, run_ref, st_ref):
    off, squares = (jnp.sum(s, axis=0, keepdims=True) for s in sums)
    mean = pilot + off / count
    squares = squares - off * off / count

    @pl.when(step == 0)
    def _():
        run_ref[0:1] = mean
        run_ref[1:2] = squares

    @pl.when(step > 0)
    def _():
        before = step.astype(f32)
        share = 1.0 / (before + 1.0)
        delta = mean - run_ref[0:1]
        run_ref[0:1] = run_ref[0:1] + delta * share
        run_ref[1:2] = run_ref[1:2] + squares + delta * delta * (count * before * share)

    @pl.when(step == steps - 1)
    def _():
        st_ref[...] = jnp.broadcast_to(run_ref[0:2][None], st_ref.shape)


def off_sums(blocks, pilot):
    sums = [jnp.zeros((8, L), f32), jnp.zeros((8, L), f32)]
    for block in blocks:
        d = block - pilot
        sums = [sums[0] + halves(d), sums[1] + halves(d * d)]
    return sums


def added(a, b):
    return b if a is None else [x + y for x, y in zip(a, b)]


def odd_place():
    return lax.rem(lax.axis_index("gx"), 2) == 1


def swapped(far, near, odd):
    return lambda k: (
        jnp.where(odd, far(k), near(k)),
        jnp.where(odd, near(k), far(k)),
    )


def rim_of(far, near, row, low, left_first):
    half = far.shape[0]
    k = row % half
    right, left = swapped(
        lambda k: far[k].astype(f32), lambda k: near[k].astype(f32), odd_place()
    )(k)
    first, second = (left, right) if left_first else (right, left)
    if row < half:
        return jnp.where(low, first, second)
    return swap(jnp.where(low, second, first))


def halves(x):
    total = x[:8]
    for k in range(8, x.shape[0], 8):
        total = total + x[k : k + 8]
    return total


def occupancy_words(occ, groups, first):
    rows = occ.shape[1]
    shape = (rows, groups * L)
    group_of = lax.broadcasted_iota(jnp.int32, shape, 1) // L + first
    inner = lax.broadcasted_iota(jnp.int32, shape, 0) - group_of * BITS
    power = jnp.where(
        (inner >= 0) & (inner < BITS), (1 << jnp.clip(inner, 0, BITS)), 0
    ).astype(bf16)
    low = occ.astype(f32).astype(bf16)
    return jnp.dot(low, power, preferred_element_type=f32).astype(jnp.int32)


def edges_kernel(
    row_ref, col_ref, occ_ref, cot_last_ref, cot_first_ref, down_ref, up_ref, corner_ref, xcol_ref
):
    cols, scan_count, rows = occ_ref.shape
    lanes = row_ref.shape[2]
    groups = -(-rows // BITS)
    low = low_half(scan_count)
    words = occupancy_words(occ_ref[...].reshape(cols * scan_count, rows), 1, groups - 1)
    words = words.reshape(cols // 2, 2, scan_count, L)
    for t in range(cols // 2):
        word = jnp.where(low, words[t, 0], words[t, 1])
        x = live(word, rows - 1, row_ref[0, :, t * L : (t + 1) * L].astype(f32)).astype(bf16)
        down_ref[:, t * L : (t + 1) * L] = x
    corner_ref[...] = x
    down_ref[:, lanes:] = cot_last_ref[0]
    up_ref[...] = cot_first_ref[...]
    words = occupancy_words(occ_ref[cols - 1], groups, 0)
    for i in range(rows // 2):
        even, odd = (
            live(
                words[:, row // BITS * L : (row // BITS + 1) * L], row, col_ref[row].astype(f32)
            )
            for row in (2 * i, 2 * i + 1)
        )
        xcol_ref[i] = jnp.where(low, swap(even), odd).astype(bf16)


def edges(x, occ, cot):
    rows, scan_count, lanes = x.shape
    r, wide = (rows // 2, lanes // 2)
    outs = [
        jax.ShapeDtypeStruct((scan_count, lanes + wide), bf16),
        jax.ShapeDtypeStruct((2, scan_count, wide), bf16),
        jax.ShapeDtypeStruct((scan_count, L), bf16),
        jax.ShapeDtypeStruct((r, scan_count, L), bf16),
    ]
    return pl.pallas_call(
        edges_kernel,
        grid=(1,),
        in_specs=[
            pl.BlockSpec((1, scan_count, lanes), lambda g: (rows - 1, 0, 0)),
            pl.BlockSpec((rows, scan_count, L), lambda g: (0, 0, lanes // L - 1)),
            whole(occ.shape),
            pl.BlockSpec((1, scan_count, wide), lambda g: (r - 1, 0, 0)),
            pl.BlockSpec((2, scan_count, wide), lambda g: (0, 0, 0)),
        ],
        out_specs=[whole(o.shape) for o in outs],
        out_shape=outs,
        compiler_params=params_of(),
        cost_estimate=cost(3),
        name="edges",
    )(hbm(x), hbm(x), hbm(occ), hbm(cot), hbm(cot))


def prep_kernel(occ_ref, kt_ref, np_ref, bits_ref, w1_ref, w2_ref, w2b_ref, w1b_ref, np2_ref):
    cols, scan_count, rows = occ_ref.shape
    groups = bits_ref.shape[0]
    words = occupancy_words(occ_ref[...].reshape(cols * scan_count, rows), groups, 0)
    words = words.reshape(cols // 2, 2, scan_count, groups * L)
    low = low_half(scan_count)
    for g in range(groups):
        for t in range(cols // 2):
            lanes = slice(g * L, (g + 1) * L)
            word = jnp.where(low, words[t, 0, :, lanes], words[t, 1, :, lanes])
            bits_ref[g, :, t * L : (t + 1) * L] = word.astype(jnp.int16)
    back = [[kt_ref[l, :, k * C : (k + 1) * C] for k in range(9)] for l in range(2)]
    fore = [[jnp.transpose(b) for b in layer] for layer in back]
    none = jnp.zeros((C, C), f32)

    def put(ref, rows_of, cols_of, pick):
        for a in range(rows_of):
            blocks = [pick(a, b) for b in range(cols_of)]
            for k in range(0, cols_of, 2):
                two = jnp.concatenate(blocks[k : k + 2], axis=1).astype(bf16)
                ref[a * C : (a + 1) * C, k * C : (k + 2) * C] = two

    def tap(table, p, q):
        return table[3 * p + q] if 0 <= p < 3 and 0 <= q < 3 else none

    put(w1_ref, 30, 4, lambda a, b: tap(fore[0], a // 6 - 2 * (b // 2), a % 6 - 2 * (b % 2) - 1))
    put(w2_ref, 16, 4, lambda a, b: tap(fore[1], a // 4 - b // 2, a % 4 - b % 2))
    put(w2b_ref, 16, 4, lambda a, b: tap(back[1], b // 2 + 2 - a // 4, b % 2 + 2 - a % 4))
    put(w1b_ref, 12, 4, lambda a, b: tap(back[0], (1, 2, 0)[a // 4], b + 3 - 2 * (a % 4)))
    np2_ref[...] = jnp.concatenate([np_ref[...], np_ref[...]], axis=1)


def prepare(occ, kt, norm_params):
    cols, scan_count, rows = occ.shape
    full = lambda *shape: jax.ShapeDtypeStruct(shape, bf16)
    outs = [
        jax.ShapeDtypeStruct((-(-rows // BITS), scan_count, cols * C), jnp.int16),
        full(30 * C, 4 * C),
        full(16 * C, 4 * C),
        full(16 * C, 4 * C),
        full(12 * C, 4 * C),
        jax.ShapeDtypeStruct((4, L), f32),
    ]
    return pl.pallas_call(
        prep_kernel,
        grid=(1,),
        in_specs=[whole(occ.shape), whole(kt.shape), whole((4, C))],
        out_specs=[whole(o.shape) for o in outs],
        out_shape=outs,
        compiler_params=params_of(),
        cost_estimate=cost(4),
        name="prepare",
    )(hbm(occ), kt, norm_params.reshape(4, C))


def mask_tile(x_ref, bits_ref, t, xs, into):
    rows = x_ref.shape[0]
    for g in range(bits_ref.shape[0]):
        word = bits_ref[g, :, t * L : (t + 1) * L]
        for row in range(g * BITS, min(rows, (g + 1) * BITS)):
            x = live(word, row, pair(x_ref, row, t))
            xs[(row + 1) // 4, (row + 1) % 4, :, into * L : (into + 1) * L] = x


def clear_rows(rows, pairs, xs):
    for k in range(rows + 1, 4 * pairs + 1):
        xs[k // 4, k % 4] = jnp.zeros_like(xs[0, 0])


def conv_rows(xs, lanes, w, r, before=()):
    pairs = (r + 1) // 2
    pieces = [xs[0:pairs, q, :, lanes] for q in range(4)] + [xs[1 : pairs + 1, 0, :, lanes]]
    pieces = [p.reshape(pairs * S, p.shape[2]) for p in pieces]
    lhs = jnp.concatenate(list(before) + pieces, axis=1)
    acc = jnp.dot(lhs, w, preferred_element_type=f32).reshape(pairs, S, 2 * L)
    return [acc[i // 2, :, (i % 2) * L : (i % 2 + 1) * L] for i in range(r)]


def first_last_kernel(
    x_ref, bits_ref, xrow_ref, xcol_ref, corner_ref, w_ref, c_ref, st_ref, er_ref, el_ref,
    edge_ref, xs, run,
):
    step, steps = (pl.program_id(0), pl.num_programs(0))
    c_ref, x_ref, bits_ref = (part_of(a, step) for a in (c_ref, x_ref, bits_ref))
    rows, lanes = (x_ref.shape[0], x_ref.shape[2])
    r = rows // 2
    low = low_half()

    @pl.when(step == 0)
    def _():
        clear_rows(rows, (r + 1) // 2, xs)

    xs[0, 0, :, :L] = xrow_ref[:, :L]
    xs[0, 0, :, L:] = xrow_ref[:, lanes - 2 * L : lanes]
    mask_tile(x_ref, bits_ref, 0, xs, 0)
    mask_tile(x_ref, bits_ref, lanes // L - 2, xs, 1)
    mask_tile(x_ref, bits_ref, lanes // L - 1, xs, 2)
    wide = 3 * L
    rows_of = lambda q, a, b: w_ref[q * wide + a * C : q * wide + b * C]
    w = jnp.concatenate([rows_of(q, 0, 4) for q in range(5)], axis=0)
    last = conv_rows(xs, slice(L, 3 * L), w, r)
    pairs = (r + 1) // 2
    none = jnp.zeros((S, L), bf16)
    beside = [corner_ref[...]] + [xcol_ref[i] for i in range(r)] + [none]
    w = [jnp.zeros((C, 2 * L), bf16)] + [rows_of(q, 3, 4) for q in range(5)]
    w = jnp.concatenate(w + [rows_of(q, 4, 6) for q in range(5)], axis=0)
    more_lhs = [
        jnp.concatenate([beside[2 * m + k] for m in range(pairs)], axis=0) for k in range(3)
    ]
    first = conv_rows(xs, slice(0, L), w, r, more_lhs)
    edge = [jnp.where(low, b, a) for a, b in zip(first, last)]
    pilot = pilot_of(jnp.concatenate(edge[: r // 2], axis=0))
    for i in range(r):
        c_ref[i, :, :L] = first[i]
        c_ref[i, :, L:] = last[i]
        edge_ref[i] = edge[i].astype(bf16)
    finish_stats(step, steps, pilot, off_sums(edge, pilot), float(r * S), run, st_ref)
    half = er_ref.shape[0]
    odd = odd_place()
    for k in range(half):
        far = swap(edge[k + half]) if k + half < r else jnp.zeros((S, L), f32)
        right, left = (jnp.where(low, edge[k], far), jnp.where(low, far, edge[k]))
        er_ref[k] = jnp.where(odd, right, left).astype(bf16)
        el_ref[k] = jnp.where(odd, left, right).astype(bf16)


def first_last(x, bits, down, xcol, corner, w):
    rows, scan_count, lanes = x.shape
    r = rows // 2
    shape = lambda dtype, *s: jax.ShapeDtypeStruct(s, dtype)
    return pl.pallas_call(
        first_last_kernel,
        grid=(scan_count // S,),
        in_specs=[
            held,
            held,
            pl.BlockSpec((S, down.shape[1]), lambda g: (g, 0)),
            scans(r, L),
            pl.BlockSpec((S, L), lambda g: (g, 0)),
            whole(w.shape),
        ],
        out_specs=[
            held,
            whole((1, 2, L)),
            scans((r + 1) // 2, L),
            scans((r + 1) // 2, L),
            scans(r, L),
        ],
        out_shape=[
            resident((r, scan_count, 2 * L), f32),
            shape(f32, 1, 2, L),
            shape(bf16, (r + 1) // 2, scan_count, L),
            shape(bf16, (r + 1) // 2, scan_count, L),
            shape(bf16, r, scan_count, L),
        ],
        scratch_shapes=[
            pltpu.VMEM(((r + 1) // 2 + 1, 4, S, 3 * L), bf16),
            pltpu.VMEM((8, L), f32),
        ],
        compiler_params=params_of(),
        cost_estimate=cost(4),
        name="conv_one_ends",
    )(vmem(x), vmem(bits), down, xcol, corner, w)


def conv_one_kernel(
    x_ref, bits_ref, xrow_ref, ends_ref, w_ref, c_ref, st_ref, up_ref, down_ref, xs, run
):
    step, steps = (pl.program_id(0), pl.num_programs(0))
    c_ref, x_ref, bits_ref = (part_of(a, step) for a in (c_ref, x_ref, bits_ref))
    rows, tiles = (x_ref.shape[0], x_ref.shape[2] // L)
    r, inner = (rows // 2, tiles // 2 - 1)

    @pl.when(step == 0)
    def _():
        clear_rows(rows, (r + 1) // 2, xs)

    xs[0, 0] = xrow_ref[:, : tiles * L]
    sums, pilot = (None, None)
    filled = 0
    for t in range(inner):
        while filled < 2 * t + 3:
            mask_tile(x_ref, bits_ref, filled, xs, filled)
            filled += 1
        blocks = conv_rows(xs, slice(2 * t * L, (2 * t + 3) * L), w_ref[...], r)
        if pilot is None:
            pilot = pilot_of(jnp.concatenate(blocks[: r // 2], axis=0))
        sums = added(sums, off_sums(blocks, pilot))
        for i, block in enumerate(blocks):
            c_ref[i, :, t * L : (t + 1) * L] = block
    finish_stats(step, steps, pilot, sums, float(r * inner * S), run, st_ref)
    up_ref[...] = c_ref[0:3].astype(bf16)
    down_ref[...] = c_ref[r - 2 : r].astype(bf16)

    @pl.when(step == steps - 1)
    def _():
        own, more = (float(r * S) * steps * n for n in (inner, 1))
        delta = ends_ref[0, 0:1] - run[0:1]
        mean = run[0:1] + delta * (more / (own + more))
        squares = run[1:2] + ends_ref[0, 1:2] + delta * delta * (own * more / (own + more))
        row = jnp.concatenate([mean, squares], axis=0)
        st_ref[...] = jnp.broadcast_to(row[None], st_ref.shape)


def conv_one(x, bits, down, ends, w, devices):
    rows, scan_count, lanes = x.shape
    r, wide = (rows // 2, lanes // 2 - L)
    shape = lambda dtype, *s: jax.ShapeDtypeStruct(s, dtype)
    return pl.pallas_call(
        conv_one_kernel,
        grid=(scan_count // S,),
        in_specs=[
            held,
            held,
            pl.BlockSpec((S, down.shape[1]), lambda g: (g, 0)),
            whole(ends.shape),
            whole(w.shape),
        ],
        out_specs=[held, whole((devices, 2, L)), scans(3, wide), scans(2, wide)],
        out_shape=[
            resident((r, scan_count, wide), f32),
            shape(f32, devices, 2, L),
            shape(bf16, 3, scan_count, wide),
            shape(bf16, 2, scan_count, wide),
        ],
        scratch_shapes=[
            pltpu.VMEM(((r + 1) // 2 + 1, 4, S, lanes), bf16),
            pltpu.VMEM((8, L), f32),
        ],
        compiler_params=params_of(),
        cost_estimate=cost(11),
        name="conv_one",
    )(vmem(x), vmem(bits), down, ends, w)


def pack_kernel(up_ref, down_ref, edge_ref, left_ref, right_ref, up_out, down_out):
    r, wide = (edge_ref.shape[0], up_ref.shape[2])
    low = low_half()
    for src, out, first in ((up_ref, up_out, 0), (down_ref, down_out, r - 2)):
        out[:, :, :wide] = src[...]
        for k in range(src.shape[0]):
            out[k, :, wide : wide + L] = edge_ref[first + k]
            out[k, :, wide + L :] = rim_of(left_ref, right_ref, first + k, low, True).astype(bf16)


def pack_rows(up, down, edge, left, right):
    r, scan_count, _lanes = edge.shape
    wide = up.shape[2]
    return pl.pallas_call(
        pack_kernel,
        grid=(scan_count // S,),
        in_specs=[
            scans(3, wide), scans(2, wide), scans(r, L), scans(left.shape[0], L),
            scans(right.shape[0], L),
        ],
        out_specs=[scans(3, wide + 2 * L), scans(2, wide + 2 * L)],
        out_shape=[
            jax.ShapeDtypeStruct((n, scan_count, wide + 2 * L), bf16) for n in (3, 2)
        ],
        compiler_params=params_of(10),
        cost_estimate=cost(1),
        name="pack_rows",
    )(up, down, edge, left, right)


def conv_two_kernel(
    c_ref, ends_ref, up_ref, down_ref, left_ref, right_ref, st_ref, np_ref, w_ref, c2_ref,
    n1_ref, hid_ref, st2_ref, rim, run, *, count,
):
    step, steps = (pl.program_id(0), pl.num_programs(0))
    c_ref, ends_ref, c2_ref, n1_ref, hid_ref = (
        part_of(a, step, S2) for a in (c_ref, ends_ref, c2_ref, n1_ref, hid_ref)
    )
    r, tiles = (c_ref.shape[0], c_ref.shape[2] // L + 2)
    t_out = tiles - 1
    mean, inv = stats_of(st_ref, count)
    offset = -mean * inv
    scale = 0.5 * np_ref[0:1] * inv
    shift = 0.5 * (np_ref[0:1] * offset + np_ref[1:2])
    f_up, f_down, f_left, f_right = inside()
    low = low_half(S2)
    left = jnp.where(low, f_left, 1.0)
    right = jnp.where(low, 1.0, f_right)
    for row in range(r):
        rim[row] = rim_of(left_ref, right_ref, row, low, True)

    def act(row, t):
        at_end = t in (0, tiles - 1)
        if 2 <= row < r + 2:
            flag = None
            c = pair(ends_ref, row - 2, min(t, 1)) if at_end else pair(c_ref, row - 2, t - 1)
            beyond = rim[row - 2] if at_end else None
        else:
            src, k, flag = (up_ref, row, f_up) if row < 2 else (down_ref, row - r - 2, f_down)
            c = pair(src, k, tiles - 2 if at_end else t - 1).astype(f32)
            beyond = pair(src, k, tiles - 1).astype(f32) if at_end else None
        if t == 0:
            c = jnp.where(low, beyond, c)
        if t == tiles - 1:
            c = jnp.where(low, c, beyond)
        h = c * scale + shift
        out = h + h * jnp.tanh(h)
        if t == 0:
            out = out * left
        if t == tiles - 1:
            out = out * right
        if flag is not None:
            out = out * flag
        out = out.astype(bf16)
        hid_ref[row, :, t * L : (t + 1) * L] = out
        if 2 <= row < r + 3:
            n1_ref[row - 2, :, t * L : (t + 1) * L] = (c * inv + offset).astype(bf16)

    pairs = (r + 3) // 2
    sums, pilot = (None, None)
    for t in range(tiles):
        for row in range(r + 5):
            act(row, t)
        k = t - 1
        if k < 0:
            continue
        lanes = slice(k * L, (k + 2) * L)
        pieces = [
            jnp.concatenate([hid_ref[2 * m + a, :, lanes] for m in range(pairs)], axis=0)
            for a in range(4)
        ]
        lhs = jnp.concatenate(pieces, axis=1)
        acc = jnp.dot(lhs, w_ref[...], preferred_element_type=f32).reshape(pairs, S2, 2 * L)
        if pilot is None:
            pilot = pilot_of(acc[1 : r // 2, :, :L])
        blocks = []
        for row in range(r + 3):
            block = acc[row // 2, :, (row % 2) * L : (row % 2 + 1) * L]
            c2_ref[row, :, k * L : (k + 1) * L] = block
            if 0 < row <= r:
                blocks.append(block)
        sums = added(sums, off_sums(blocks, pilot))
    finish_stats(step, steps, pilot, sums, float(r * t_out * S2), run, st2_ref)


def conv_two(c1, ends, up, down, left, right, st, np2, w, count):
    r, scan_count, wide = c1.shape
    wide = wide + 2 * L
    lanes = wide - L
    devices = st.shape[0]
    return pl.pallas_call(
        functools.partial(conv_two_kernel, count=count),
        grid=(scan_count // S2,),
        in_specs=[
            held,
            held,
            more(2, wide),
            more(3, wide),
            more(left.shape[0], L),
            more(right.shape[0], L),
            whole(st.shape),
            whole(np2.shape),
            whole(w.shape),
        ],
        out_specs=[held, held, held, whole((devices, 2, L))],
        out_shape=[
            resident((r + 3, scan_count, lanes), f32),
            resident((r + 1, scan_count, wide), bf16),
            resident((r + 5, scan_count, wide), bf16),
            jax.ShapeDtypeStruct((devices, 2, L), f32),
        ],
        scratch_shapes=[
            pltpu.VMEM((r, S2, L), f32),
            pltpu.VMEM((8, L), f32),
        ],
        compiler_params=params_of(10),
        cost_estimate=cost(14),
        name="conv_two",
    )(c1, ends, up, down, left, right, st, np2, w)


def output_kernel(
    c2_ref, st_ref, np_ref, cot_ref, up_ref, down_ref, feat_ref, d_ref, sum_ref, run, *, count,
):
    step, steps = (pl.program_id(0), pl.num_programs(0))
    c2_ref, d_ref, cot_ref = (part_of(a, step, S2) for a in (c2_ref, d_ref, cot_ref))
    r, tiles = (cot_ref.shape[0], cot_ref.shape[2] // L)
    mean, inv = stats_of(st_ref, count)
    offset = -mean * inv
    scale = 0.5 * np_ref[2:3] * inv
    shift = 0.5 * (np_ref[2:3] * offset + np_ref[3:4])
    above = 2 * tiles

    def slope(c, cot):
        h = c * scale + shift
        s = 1.0 + jnp.tanh(h)
        f = h * s
        return (f, cot.astype(f32) * (s + f * (2.0 - s)))

    sums = None
    for t in range(tiles):
        part = [jnp.zeros((8, L), f32), jnp.zeros((8, L), f32)]
        for i in range(r):
            c = pair(c2_ref, i + 1, t)
            f, d = slope(c, pair(cot_ref, i, t))
            feat_ref[i, :, t * L : (t + 1) * L] = f.astype(bf16)
            d_ref[i + 1, :, t * L : (t + 1) * L] = d
            part = [part[0] + halves(d), part[1] + halves(d * c)]
        sums = added(sums, part)
    for t in range(tiles):
        lanes = slice(t * L, (t + 1) * L)
        cot = up_ref[:, (above + t) * L : (above + t + 1) * L]
        d_ref[0, :, lanes] = slope(pair(c2_ref, 0, t), cot)[1]
        for k in range(2):
            row = r + 1 + k
            d_ref[row, :, lanes] = slope(pair(c2_ref, row, t), pair(down_ref, k, t))[1]
    sums = (0.5 * sums[0], (0.5 * inv) * (sums[1] - mean * sums[0]))
    add_sums(step, steps, sums, run, sum_ref)


def add_sums(step, steps, sums, run, sum_ref):
    rows = jnp.concatenate([jnp.sum(s, axis=0, keepdims=True) for s in sums], axis=0)

    @pl.when(step == 0)
    def _():
        run[0:2] = rows

    @pl.when(step > 0)
    def _():
        run[0:2] = run[0:2] + rows

    @pl.when(step == steps - 1)
    def _():
        sum_ref[...] = jnp.broadcast_to(run[0:2][None], sum_ref.shape)


def output(c2, st, np2, cot, up, down, count):
    r, scan_count, lanes = cot.shape
    devices = st.shape[0]
    return pl.pallas_call(
        functools.partial(output_kernel, count=count),
        grid=(scan_count // S2,),
        in_specs=[
            held,
            whole(st.shape),
            whole(np2.shape),
            held,
            pl.BlockSpec((S2, up.shape[1]), lambda g: (g, 0)),
            more(2, lanes),
        ],
        out_specs=[more(r, lanes), held, whole((devices, 2, L))],
        out_shape=[
            jax.ShapeDtypeStruct((r, scan_count, lanes), bf16),
            resident((r + 3, scan_count, lanes), f32),
            jax.ShapeDtypeStruct((devices, 2, L), f32),
        ],
        scratch_shapes=[pltpu.VMEM((8, L), f32)],
        compiler_params=params_of(10),
        cost_estimate=cost(12),
        name="output",
    )(c2, st, np2, vmem(cot), up, down)


def norm_back_two(st_ref, sum_ref, np_ref, count, rows):
    cells = 2.0 * count * st_ref.shape[0]
    mean, inv = stats_of(st_ref, count)
    shift_sum, gain_sum = sums_of(sum_ref)
    gain = np_ref[2:3] * inv
    c_n = -gain * inv * gain_sum / cells
    c_0 = -gain * shift_sum / cells - c_n * mean
    gain = 0.5 * gain
    f_up, f_down = inside()[:2]

    def back(row, d, c):
        d = d * gain + (c * c_n + c_0)
        if isinstance(row, int):
            if row == 0:
                d = d * f_up
            if row > rows:
                d = d * f_down
        return d

    return back


def rim_two_kernel(
    d_ref, c_ref, st_ref, sum_ref, np_ref, er_ref, el_ref, *, count
):
    d_ref, c_ref = (part_of(a, pl.program_id(0), S2) for a in (d_ref, c_ref))
    rows, last = (d_ref.shape[0], d_ref.shape[2] // L - 1)
    back = norm_back_two(st_ref, sum_ref, np_ref, count, rows - 3)
    low = low_half(S2)
    half = rows // 2
    column = lambda row, t: back(row, pair(d_ref, row, t), pair(c_ref, row, t))
    both = lambda row: jnp.where(low, column(row, 0), column(row, last))
    odd = odd_place()
    for k in range(half):
        near, far = (both(k), swap(both(k + half)))
        right, left = (jnp.where(low, far, near), jnp.where(low, near, far))
        er_ref[k] = jnp.where(odd, right, left).astype(bf16)
        el_ref[k] = jnp.where(odd, left, right).astype(bf16)


def rim_two(d, c2, st, sums, np2, count):
    rows, scan_count, lanes = d.shape
    return pl.pallas_call(
        functools.partial(rim_two_kernel, count=count),
        grid=(scan_count // S2,),
        in_specs=[
            held, held, whole(st.shape),
            whole(sums.shape), whole(np2.shape),
        ],
        out_specs=[more(rows // 2, L)] * 2,
        out_shape=[jax.ShapeDtypeStruct((rows // 2, scan_count, L), bf16)] * 2,
        compiler_params=params_of(10),
        cost_estimate=cost(3),
        name="rim_two",
    )(d, c2, st, sums, np2)


def back_two_kernel(
    d_ref, c2_ref, hid_ref, st_ref, sum_ref, np_ref, ds_ref, kg_ref, grad, *, count
):
    step, steps = (pl.program_id(0), pl.num_programs(0))
    d_ref, c2_ref, ds_ref, hid_ref = (
        part_of(a, step, S2) for a in (d_ref, c2_ref, ds_ref, hid_ref)
    )
    r, tiles = (c2_ref.shape[0] - 3, c2_ref.shape[2] // L)
    back = norm_back_two(st_ref, sum_ref, np_ref, count, r)

    @pl.when(step == 0)
    def _():
        grad[...] = jnp.zeros_like(grad)

    total = None
    for t in range(tiles):
        for row in range(r + 3):
            d = back(row, pair(d_ref, row, t), pair(c2_ref, row, t))
            ds_ref[row, :, t * L : (t + 1) * L] = d.astype(bf16)
        own = [ds_ref[i + 1, :, t * L : (t + 1) * L] for i in range(r)]
        none = jnp.zeros_like(own[0])
        lhs = jnp.concatenate(
            [
                jnp.transpose(jnp.concatenate([none] * p + own + [none] * (2 - p), axis=0))
                for p in range(3)
            ],
            axis=0,
        )
        rhs = hid_ref[1 : r + 3, :, t * L : (t + 2) * L].reshape((r + 2) * S2, 2 * L)
        part = jnp.dot(lhs, rhs, preferred_element_type=f32)
        total = part if total is None else total + part
    grad[...] += total

    @pl.when(step == steps - 1)
    def _():
        for p in range(3):
            for q in range(3):
                block = None
                for w in range(2):
                    at = (2 * p + w) * C
                    part = grad[at : at + C, (w + q) * C : (w + q + 1) * C]
                    block = part if block is None else block + part
                kg_ref[3 * p + q] = block


def back_two(d, c2, hid, st, sums, np2, count):
    r, scan_count, wide = hid.shape
    r, lanes = (r - 5, wide - L)
    return pl.pallas_call(
        functools.partial(back_two_kernel, count=count),
        grid=(scan_count // S2,),
        in_specs=[
            held,
            held,
            held,
            whole(st.shape),
            whole(sums.shape),
            whole(np2.shape),
        ],
        out_specs=[held, whole((9, C, C))],
        out_shape=[
            resident((r + 3, scan_count, lanes), bf16),
            jax.ShapeDtypeStruct((9, C, C), f32),
        ],
        scratch_shapes=[pltpu.VMEM((6 * C, 4 * C), f32)],
        compiler_params=params_of(10),
        cost_estimate=cost(12),
        name="back_two",
    )(d, c2, hid, st, sums, np2)


def hidden_tile(t, parts, n1_ref, np_ref, w_ref, dp_ref, into, first, last):
    r = n1_ref.shape[0] - 1
    pairs, n_scans = ((r + 1) // 2, n1_ref.shape[1])
    low = low_half(n_scans)
    scale, shift = (0.5 * np_ref[0:1], 0.5 * np_ref[1:2])
    parts = [p.reshape(pairs + 1, 2, n_scans, L) for p in parts]
    pieces = [p[a : a + pairs, b] for a in range(2) for b in range(2) for p in parts]
    lhs = jnp.concatenate([p.reshape(pairs * n_scans, L) for p in pieces], axis=1)
    acc = jnp.dot(lhs, w_ref[...], preferred_element_type=f32).reshape(pairs, n_scans, 2 * L)
    sums = [jnp.zeros((8, L), f32), jnp.zeros((8, L), f32)]
    for i in range(r + 1):
        n = pair(n1_ref, i, t).astype(f32)
        h = n * scale + shift
        s = 1.0 + jnp.tanh(h)
        d = acc[i // 2, :, (i % 2) * L : (i % 2 + 1) * L] * (s + h * s * (2.0 - s))
        dp_ref[i, :, into * L : (into + 1) * L] = d
        if i < r:
            if first:
                d = jnp.where(low, 0.0, d)
            if last:
                d = jnp.where(low, d, 0.0)
            sums = [sums[0] + halves(d), sums[1] + halves(d * n)]
    return sums


def hidden_kernel(ds_ref, n1_ref, np_ref, w_ref, dp_ref, sum_ref, run):
    step, steps = (pl.program_id(0), pl.num_programs(0))
    ds_ref, n1_ref, dp_ref = (part_of(a, step) for a in (ds_ref, n1_ref, dp_ref))
    sums = None
    for t in range(1, n1_ref.shape[2] // L - 1):
        parts = [ds_ref[:, :, k * L : (k + 1) * L] for k in (t - 1, t)]
        sums = added(
            sums, hidden_tile(t, parts, n1_ref, np_ref, w_ref, dp_ref, t - 1, False, False)
        )
    add_sums(step, steps, [0.5 * x for x in sums], run, sum_ref)


def hidden_gradient(ds, n1, np2, w):
    r, scan_count, wide = n1.shape
    return pl.pallas_call(
        hidden_kernel,
        grid=(scan_count // S,),
        in_specs=[held, held, whole(np2.shape), whole(w.shape)],
        out_specs=[held, whole((1, 2, L))],
        out_shape=[
            resident((r, scan_count, wide - 2 * L), f32),
            jax.ShapeDtypeStruct((1, 2, L), f32),
        ],
        scratch_shapes=[pltpu.VMEM((8, L), f32)],
        compiler_params=params_of(10),
        cost_estimate=cost(6),
        name="hidden_gradient",
    )(ds, n1, np2, w)


def hidden_ends_kernel(
    ds_ref, left_ref, right_ref, n1_ref, np_ref, w_ref, inner_ref, dp_ref, edge_ref, sum_ref, rim,
    run,
):
    step, steps = (pl.program_id(0), pl.num_programs(0))
    ds_ref, n1_ref, dp_ref = (part_of(a, step, S2) for a in (ds_ref, n1_ref, dp_ref))
    r, tiles = (n1_ref.shape[0] - 1, n1_ref.shape[2] // L)
    low = low_half(S2)
    for row in range(r + 3):
        rim[row] = rim_of(left_ref, right_ref, row, low, False).astype(bf16)
    first, last = (ds_ref[:, :, k * L : (k + 1) * L] for k in (0, tiles - 2))
    args = (n1_ref, np_ref, w_ref, dp_ref)
    sums = hidden_tile(0, [rim[...], first], *args, 0, True, False)
    sums = added(sums, hidden_tile(tiles - 1, [last, rim[...]], *args, 1, False, True))
    sums = [0.5 * jnp.sum(x, axis=0, keepdims=True) for x in sums]
    sums = [x + inner_ref[0, k : k + 1] / steps for k, x in enumerate(sums)]
    add_sums(step, steps, sums, run, sum_ref)
    half = edge_ref.shape[0]
    for i in range(half):
        both = jnp.where(low, swap(pair(dp_ref, half + i, 0)), pair(dp_ref, i, 0))
        edge_ref[i] = both.astype(bf16)


def hidden_ends(ds, left, right, n1, np2, w, inner, devices):
    r, scan_count, _wide = n1.shape
    half = left.shape[0]
    return pl.pallas_call(
        hidden_ends_kernel,
        grid=(scan_count // S2,),
        in_specs=[
            held,
            more(half, L),
            more(half, L),
            held,
            whole(np2.shape),
            whole(w.shape),
            whole(inner.shape),
        ],
        out_specs=[held, more(r // 2, L), whole((devices, 2, L))],
        out_shape=[
            resident((r, scan_count, 2 * L), f32),
            jax.ShapeDtypeStruct((r // 2, scan_count, L), bf16),
            jax.ShapeDtypeStruct((devices, 2, L), f32),
        ],
        scratch_shapes=[pltpu.VMEM((r + 2, S2, L), bf16), pltpu.VMEM((8, L), f32)],
        compiler_params=params_of(10),
        cost_estimate=cost(3),
        name="hidden_gradient_ends",
    )(ds, left, right, n1, np2, w, inner)


def back_one_kernel(
    dp_ref, ends_ref, edge_ref, n1_ref, x_ref, bits_ref, st_ref, sum_ref, np_ref, kg2_ref, ds, kg_ref,
    xm, grad, flat, *, count,
):
    step, steps = (pl.program_id(0), pl.num_programs(0))
    dp_ref, ends_ref, n1_ref = (part_of(a, step) for a in (dp_ref, ends_ref, n1_ref))
    r, tiles = (n1_ref.shape[0] - 1, n1_ref.shape[2] // L - 1)
    cells = 2.0 * count * st_ref.shape[0]
    _mean, inv = stats_of(st_ref, count)
    shift_sum, gain_sum = sums_of(sum_ref)
    gain = np_ref[0:1] * inv
    c_n = -gain * gain_sum / cells
    c_0 = -gain * shift_sum / cells
    gain = 0.5 * gain
    f_down, f_right = inside()[1::2]
    packed = edge_ref.shape[0]
    low = low_half()
    right = jnp.where(low, 1.0, f_right)

    @pl.when(step == 0)
    def _():
        grad[...] = jnp.zeros_like(grad)

    def line(i, t):
        d = pair(ends_ref, i, min(t, 1)) if t in (0, tiles) else pair(dp_ref, i, t - 1)
        if t == tiles:
            beyond = edge_ref[i % packed].astype(f32)
            d = jnp.where(low, d, swap(beyond) if i >= packed else beyond)
        d = d * gain + (pair(n1_ref, i, t).astype(f32) * c_n + c_0)
        if t == tiles:
            d = d * right
        if i == r:
            d = d * f_down
        ds[i, :, t * L : (t + 1) * L] = d.astype(bf16)

    def turned(t, first):
        return jnp.transpose(ds[first : first + r, :, t * L : (t + 1) * L].reshape(r * S, L))

    columns = []
    total_even, total_odd = (None, None)
    for t in range(tiles + 1):
        for i in range(r + 1):
            line(i, t)
        columns.append([turned(t, 0), turned(t, 1)])
        if t == 0:
            continue
        k = t - 1
        for a in (2 * k, 2 * k + 1):
            for g in range(bits_ref.shape[0]):
                word = bits_ref[g, :, a * L : (a + 1) * L]
                for row in range(g * BITS, min(2 * r, (g + 1) * BITS)):
                    x = live(word, row, pair(x_ref, row, a))
                    xm[row % 2, row // 2, :, a * L : (a + 1) * L] = x
        xl = slice(2 * k * L, 2 * (k + 1) * L)
        xe, xo = (xm[a, :, :, xl].reshape(r * S, 2 * L) for a in range(2))
        here, below = (
            jnp.concatenate([columns[k][a][C:], columns[t][a]], axis=0) for a in range(2)
        )
        even = jnp.dot(here, xe, preferred_element_type=f32)
        odd = jnp.dot(
            jnp.concatenate([here, below], axis=0), xo, preferred_element_type=f32
        )
        total_even = even if total_even is None else total_even + even
        total_odd = odd if total_odd is None else total_odd + odd
    grad[: 3 * C] += total_even
    grad[3 * C :] += total_odd

    @pl.when(step == steps - 1)
    def _():
        blocks = []
        for p in range(3):
            first = (6, 0, 3)[p] * C
            for q in range(3):
                block = None
                for v in range(1, 4):
                    u = q - 3 + 2 * v
                    if 0 <= u < 4:
                        at = first + (v - 1) * C
                        part = grad[at : at + C, u * C : (u + 1) * C]
                        block = part if block is None else block + part
                blocks.append(block)
        blocks += [kg2_ref[8]] + [kg2_ref[k] for k in range(8)]
        for a in range(9):
            flat[a * C : (a + 1) * C] = jnp.concatenate(blocks[2 * a : 2 * a + 2], axis=1)
        if flat.shape[0] > 9 * C:
            flat[9 * C :] = jnp.zeros((flat.shape[0] - 9 * C, L), f32)
        devices, share, _lanes = kg_ref.shape
        for k in range(devices):
            kg_ref[k] = flat[k * share : (k + 1) * share].astype(bf16)


def back_one(dp, ends, edge, n1, x, bits, st, sums, np2, kg2, count):
    rows, scan_count, lanes = x.shape
    r, tiles = (rows // 2, lanes // L // 2)
    devices = st.shape[0]
    share = 8 * -(-9 * C // (8 * devices))
    wide = (tiles + 1) * L
    return pl.pallas_call(
        functools.partial(back_one_kernel, count=count),
        grid=(scan_count // S,),
        in_specs=[
            held,
            held,
            scans(edge.shape[0], L),
            held,
            scans(rows, lanes),
            scans(bits.shape[0], lanes),
            whole(st.shape),
            whole(sums.shape),
            whole(np2.shape),
            whole(kg2.shape),
        ],
        out_specs=[scans(r + 1, wide), whole((devices, share, L))],
        out_shape=[
            pltpu.HBM((r + 1, scan_count, wide), bf16),
            jax.ShapeDtypeStruct((devices, share, L), bf16),
        ],
        scratch_shapes=[
            pltpu.VMEM((2, r, S, lanes), bf16),
            pltpu.VMEM((9 * C, 4 * C), f32),
            pltpu.VMEM((devices * share, L), f32),
        ],
        compiler_params=params_of(),
        cost_estimate=cost(16),
        name="back_one",
    )(dp, ends, edge, n1, hbm(x), hbm(bits), st, sums, np2, kg2)


def input_grad_kernel(ds, bits_ref, w_ref, *rest):
    ig_ref = rest[-1]
    r, tiles = (ds.shape[0] - 1, ds.shape[2] // L - 1)
    for t in range(tiles):
        lanes = slice(t * L, (t + 2) * L)
        rows = [ds[a : a + r, :, lanes].reshape(r * S, 2 * L) for a in range(2)]
        even = jnp.dot(rows[0], w_ref[: 4 * C], preferred_element_type=f32)
        odd = jnp.dot(
            jnp.concatenate(rows, axis=1), w_ref[4 * C :], preferred_element_type=f32
        )
        for k, block in enumerate((even, odd)):
            block = block.reshape(r, S, 2 * L)
            for h in range(2):
                xl = slice((2 * t + h) * L, (2 * t + h + 1) * L)
                for i in range(r):
                    row = 2 * i + k
                    d = block[i, :, h * L : (h + 1) * L].astype(bf16)
                    ig_ref[row, :, xl] = live(bits_ref[row // BITS, :, xl], row, d)


def input_gradient(d, bits, w, part, before):
    r, scan_count, wide = d.shape
    rows, lanes = (2 * (r - 1), 2 * (wide - L))
    steps = scan_count // S // 2
    at = lambda n, m: pl.BlockSpec((n, S, m), lambda g: (0, g + part * steps, 0))
    earlier = () if before is None else (before,)
    return pl.pallas_call(
        input_grad_kernel,
        grid=(steps,),
        in_specs=[at(r, wide), at(bits.shape[0], lanes), whole(w.shape)]
        + [pl.BlockSpec(memory_space=pl.ANY)] * len(earlier),
        out_specs=at(rows, lanes),
        out_shape=jax.ShapeDtypeStruct((rows, scan_count, lanes), bf16),
        input_output_aliases={3: 0} if earlier else {},
        compiler_params=params_of(),
        cost_estimate=cost(7),
        name="input_gradient",
    )(hbm(d), hbm(bits), w, *earlier)


def share_kernel(g_ref, out_ref):
    devices = g_ref.shape[0]
    total = g_ref[0].astype(f32)
    for k in range(1, devices):
        total = total + g_ref[k].astype(f32)
    total = total.astype(bf16)
    for k in range(devices):
        out_ref[k] = total


def sum_share(grads):
    return pl.pallas_call(
        share_kernel,
        in_specs=[held],
        out_specs=held,
        out_shape=jax.ShapeDtypeStruct(grads.shape, bf16),
        compiler_params=pltpu.CompilerParams(vmem_limit_bytes=8 << 20),
        cost_estimate=cost(1),
        name="sum_share",
    )(grads)


def adam_step(weight_now, gradient, moment_one, moment_two, step_rate, decay_rate):
    first_new = adam_beta * moment_one + (1.0 - adam_beta) * gradient
    second_new = adam_beta * moment_two + (1.0 - adam_beta) * gradient * gradient
    correction = 1.0 - adam_beta**step_count
    update = first_new / correction / (jnp.sqrt(second_new / correction) + adam_eps)
    return (weight_now - step_rate * (update + decay_rate * weight_now), first_new, second_new)


def update_kernel(
    g_ref, s1_ref, s2_ref, k_ref, km_ref, kv_ref, n_ref, nm_ref, nv_ref, gn_ref, ok_ref, okm_ref,
    okv_ref, olow_ref, on_ref, onm_ref, onv_ref, flat,
):
    devices, share, _lanes = g_ref.shape
    for k in range(devices):
        flat[k * share : (k + 1) * share] = g_ref[k].astype(f32)
    norm_rows = []
    for ref in (s1_ref, s2_ref):
        shift_sum, gain_sum = sums_of(ref)
        norm_rows += [gain_sum[:, :C], shift_sum[:, :C]]
    g_norm = jnp.concatenate(norm_rows, axis=0)
    squares = jnp.sum(jnp.sum(flat[: 9 * C] ** 2, axis=0, keepdims=True), axis=1, keepdims=True)
    squares = squares + jnp.sum(
        jnp.sum(g_norm * g_norm, axis=0, keepdims=True), axis=1, keepdims=True
    )
    norm = jnp.sqrt(squares)
    gn_ref[...] = norm
    factor = jnp.minimum(1.0, clip_limit / norm)
    on, onm, onv = adam_step(
        n_ref[...], g_norm * factor, nm_ref[...], nv_ref[...], norm_rate, 0.0
    )
    on_ref[...] = on
    onm_ref[...] = onm
    onv_ref[...] = onv
    for layer in range(2):
        for a in range(5):
            width = L if a < 4 else C
            at = slice(a * L, a * L + width)
            if a == 4:
                g = flat[4 * C : 5 * C, layer * C : (layer + 1) * C]
            else:
                first = (a + 5 * layer) * C
                g = flat[first : first + C, :]
            k, km, kv = adam_step(
                k_ref[layer, :, at], g * factor, km_ref[layer, :, at], kv_ref[layer, :, at],
                kernel_rate, kernel_decay,
            )
            ok_ref[layer, :, at] = k
            okm_ref[layer, :, at] = km
            okv_ref[layer, :, at] = kv
            olow_ref[layer, :, at] = k.astype(bf16)


def update(grads, sums1, sums2, kt, kmt, kvt, norm_params, norm_m, norm_v):
    flat = lambda a: a.reshape(4, C)
    big = jax.ShapeDtypeStruct(kt.shape, f32)
    small = jax.ShapeDtypeStruct((4, C), f32)
    outs = [
        jax.ShapeDtypeStruct((1, 1), f32), big, big, big,
        jax.ShapeDtypeStruct(kt.shape, bf16), small, small, small,
    ]
    args = [grads, sums1, sums2, kt, kmt, kvt, flat(norm_params), flat(norm_m), flat(norm_v)]
    return pl.pallas_call(
        update_kernel,
        grid=(1,),
        in_specs=[whole(a.shape) for a in args],
        out_specs=[whole(o.shape) for o in outs],
        out_shape=outs,
        scratch_shapes=[pltpu.VMEM((grads.shape[0] * grads.shape[1], L), f32)],
        compiler_params=params_of(),
        cost_estimate=cost(3),
        name="update",
    )(*args)


def shifted(block, axis, distance):
    devices = range(lax.axis_size(axis))
    route = [(i - distance, i) for i in devices if i - distance in devices]
    return lax.ppermute(block, axis, route)


def partnered(block, first):
    route = []
    for i in range(first, lax.axis_size("gx") - 1, 2):
        route += [(i, i + 1), (i + 1, i)]
    return lax.ppermute(block, "gx", route)


def exchange(rows):
    return lax.all_to_all(rows, BOTH, 0, 0, tiled=True)


def per_device(
    scan_features, occupancy, kernels, kernel_m, kernel_v, norm_params, norm_m, norm_v, cotangent
):
    x = jnp.transpose(scan_features, (1, 0, 2))
    cot = jnp.transpose(cotangent, (1, 0, 2))
    occ = jnp.transpose(occupancy, (2, 0, 1))
    kt, kmt, kvt = (jnp.transpose(a, (0, 2, 1)) for a in (kernels, kernel_m, kernel_v))
    gy, gx = (lax.axis_size("gy"), lax.axis_size("gx"))
    devices = gy * gx
    rows, scan_count, lanes = x.shape
    r, tiles = (rows // 2, lanes // L // 2)
    count = float(scan_count * r * tiles)
    last = (tiles - 1) * L

    down, cot_down, corner, xcol = edges(x, occ, cot)
    xcol = shifted(xcol, "gx", 1)
    down = shifted(down, "gy", 1)
    cot_down = shifted(cot_down, "gy", -1)
    corner = lax.ppermute(
        corner, BOTH, [(i, i + gx + 1) for i in range(devices - gx) if (i + 1) % gx]
    )
    bits, w1, w2, w2b, w1b, np2 = prepare(occ, kt, norm_params)

    xcol, cot_down = lax.optimization_barrier((xcol, cot_down))
    ends, st1, for_far, for_near, edge = first_last(x, bits, down, xcol, corner, w1)
    far_in = partnered(for_far, 1)
    near_in = partnered(for_near, 0)
    c1, st1, up, low_rows = conv_one(x, bits, down, st1, w1, devices)
    up, low_rows = pack_rows(up, low_rows, edge, far_in, near_in)
    down_in = shifted(up, "gy", -1)
    up_in = shifted(low_rows, "gy", 1)
    st1 = exchange(st1)

    c2, n1, hid, st2 = conv_two(
        c1, ends, up_in, down_in, far_in, near_in, st1, np2, w2, count
    )
    st2 = exchange(st2)
    features, d2, sums2 = output(c2, st2, np2, cot, down, cot_down, count)
    sums2 = exchange(sums2)
    for_far, for_near = rim_two(d2, c2, st2, sums2, np2, count)
    far_in = partnered(for_far, 1)
    near_in = partnered(for_near, 0)
    ds, kg2 = back_two(d2, c2, hid, st2, sums2, np2, count)
    d1, sums1 = hidden_gradient(ds, n1, np2, w2b)
    d1_ends, edge, sums1 = hidden_ends(ds, far_in, near_in, n1, np2, w2b, sums1, devices)
    edge = shifted(edge, "gx", -1)
    sums1 = exchange(sums1)
    d1, grads = back_one(d1, d1_ends, edge, n1, x, bits, st1, sums1, np2, kg2, count)
    grads = exchange(grads)
    input_grad = input_gradient(d1, bits, w1b, 0, None)
    grads, input_grad = lax.optimization_barrier((sum_share(grads), input_grad))
    grads = exchange(grads)
    input_grad = input_gradient(d1, bits, w1b, 1, input_grad)
    norm, k, km, kv, low, n, nm, nv = update(
        grads, sums1, sums2, kt, kmt, kvt, norm_params, norm_m, norm_v
    )
    back = lambda a: jnp.transpose(a, (0, 2, 1))
    deep = lambda a: a.reshape(norm_params.shape)
    return (
        jnp.transpose(features, (1, 0, 2)),
        jnp.transpose(input_grad, (1, 0, 2)),
        norm.reshape(()),
        back(k),
        back(km),
        back(kv),
        back(low),
        deep(n),
        deep(nm),
        deep(nv),
    )


def solution(mesh):
    split = P(None, "gy", "gx")
    return jax.shard_map(
        per_device,
        mesh=mesh,
        in_specs=(split, split) + (P(),) * 6 + (split,),
        out_specs=(split, split) + (P(),) * 8,
        check_vma=False,
    )
```
